32 devices in a mesh: attn: 2 (over y), exp: 4 (over z), seq: 4 (over x, core).
Axes of the slice: x: 2, y: 2, z: 4, core: 2. Of those that a mesh axis runs over, the one named last changes fastest.
Arguments:
- tokens: bfloat16 [16, 6144], P(('attn', 'exp'), 'seq'), may hold values from -6 to 6
- modality: int32 [16], P(('attn', 'exp')), may hold values from 0 to 1, as said below
- cotangent: bfloat16 [16, 6144], P(('attn', 'exp'), 'seq'), may hold values from -6 to 6
- gate_speech: bfloat16 [6144, 24576], P('seq', ('attn', 'exp')), may hold values from -0.078125 to 0.078125
- up_speech: bfloat16 [6144, 24576], P('seq', ('attn', 'exp')), may hold values from -0.078125 to 0.078125
- down_speech: bfloat16 [24576, 6144], P(('attn', 'exp'), 'seq'), may hold values from -0.078125 to 0.078125
- gate_text: bfloat16 [6144, 16384], P('seq', ('attn', 'exp')), may hold values from -0.078125 to 0.078125
- up_text: bfloat16 [6144, 16384], P('seq', ('attn', 'exp')), may hold values from -0.078125 to 0.078125
- down_text: bfloat16 [16384, 6144], P(('attn', 'exp'), 'seq'), may hold values from -0.09375 to 0.09375
Outputs:
- mixed: bfloat16 [16, 6144], P(('attn', 'exp'), 'seq')
- token_grad: bfloat16 [16, 6144], P(('attn', 'exp'), 'seq')
- down_speech_grad: bfloat16 [24576, 6144], P(('attn', 'exp'), 'seq')
- down_text_grad: bfloat16 [16384, 6144], P(('attn', 'exp'), 'seq')
The draws below stay inside these ranges and needn't reach their ends.
Inputs may be any that keep to these rules, and one draw needn't show every extreme that they name: Exactly 10 tokens of the window have modality 0 and the other 6 have modality 1, at places drawn from the seed.
All inputs are finite; a program needn't handle non-finite values.
Results may differ from the reference program's by a relative error of at most 0.005.
Values may be sent and summed in bfloat16 or wider, within the bound.
No kernel may reach another device: no remote copies, remote signals or barrier semaphores. Data moves between devices by JAX's collectives and lax.ppermute only.
A program may use at most 256 MiB of HBM per device.

```python
import jax
import jax.numpy as jnp

D = 6144
FFS = 24576
FFT = 16384
TOKENS = 16
SPEECH = 10


def draw_modality(key, part):
    placed = jax.random.permutation(key, TOKENS)
    return (placed >= SPEECH).astype(jnp.int32)


def steps_of(stream_key, extent, split, low, high):
    def one(position, blocks):
        draws = jax.random.uniform(jax.random.fold_in(jax.random.fold_in(stream_key, 6), position), (blocks,), jnp.float32, low / len(split), high / len(split))
        return jnp.repeat(jnp.exp(draws), extent[position] // blocks).reshape((-1,) + (1,) * (len(extent) - position - 1))

    loudness = one(*split[0])
    for cut in split[1:]:
        loudness = loudness * one(*cut)
    return loudness


def noise(own_key, dims, width, bound, cuts=(), held_as=jnp.bfloat16):
    level = steps_of(own_key, dims, cuts, -0.22, 0.18) if cuts else 1.0
    entries = jax.random.normal(own_key, dims, jnp.float32) * width * level
    return jnp.minimum(jnp.maximum(entries, -bound), bound).astype(held_as)


def setup_inputs(seed: int = 0) -> dict:
    streams_of = jax.random.split(jax.random.key(seed), 10)
    tokens = noise(streams_of[0], (TOKENS, D), 1.0, 6.0, ((0, 8), (1, 4)))
    modality = draw_modality(jax.random.fold_in(streams_of[9], 71), 0)
    cotangent = noise(streams_of[2], (TOKENS, D), 1.0, 6.0, ((0, 8), (1, 4)))
    gate_speech = noise(streams_of[3], (D, FFS), D ** -0.5, 0.078125, ((0, 4), (1, 8)))
    up_speech = noise(streams_of[4], (D, FFS), D ** -0.5, 0.078125, ((0, 4), (1, 8)))
    down_speech = noise(streams_of[5], (FFS, D), (FFS // 4) ** -0.5, 0.078125, ((0, 8), (1, 4)))
    gate_text = noise(streams_of[6], (D, FFT), D ** -0.5, 0.078125, ((0, 4), (1, 8)))
    up_text = noise(streams_of[7], (D, FFT), D ** -0.5, 0.078125, ((0, 4), (1, 8)))
    down_text = noise(streams_of[8], (FFT, D), (FFT // 4) ** -0.5, 0.09375, ((0, 8), (1, 4)))
    return dict(tokens=tokens, modality=modality, cotangent=cotangent, gate_speech=gate_speech, up_speech=up_speech, down_speech=down_speech, gate_text=gate_text, up_text=up_text, down_text=down_text)


def reference(tokens, modality, cotangent, gate_speech, up_speech, down_speech, gate_text, up_text, down_text):
    speech = (modality == 0)[:, None]
    gs = jnp.dot(tokens, gate_speech, preferred_element_type=jnp.float32)
    us = jnp.dot(tokens, up_speech, preferred_element_type=jnp.float32)
    gt = jnp.dot(tokens, gate_text, preferred_element_type=jnp.float32)
    ut = jnp.dot(tokens, up_text, preferred_element_type=jnp.float32)
    hs = (jax.nn.silu(gs) * us).astype(jnp.bfloat16)
    ht = (jax.nn.silu(gt) * ut).astype(jnp.bfloat16)
    ys = jnp.dot(hs, down_speech, preferred_element_type=jnp.float32)
    yt = jnp.dot(ht, down_text, preferred_element_type=jnp.float32)
    mixed = jnp.where(speech, ys, yt).astype(jnp.bfloat16)
    zero = jnp.zeros_like(cotangent)
    cs = jnp.where(speech, cotangent, zero)
    ct = jnp.where(speech, zero, cotangent)
    dhs = jnp.dot(cs, down_speech.T, preferred_element_type=jnp.float32)
    dht = jnp.dot(ct, down_text.T, preferred_element_type=jnp.float32)
    sig_s = jax.nn.sigmoid(gs)
    sig_t = jax.nn.sigmoid(gt)
    dgs = (dhs * us * sig_s * (1.0 + gs * (1.0 - sig_s))).astype(jnp.bfloat16)
    dus = (dhs * jax.nn.silu(gs)).astype(jnp.bfloat16)
    dgt = (dht * ut * sig_t * (1.0 + gt * (1.0 - sig_t))).astype(jnp.bfloat16)
    dut = (dht * jax.nn.silu(gt)).astype(jnp.bfloat16)
    token_grad = jnp.dot(dgs, gate_speech.T, preferred_element_type=jnp.float32)
    token_grad = token_grad + jnp.dot(dus, up_speech.T, preferred_element_type=jnp.float32)
    token_grad = token_grad + jnp.dot(dgt, gate_text.T, preferred_element_type=jnp.float32)
    token_grad = token_grad + jnp.dot(dut, up_text.T, preferred_element_type=jnp.float32)
    down_speech_grad = jnp.dot(hs.T, cs, preferred_element_type=jnp.float32).astype(jnp.bfloat16)
    down_text_grad = jnp.dot(ht.T, ct, preferred_element_type=jnp.float32).astype(jnp.bfloat16)
    return mixed, token_grad.astype(jnp.bfloat16), down_speech_grad, down_text_grad
```

```python
import jax
import jax.numpy as jnp
from jax import lax
from jax.sharding import PartitionSpec as P

TOK = ("attn", "exp")
F32 = jnp.float32
BF16 = jnp.bfloat16


def contract_first(left, right):
    return lax.dot_general(left, right, (((0,), (0,)), ((), ())), preferred_element_type=F32)


def contract_last(left, right):
    return lax.dot_general(left, right, (((1,), (1,)), ((), ())), preferred_element_type=F32)


def flip(value, bit, n):
    return lax.ppermute(value, "seq", [(i, i ^ bit) for i in range(n)])


def sum_and_share(parts, apply, n):
    width = parts[0].shape[1]
    half = width // 2
    odd = lax.axis_index("seq") % 2
    packed = jnp.stack(parts).astype(BF16)
    first, second = packed[:, :, :half], packed[:, :, half:]
    theirs = jnp.where(odd == 1, first, second)
    mine = jnp.where(odd == 1, second, first)
    got = flip(theirs, 1, n)
    mine = mine.astype(F32) + got.astype(F32)
    got = flip(mine.astype(BF16), 2, n)
    mine = mine + got.astype(F32)
    done = jnp.stack(apply(*mine)).astype(BF16)
    other = flip(done, 1, n)
    low = jnp.where(odd == 1, other, done)
    high = jnp.where(odd == 1, done, other)
    return jnp.concatenate([low, high], axis=2)


def middle(g, u, dh):
    sig = jax.nn.sigmoid(g)
    silu = g * sig
    h = silu * u
    dg = dh * u * sig * (1.0 + g * (1.0 - sig))
    du = dh * silu
    return h, dg, du


def shards(sizes, tokens, modality, cotangent, gate_s, up_s, down_s, gate_t, up_t, down_t):
    n_seq, n_tok = sizes
    width = tokens.shape[1]
    fs, ft = gate_s.shape[1], gate_t.shape[1]
    kind = jnp.broadcast_to(modality.astype(BF16)[:, None], (modality.shape[0], 128))
    packed = jnp.concatenate([tokens, cotangent, kind], axis=1)
    packed = lax.all_gather(packed, TOK, axis=0, tiled=True)
    rows, grads = packed[:, :width], packed[:, width : 2 * width]
    speech = packed[:, 2 * width : 2 * width + 1] == 0

    def pick(s, t):
        return jnp.concatenate([jnp.where(speech, s[:, :ft], t), s[:, ft:]], axis=1)

    g = pick(jnp.dot(rows, gate_s, preferred_element_type=F32), jnp.dot(rows, gate_t, preferred_element_type=F32))
    u = pick(jnp.dot(rows, up_s, preferred_element_type=F32), jnp.dot(rows, up_t, preferred_element_type=F32))
    dh = pick(contract_last(grads, down_s), contract_last(grads, down_t))
    h, dg, du = sum_and_share((g, u, dh), middle, n_seq)
    zero = jnp.zeros((), BF16)

    def halves(v):
        return jnp.where(speech, v, zero), jnp.where(speech, zero, v[:, :ft])

    hs, ht = halves(h)
    dgs, dgt = halves(dg)
    dus, dut = halves(du)
    mixed = jnp.dot(hs, down_s, preferred_element_type=F32) + jnp.dot(ht, down_t, preferred_element_type=F32)
    back = (
        contract_last(dgs, gate_s)
        + contract_last(dus, up_s)
        + contract_last(dgt, gate_t)
        + contract_last(dut, up_t)
    )
    out = jnp.concatenate([mixed, back], axis=1).astype(BF16)
    out = out.reshape(n_tok, out.shape[0] // n_tok, out.shape[1])
    out = lax.all_to_all(out, TOK, split_axis=0, concat_axis=0, tiled=True)
    out = jnp.sum(out.astype(F32), axis=0).astype(BF16)
    down_s_grad = contract_first(hs, grads).astype(BF16)
    down_t_grad = contract_first(ht, grads).astype(BF16)
    return out[:, :width], out[:, width:], down_s_grad, down_t_grad


def solution(mesh):
    sizes = (mesh.shape["seq"], mesh.shape["attn"] * mesh.shape["exp"])

    def run(*args):
        return shards(sizes, *args)

    return jax.shard_map(
        run,
        mesh=mesh,
        in_specs=(
            P(TOK, "seq"),
            P(TOK),
            P(TOK, "seq"),
            P("seq", TOK),
            P("seq", TOK),
            P(TOK, "seq"),
            P("seq", TOK),
            P("seq", TOK),
            P(TOK, "seq"),
        ),
        out_specs=(P(TOK, "seq"),) * 4,
        check_vma=False,
    )
```

```python
import functools

import jax
import jax.numpy as jnp
from jax import lax
from jax.experimental import pallas as pl
from jax.experimental.pallas import tpu as pltpu
from jax.sharding import PartitionSpec as P

TOK = ("attn", "exp")
F32 = jnp.float32
BF16 = jnp.bfloat16
MIB = 1 << 20
CUTS = 4
BLOCK = 512
HBM = pl.BlockSpec(memory_space=pl.ANY)
VMEM = pl.BlockSpec(memory_space=pltpu.VMEM)


def contract_first(left, right):
    return lax.dot_general(left, right, (((0,), (0,)), ((), ())), preferred_element_type=F32)


def contract_last(left, right):
    return lax.dot_general(left, right, (((1,), (1,)), ((), ())), preferred_element_type=F32)


def times(left, right):
    return jnp.dot(left, right, preferred_element_type=F32)


def copies_of(src, dst, sems):
    rows = src.shape[0] // CUTS
    cuts = [pl.ds(j * rows, rows) for j in range(CUTS)]
    return [pltpu.make_async_copy(src.at[c], dst.at[c], sems.at[j]) for j, c in enumerate(cuts)]


def blocks(count):
    return pl.loop(0, count)


def at(step, size):
    return pl.ds(pl.multiple_of(step * size, size), size)


def is_speech(arr_ref):
    return arr_ref[:, arr_ref.shape[1] - 1 :] == 0


def hbm(x):
    return pltpu.with_memory_space_constraint(x, pltpu.HBM)


def vmem(x):
    return pltpu.with_memory_space_constraint(x, pltpu.VMEM)


def size_of(*arrays):
    return sum(a.size * a.dtype.itemsize for a in arrays)


def call(body, name, outs, ins, in_vmem, scratch, flops, traffic, limit=8):
    return pl.pallas_call(
        body,
        out_shape=outs,
        in_specs=[VMEM if v else HBM for v in in_vmem],
        out_specs=[VMEM] * len(outs),
        scratch_shapes=scratch,
        compiler_params=pltpu.CompilerParams(vmem_limit_bytes=limit * MIB),
        cost_estimate=pl.CostEstimate(flops=flops, bytes_accessed=traffic, transcendentals=0),
        name=name,
    )(*[(vmem(x) if v else hbm(x)) if v is not None else x for x, v in zip(ins, in_vmem)])


def load_body(after_ref, gate_ref, up_ref, gate_out, up_out, sems):
    copies = copies_of(gate_ref, gate_out, sems.at[0]) + copies_of(up_ref, up_out, sems.at[1])
    for copy in copies:
        copy.start()
    for copy in copies:
        copy.wait()


def load(after, gate, up):
    outs = [pltpu.VMEM(w.shape, w.dtype) for w in (gate, up)]
    return call(
        load_body,
        "load_speech",
        outs,
        (after, gate, up),
        (True, False, False),
        [pltpu.SemaphoreType.DMA((2, CUTS))],
        0,
        size_of(gate, up),
    )


def forward_body(
    arr_ref, gs_ref, us_ref, gt_hbm, ut_hbm, dt_hbm, g_ref, u_ref, gt_ref, ut_ref, dt_ref, sems
):
    copies = [
        copies_of(src, dst, sems.at[i])
        for i, (src, dst) in enumerate(((gt_hbm, gt_ref), (ut_hbm, ut_ref), (dt_hbm, dt_ref)))
    ]
    for group in copies:
        for copy in group:
            copy.start()
    width = gs_ref.shape[0]
    x = arr_ref[:, :width]
    speech = is_speech(arr_ref)

    @blocks(gs_ref.shape[1] // BLOCK)
    def _(j):
        cut = at(j, BLOCK)
        g_ref[:, cut] = times(x, gs_ref[:, cut])
        u_ref[:, cut] = times(x, us_ref[:, cut])

    for group, src, out in ((copies[0], gt_ref, g_ref), (copies[1], ut_ref, u_ref)):
        for copy in group:
            copy.wait()

        @blocks(src.shape[1] // BLOCK)
        def _(j):
            cut = at(j, BLOCK)
            out[:, cut] = jnp.where(speech, out[:, cut], times(x, src[:, cut]))

    for copy in copies[2]:
        copy.wait()


def forward(arr, gate_s, up_s, gate_t, up_t, down_t):
    rows, fs = arr.shape[0], gate_s.shape[1]
    outs = [pltpu.VMEM((rows, fs), F32)] * 2 + [pltpu.VMEM(w.shape, w.dtype) for w in (gate_t, up_t, down_t)]
    return call(
        forward_body,
        "hidden_partials",
        outs,
        (arr, gate_s, up_s, gate_t, up_t, down_t),
        (True, True, True, False, False, False),
        [pltpu.SemaphoreType.DMA((3, CUTS))],
        2 * rows * (gate_s.size + gate_t.size) * 2,
        size_of(gate_t, up_t, down_t),
    )


def hidden_grad_body(arr_ref, dt_ref, ds_hbm, dh_ref, ds_ref, sems):
    copies = copies_of(ds_hbm, ds_ref, sems.at[0])
    for copy in copies:
        copy.start()
    width = dt_ref.shape[1]
    c = arr_ref[:, width : 2 * width]
    speech = is_speech(arr_ref)
    ft = dt_ref.shape[0]

    @blocks(ft // BLOCK)
    def _(j):
        cut = at(j, BLOCK)
        dh_ref[:, cut] = contract_last(c, dt_ref[cut, :])

    per = ds_ref.shape[0] // CUTS
    size = min(per, BLOCK // 2)
    for i in range(CUTS):
        copies[i].wait()

        @blocks(per // size)
        def _(j):
            cut = at(i * (per // size) + j, size)
            value = contract_last(c, ds_ref[cut, :])
            if i * per < ft:
                value = jnp.where(speech, value, dh_ref[:, cut])
            dh_ref[:, cut] = value


def hidden_grad(arr, down_t, down_s):
    rows, fs = arr.shape[0], down_s.shape[0]
    return call(
        hidden_grad_body,
        "hidden_grad_partials",
        [pltpu.VMEM((rows, fs), F32), pltpu.VMEM(down_s.shape, down_s.dtype)],
        (arr, down_t, down_s),
        (True, True, False),
        [pltpu.SemaphoreType.DMA((1, CUTS))],
        2 * rows * (down_s.size + down_t.size),
        size_of(down_s),
    )


def split(value, speech):
    zero = jnp.zeros_like(value)
    return jnp.where(speech, value, zero), jnp.where(speech, zero, value)


def mixed_body(arr_ref, h_ref, ds_ref, dt_ref, out_ref):
    speech = is_speech(arr_ref)
    out_ref[...] = jnp.zeros_like(out_ref)

    @blocks(dt_ref.shape[0] // BLOCK)
    def _(j):
        cut = at(j, BLOCK)
        hs, ht = split(h_ref[:, cut], speech)
        out_ref[...] += times(hs, ds_ref[cut, :]) + times(ht, dt_ref[cut, :])

    @pl.loop(dt_ref.shape[0] // BLOCK, ds_ref.shape[0] // BLOCK)
    def _(j):
        cut = at(j, BLOCK)
        hs, _ = split(h_ref[:, cut], speech)
        out_ref[...] += times(hs, ds_ref[cut, :])


def mixed_part(arr, h, down_s, down_t):
    return call(
        mixed_body,
        "mixed_partial",
        [pltpu.VMEM((h.shape[0], down_s.shape[1]), F32)],
        (arr, h, down_s, down_t),
        (True,) * 4,
        [],
        2 * h.shape[0] * (down_s.size + down_t.size),
        0,
    )[0]


def token_grad_body(arr_ref, dg_ref, du_ref, gs_ref, us_ref, gt_ref, ut_ref, out_ref, dgs, dus, dgt, dut):
    speech = is_speech(arr_ref)
    ft = gt_ref.shape[1]
    for src, s, t in ((dg_ref, dgs, dgt), (du_ref, dus, dut)):
        value = src[...]
        zero = jnp.zeros_like(value)
        s[...] = jnp.where(speech, value, zero)
        t[...] = jnp.where(speech, zero[:, :ft], value[:, :ft])

    size = BLOCK // 2

    @blocks(out_ref.shape[1] // size)
    def _(j):
        cut = at(j, size)
        out_ref[:, cut] = (
            contract_last(dgs[...], gs_ref[cut, :])
            + contract_last(dus[...], us_ref[cut, :])
            + contract_last(dgt[...], gt_ref[cut, :])
            + contract_last(dut[...], ut_ref[cut, :])
        )


def token_grad_part(arr, dg, du, gate_s, up_s, gate_t, up_t):
    rows, fs = dg.shape
    ft = gate_t.shape[1]
    return call(
        token_grad_body,
        "token_grad_partial",
        [pltpu.VMEM((rows, gate_s.shape[0]), F32)],
        (arr, dg, du, gate_s, up_s, gate_t, up_t),
        (True,) * 7,
        [pltpu.VMEM((rows, n), BF16) for n in (fs, fs, ft, ft)],
        2 * rows * (gate_s.size + gate_t.size) * 2,
        0,
    )[0]


def outer_body(keep, arr_ref, h_ref, out_ref):
    speech = is_speech(arr_ref)
    width = out_ref.shape[1]
    h = h_ref[...]
    zero = jnp.zeros_like(h)
    h = jnp.where(speech, h, zero) if keep else jnp.where(speech, zero, h)
    out_ref[...] = contract_first(h, arr_ref[:, width : 2 * width]).astype(BF16)


def outer(arr, h, count, width, keep, name):
    rows = arr.shape[0]
    size = 256
    return pl.pallas_call(
        functools.partial(outer_body, keep),
        grid=(count // size,),
        out_shape=jax.ShapeDtypeStruct((count, width), BF16),
        in_specs=[pl.BlockSpec(arr.shape, lambda i: (0, 0)), pl.BlockSpec((rows, size), lambda i: (0, i))],
        out_specs=pl.BlockSpec((size, width), lambda i: (i, 0)),
        compiler_params=pltpu.CompilerParams(vmem_limit_bytes=8 * MIB),
        cost_estimate=pl.CostEstimate(flops=2 * rows * count * width, bytes_accessed=2 * count * width, transcendentals=0),
        name=name,
    )(arr, h)


def flip(value, axes, bit, n):
    return lax.ppermute(value, axes, [(i, i ^ bit) for i in range(n)])


def sum_over_seq(parts, n):
    half = parts[0].shape[1] // 2
    odd = lax.axis_index("seq") % 2
    packed = jnp.stack(parts)
    first, second = packed[:, :, :half], packed[:, :, half:]
    theirs = jnp.where(odd == 1, first, second)
    mine = jnp.where(odd == 1, second, first)
    mine = mine + flip(theirs, "seq", 1, n)
    return mine + flip(mine.astype(BF16), "seq", 2, n).astype(F32)


def share(done, n):
    odd = lax.axis_index("seq") % 2
    done = jnp.stack(done).astype(BF16)
    other = flip(done, "seq", 1, n)
    low = jnp.where(odd == 1, other, done)
    high = jnp.where(odd == 1, done, other)
    return jnp.concatenate([low, high], axis=2)


def hidden(g, u):
    return g * jax.nn.sigmoid(g) * u


def hidden_back(g, u, dh):
    sig = jax.nn.sigmoid(g)
    return dh * u * sig * (1.0 + g * (1.0 - sig)), dh * (g * sig)


def by_kernels(n_seq, n_tok, tokens, modality, cotangent, gate_s, up_s, down_s, gate_t, up_t, down_t):
    width = tokens.shape[1]
    kind = jnp.broadcast_to(modality.astype(BF16)[:, None], (modality.shape[0], 128))
    packed = jnp.concatenate([tokens, cotangent, kind], axis=1)
    arrived = [packed] + [flip(packed, TOK, k, n_tok) for k in range(1, n_tok)]
    gate_s, up_s = load(packed, gate_s, up_s)
    arr = jnp.concatenate(arrived, axis=0)
    g, u, gate_t, up_t, down_t = forward(arr, gate_s, up_s, gate_t, up_t, down_t)
    dh, down_s = hidden_grad(arr, down_t, down_s)
    g, u = sum_over_seq((g, u), n_seq)
    (h,) = share((hidden(g, u),), n_seq)
    (dh,) = sum_over_seq((dh,), n_seq)
    mixed = mixed_part(arr, h, down_s, down_t)
    dg, du = share(hidden_back(g, u, dh), n_seq)
    back = token_grad_part(arr, dg, du, gate_s, up_s, gate_t, up_t)
    out = jnp.concatenate([mixed, back], axis=1).astype(BF16)
    own = out.shape[0] // n_tok
    total = out[:own].astype(F32)
    for k in range(1, n_tok):
        total = total + flip(out[k * own : (k + 1) * own], TOK, k, n_tok).astype(F32)
    total = total.astype(BF16)
    down_s_grad = outer(arr, h, down_s.shape[0], width, True, "down_speech_grad")
    down_t_grad = outer(arr, h, down_t.shape[0], width, False, "down_text_grad")
    return total[:, :width], total[:, width:], down_s_grad, down_t_grad


def by_arrays(n_seq, n_tok, tokens, modality, cotangent, gate_s, up_s, down_s, gate_t, up_t, down_t):
    width = tokens.shape[1]
    ft = gate_t.shape[1]
    kind = jnp.broadcast_to(modality.astype(BF16)[:, None], (modality.shape[0], 128))
    packed = jnp.concatenate([tokens, cotangent, kind], axis=1)
    arrived = lax.all_gather(packed, TOK, axis=0, tiled=True)
    rows, grads = arrived[:, :width], arrived[:, width : 2 * width]
    speech = arrived[:, 2 * width : 2 * width + 1] == 0

    def pick(s, t):
        return jnp.concatenate([jnp.where(speech, s[:, :ft], t), s[:, ft:]], axis=1)

    g = pick(times(rows, gate_s), times(rows, gate_t))
    u = pick(times(rows, up_s), times(rows, up_t))
    dh = pick(contract_last(grads, down_s), contract_last(grads, down_t))
    g, u, dh = sum_over_seq((g, u, dh), n_seq)
    h, dg, du = share((hidden(g, u), *hidden_back(g, u, dh)), n_seq)
    zero = jnp.zeros((), BF16)

    def halves(v):
        return jnp.where(speech, v, zero), jnp.where(speech, zero, v[:, :ft])

    (hs, ht), (dgs, dgt), (dus, dut) = halves(h), halves(dg), halves(du)
    mixed = times(hs, down_s) + times(ht, down_t)
    back = contract_last(dgs, gate_s) + contract_last(dus, up_s)
    back = back + contract_last(dgt, gate_t) + contract_last(dut, up_t)
    out = jnp.concatenate([mixed, back], axis=1).astype(BF16)
    out = out.reshape(n_tok, out.shape[0] // n_tok, out.shape[1])
    out = lax.all_to_all(out, TOK, split_axis=0, concat_axis=0, tiled=True)
    total = jnp.sum(out.astype(F32), axis=0).astype(BF16)
    down_s_grad = contract_first(hs, grads).astype(BF16)
    down_t_grad = contract_first(ht, grads).astype(BF16)
    return total[:, :width], total[:, width:], down_s_grad, down_t_grad


def solution(mesh):
    n_seq, n_tok = mesh.shape["seq"], mesh.shape["attn"] * mesh.shape["exp"]

    def run(*args):
        fits = n_tok == 8 and all(w.shape[0] % 512 == 0 and w.shape[1] % 512 == 0 for w in args[3:])
        return (by_kernels if fits else by_arrays)(n_seq, n_tok, *args)

    return jax.shard_map(
        run,
        mesh=mesh,
        in_specs=(
            P(TOK, "seq"),
            P(TOK),
            P(TOK, "seq"),
            P("seq", TOK),
            P("seq", TOK),
            P(TOK, "seq"),
            P("seq", TOK),
            P("seq", TOK),
            P(TOK, "seq"),
        ),
        out_specs=(P(TOK, "seq"),) * 4,
        check_vma=False,
    )
```

```python
import functools

import jax
import jax.numpy as jnp
from jax import lax
from jax.experimental import pallas as pl
from jax.experimental.pallas import tpu as pltpu
from jax.sharding import PartitionSpec as P

TOK = ("attn", "exp")
HOPS = (2, 1, 4)
F32 = jnp.float32
BF16 = jnp.bfloat16
MIB = 1 << 20
BLOCK = 512
WIDE = 1024
ROWS = 256
SLOTS = 4
PLACES = {"h": pl.ANY, "v": pltpu.VMEM, "s": pltpu.SMEM}


def contract_first(left, right):
    return lax.dot_general(left, right, (((0,), (0,)), ((), ())), preferred_element_type=F32)


def contract_last(left, right):
    return lax.dot_general(left, right, (((1,), (1,)), ((), ())), preferred_element_type=F32)


def times(left, right):
    return jnp.dot(left, right, preferred_element_type=F32)


def size_of(*arrays):
    return sum(a.size * jnp.dtype(a.dtype).itemsize for a in arrays)


def constrain(x, place):
    if place == "s":
        return x
    return pltpu.with_memory_space_constraint(x, pltpu.VMEM if place == "v" else pltpu.HBM)


def call(
    body, name, outs, ins, places, scratch=(), flops=0, traffic=0, limit=4, out_places=None, aliases=None, also=()
):
    out_places = out_places or "v" * len(outs)
    shapes = [pltpu.VMEM(*o) if p == "v" else jax.ShapeDtypeStruct(*o) for o, p in zip(outs, out_places)]
    count = len(ins)

    def seen(*refs):
        body(*refs[:count], *refs[count + len(also) :])

    ins, places = (*ins, *also), places + "v" * len(also)
    return pl.pallas_call(
        seen,
        out_shape=shapes,
        in_specs=[pl.BlockSpec(memory_space=PLACES[p]) for p in places],
        out_specs=[pl.BlockSpec(memory_space=PLACES[p]) for p in out_places],
        scratch_shapes=list(scratch),
        input_output_aliases=aliases or {},
        compiler_params=pltpu.CompilerParams(vmem_limit_bytes=limit * MIB),
        cost_estimate=pl.CostEstimate(flops=flops, bytes_accessed=traffic, transcendentals=0),
        name=name,
    )(*[constrain(x, p) for x, p in zip(ins, places)])


def like(x):
    return x.shape, x.dtype


def parity():
    return lax.rem(lax.axis_index("seq"), 2)


def is_speech(arr_ref):
    return arr_ref[:, arr_ref.shape[1] - 1 :] == 0


def pack_body(kind_hbm, tok_hbm, cot_hbm, wide_ref, tall_ref, out_ref, tok_ref, cot_ref, kind_ref, sems):
    copies = [
        pltpu.make_async_copy(kind_hbm, kind_ref, sems.at[2]),
        pltpu.make_async_copy(tok_hbm, tok_ref, sems.at[0]),
        pltpu.make_async_copy(cot_hbm, cot_ref, sems.at[1]),
    ]
    for copy in copies:
        copy.start()
    width = tok_ref.shape[1]
    row = lax.broadcasted_iota(jnp.int32, (tok_ref.shape[0], 128), 0)
    kind = jnp.zeros(row.shape, F32)
    for copy in copies:
        copy.wait()
    for i in range(tok_ref.shape[0]):
        kind = jnp.where(row == i, kind_ref[i].astype(F32), kind)
    out_ref[:, 2 * width :] = kind.astype(BF16)
    out_ref[:, :width] = tok_ref[...]
    out_ref[:, width : 2 * width] = cot_ref[...]


def join_body(a_ref, b_ref, out_ref):
    both = jnp.concatenate([a_ref[...].astype(F32), b_ref[...].astype(F32)], axis=0)
    out_ref[...] = both.astype(BF16)


def join(a, b, name, also):
    return call(join_body, name, [((2 * a.shape[0], a.shape[1]), BF16)], (a, b), "vv", also=also)[0]


def column_blocks(src, wide, first):
    return [(src.at[:, pl.ds(i * WIDE, WIDE)], wide.at[first + i]) for i in range(src.shape[1] // WIDE)]


def row_blocks(src, tall, first):
    return [
        (src.at[pl.ds(i, BLOCK)], tall.at[pl.ds(first + i, BLOCK)]) for i in range(0, src.shape[0], BLOCK)
    ]


def started(pairs, sems, first):
    copies = [pltpu.make_async_copy(s, d, sems.at[first + i]) for i, (s, d) in enumerate(pairs)]
    for copy in copies:
        copy.start()
    return copies


def load_body(first, after_ref, src_hbm, old_ref, wide_ref, sems):
    for copy in started(column_blocks(src_hbm, wide_ref, first), sems, 0):
        copy.wait()


def load(after, src, wide, tall, first, name):
    return call(
        functools.partial(load_body, first),
        name,
        [like(wide)],
        (after, src, wide),
        "vhv",
        [pltpu.SemaphoreType.DMA((src.shape[1] // WIDE,))],
        traffic=size_of(src),
        aliases={2: 0},
        also=(tall,),
    )[0]


def partials_body(
    arr_ref, gs_hbm, us_hbm, dt_hbm, ds_hbm, old_wide, old_tall,
    mine_ref, theirs_ref, wide_ref, tall_ref, part, sems,
):
    fs, ft, width = ds_hbm.shape[0], dt_hbm.shape[0], dt_hbm.shape[1]
    ns, nt = fs // WIDE, ft // WIDE
    text_copies = started(column_blocks(gs_hbm, wide_ref, 2 * nt), sems, 0)
    text_copies = [text_copies, started(column_blocks(us_hbm, wide_ref, 2 * nt + ns), sems, ns)]
    dt_copies = started(row_blocks(dt_hbm, tall_ref, fs), sems, 2 * ns)
    ds_copies = started(row_blocks(ds_hbm, tall_ref, 0), sems, 2 * ns + ft // BLOCK)
    x = arr_ref[:, :width]
    c = arr_ref[:, width : 2 * width]
    speech = is_speech(arr_ref)

    for k in range(2):
        for i in range(nt):
            part[k, :, i * WIDE : (i + 1) * WIDE] = times(x, wide_ref[k * nt + i])
    for k in range(2):
        for i in range(ns):
            text_copies[k][i].wait()
            value = times(x, wide_ref[2 * nt + k * ns + i])
            cut = slice(i * WIDE, (i + 1) * WIDE)
            if i < nt:
                value = jnp.where(speech, value, part[k, :, cut])
            part[k, :, cut] = value
    for i, copy in enumerate(dt_copies):
        copy.wait()
        cut = slice(i * BLOCK, (i + 1) * BLOCK)
        part[2, :, cut] = contract_last(c, tall_ref[fs + i * BLOCK : fs + (i + 1) * BLOCK, :])
    for i, copy in enumerate(ds_copies):
        copy.wait()
        cut = slice(i * BLOCK, (i + 1) * BLOCK)
        value = contract_last(c, tall_ref[cut, :])
        if i * BLOCK < ft:
            value = jnp.where(speech, value, part[2, :, cut])
        part[2, :, cut] = value
    half = fs // 2
    odd = parity()
    for k in range(3):
        mine_ref[k] = part[k, :, pl.ds(pl.multiple_of(odd * half, half), half)]
        theirs_ref[k] = part[k, :, pl.ds(pl.multiple_of((1 - odd) * half, half), half)]


def partials(arr, gate_s, up_s, down_s, down_t, wide, tall):
    rows, fs = arr.shape[0], gate_s.shape[1]
    half = ((3, rows, fs // 2), F32)
    n_sems = 2 * fs // WIDE + tall.shape[0] // BLOCK
    return call(
        partials_body,
        "hidden_partials",
        [half, half, like(wide), like(tall)],
        (arr, gate_s, up_s, down_t, down_s, wide, tall),
        "vhhhhvv",
        [pltpu.VMEM((3, rows, fs), F32), pltpu.SemaphoreType.DMA((n_sems,))],
        2 * rows * (wide.size + tall.size),
        size_of(gate_s, up_s, down_s, down_t),
        aliases={5: 2, 6: 3},
    )


def core_sum_body(mine_ref, got_ref, sum_ref, send_ref):
    total = mine_ref[...] + got_ref[...]
    sum_ref[...] = total
    send_ref[...] = total.astype(BF16)


def hidden_body(sum_ref, got_ref, out_ref):
    total = [sum_ref[k] + got_ref[k].astype(F32) for k in range(3)]
    g, u, dh = total
    sig = jax.nn.sigmoid(g)
    silu = g * sig
    out_ref[0] = (silu * u).astype(BF16)
    out_ref[1] = (dh * u * sig * (1.0 + g * (1.0 - sig))).astype(BF16)
    out_ref[2] = (dh * silu).astype(BF16)


def back_body(
    arr_ref, done_ref, other_ref, wide_ref, tall_ref,
    keep_ref, send_ref, hs_ref, ht_ref, dgs, dgt, dus, dut, out,
):
    speech = is_speech(arr_ref)
    fs, ft = hs_ref.shape[1], ht_ref.shape[1]
    ns, nt = fs // WIDE, ft // WIDE
    odd = parity() == 1
    for k, (s, t) in enumerate(((hs_ref, ht_ref), (dgs, dgt), (dus, dut))):
        done, other = done_ref[k], other_ref[k]
        value = jnp.concatenate([jnp.where(odd, other, done), jnp.where(odd, done, other)], axis=1)
        zero = jnp.zeros_like(value)
        s[...] = jnp.where(speech, value, zero)
        t[...] = jnp.where(speech, zero, value)[:, :ft]
    width = tall_ref.shape[1]
    for i in range(0, width, BLOCK):
        cut = slice(i, i + BLOCK)
        out[:, cut] = times(hs_ref[...], tall_ref[:fs, cut]) + times(ht_ref[...], tall_ref[fs:, cut])
    blocks = [(dgt, nt), (dut, nt), (dgs, ns), (dus, ns)]
    blocks = [(ref, i) for ref, n in blocks for i in range(n)]
    size = BLOCK // 2
    for i in range(0, width, size):
        total = jnp.zeros((out.shape[0], size), F32)
        for b, (ref, j) in enumerate(blocks):
            total += contract_last(ref[:, j * WIDE : (j + 1) * WIDE], wide_ref[b, i : i + size, :])
        out[:, width + i : width + i + size] = total
    half = keep_ref.shape[0]
    keep_ref[...] = out[:half]
    send_ref[...] = out[half:].astype(BF16)


def back(arr, done, other, wide, tall, fs, ft):
    rows, width = arr.shape[0], tall.shape[1]
    hidden = [((rows, fs), BF16), ((rows, ft), BF16)]
    return call(
        back_body,
        "token_partials",
        [((rows // 2, 2 * width), F32), ((rows // 2, 2 * width), BF16)] + hidden,
        (arr, done, other, wide, tall),
        "vvvvv",
        [pltpu.VMEM(*s) for s in hidden + hidden] + [pltpu.VMEM((rows, 2 * width), F32)],
        2 * rows * (wide.size + tall.size),
    )


def token_sum_body(keep_ref, got_ref, after_ref, next_ref, send_ref):
    total = keep_ref[...] + got_ref[...].astype(F32)
    half = next_ref.shape[0]
    next_ref[...] = total[:half]
    send_ref[...] = total[half:].astype(send_ref.dtype)


def token_sum(keep, got, after, dtype, name):
    rows, width = keep.shape
    outs = [((rows // 2, width), F32), ((rows // 2, width), dtype)]
    return call(token_sum_body, name, outs, (keep, got, after), "vvh")


def last_sum_body(keep_ref, got_ref, mixed_hbm, grad_hbm, mixed_ref, grad_ref, sems):
    total = (keep_ref[...] + got_ref[...].astype(F32)).astype(BF16)
    width = mixed_ref.shape[1]
    mixed_ref[...] = total[:, :width]
    grad_ref[...] = total[:, width:]
    copies = [
        pltpu.make_async_copy(mixed_ref, mixed_hbm, sems.at[0]),
        pltpu.make_async_copy(grad_ref, grad_hbm, sems.at[1]),
    ]
    for copy in copies:
        copy.start()
    for copy in copies:
        copy.wait()


def outer_body(after_ref, arr_ref, h_ref, out_ref, slots, sems):
    width = out_ref.shape[1]
    steps = out_ref.shape[0] // ROWS
    c = arr_ref[:, width : 2 * width]

    def copy(step, slot):
        start = pl.multiple_of(step * ROWS, ROWS)
        return pltpu.make_async_copy(slots.at[slot], out_ref.at[pl.ds(start, ROWS)], sems.at[slot])

    @pl.loop(0, steps // 2)
    def _(pair):
        for side in range(2):
            step = 2 * pair + side
            slot = 2 * lax.rem(pair, 2) + side

            @pl.when(pair >= 2)
            def _():
                copy(step - 4, slot).wait()

        for side in range(2):
            step = 2 * pair + side
            slot = 2 * lax.rem(pair, 2) + side
            h = h_ref[:, pl.ds(pl.multiple_of(step * ROWS, ROWS), ROWS)]
            slots[slot] = contract_first(h, c).astype(BF16)
        for side in range(2):
            copy(2 * pair + side, 2 * lax.rem(pair, 2) + side).start()

    for step in range(steps - 4, steps):
        copy(step, step % 4).wait()


def outer(after, arr, h, width, name):
    rows, count = h.shape
    return call(
        outer_body,
        name,
        [((count, width), BF16)],
        (after, arr, h),
        "vvv",
        [pltpu.VMEM((SLOTS, ROWS, width), BF16), pltpu.SemaphoreType.DMA((SLOTS,))],
        2 * rows * count * width,
        2 * count * width,
        limit=8,
        out_places="h",
    )[0]


def flip(value, axes, bit, n):
    return lax.ppermute(value, axes, [(i, i ^ bit) for i in range(n)])


def by_kernels(n_seq, n_tok, tokens, modality, cotangent, gate_s, up_s, down_s, gate_t, up_t, down_t):
    rows, width = tokens.shape
    fs, ft = gate_s.shape[1], gate_t.shape[1]
    wide = ((2 * (fs + ft) // WIDE, width, WIDE), BF16)
    tall = ((fs + ft, width), BF16)
    pair = [pltpu.VMEM((rows, width), BF16)] * 2

    packed = ((rows, 2 * width + 128), BF16)
    scratch = pair + [pltpu.SMEM((rows,), jnp.int32), pltpu.SemaphoreType.DMA((3,))]
    wide, tall, arr = call(pack_body, "pack", [wide, tall, packed], (modality, tokens, cotangent), "hhh", scratch)
    got = flip(arr, TOK, HOPS[0], n_tok)
    wide = load(arr, gate_t, wide, tall, 0, "load_gate_text")
    arr = join(arr, got, "join_4", (wide, tall))
    got = flip(arr, TOK, HOPS[1], n_tok)
    wide = load(arr, up_t, wide, tall, ft // WIDE, "load_up_text")
    arr = join(arr, got, "join_8", (wide, tall))
    arr = join(arr, flip(arr, TOK, HOPS[2], n_tok), "join_16", (wide, tall))

    mine, theirs, wide, tall = partials(arr, gate_s, up_s, down_s, down_t, wide, tall)
    got = flip(theirs, "seq", 1, n_seq)
    total, send = call(core_sum_body, "core_sum", [like(mine), (mine.shape, BF16)], (mine, got), "vv", also=(wide, tall))
    got = flip(send, "seq", 2, n_seq)
    done = call(hidden_body, "hidden", [(mine.shape, BF16)], (total, got), "vv", also=(wide, tall))[0]
    other = flip(done, "seq", 1, n_seq)

    keep, send, hs, ht = back(arr, done, other, wide, tall, fs, ft)
    got = flip(send, TOK, HOPS[2], n_tok)
    down_t_grad = outer(keep, arr, ht, width, "down_text_grad")
    keep, send = token_sum(keep, got, down_t_grad, BF16, "token_sum_4")
    got = flip(send, TOK, HOPS[1], n_tok)
    down_s_grad = outer(keep, arr, hs, width, "down_speech_grad")
    keep, send = token_sum(keep, got, down_s_grad, F32, "token_sum_2")
    got = flip(send, TOK, HOPS[0], n_tok)
    outs = [((rows, width), BF16)] * 2
    mixed, token_grad = call(last_sum_body, "token_sum_1", outs, (keep, got), "vv", pair + [pltpu.SemaphoreType.DMA((2,))], out_places="hh")
    return mixed, token_grad, down_s_grad, down_t_grad


def by_arrays(n_seq, n_tok, tokens, modality, cotangent, gate_s, up_s, down_s, gate_t, up_t, down_t):
    width = tokens.shape[1]
    ft = gate_t.shape[1]
    kind = jnp.broadcast_to(modality.astype(BF16)[:, None], (modality.shape[0], 128))
    packed = jnp.concatenate([tokens, cotangent, kind], axis=1)
    arrived = lax.all_gather(packed, TOK, axis=0, tiled=True)
    rows, grads = arrived[:, :width], arrived[:, width : 2 * width]
    speech = arrived[:, 2 * width : 2 * width + 1] == 0

    def pick(s, t):
        return jnp.concatenate([jnp.where(speech, s[:, :ft], t), s[:, ft:]], axis=1)

    def halves(v):
        zero = jnp.zeros((), v.dtype)
        return jnp.where(speech, v, zero), jnp.where(speech, zero, v[:, :ft])

    g = pick(times(rows, gate_s), times(rows, gate_t))
    u = pick(times(rows, up_s), times(rows, up_t))
    dh = pick(contract_last(grads, down_s), contract_last(grads, down_t))
    sums = jnp.stack([g, u, dh])
    sums = sums + flip(sums, "seq", 1, n_seq)
    g, u, dh = sums + flip(sums.astype(BF16), "seq", 2, n_seq).astype(F32)
    sig = jax.nn.sigmoid(g)
    h = (g * sig * u).astype(BF16)
    dg = (dh * u * sig * (1.0 + g * (1.0 - sig))).astype(BF16)
    du = (dh * (g * sig)).astype(BF16)
    (hs, ht), (dgs, dgt), (dus, dut) = halves(h), halves(dg), halves(du)
    mixed = times(hs, down_s) + times(ht, down_t)
    grad = contract_last(dgs, gate_s) + contract_last(dus, up_s)
    grad = grad + contract_last(dgt, gate_t) + contract_last(dut, up_t)
    out = jnp.concatenate([mixed, grad], axis=1).astype(BF16)
    out = out.reshape(n_tok, out.shape[0] // n_tok, out.shape[1])
    out = lax.all_to_all(out, TOK, split_axis=0, concat_axis=0, tiled=True)
    total = jnp.sum(out.astype(F32), axis=0).astype(BF16)
    down_s_grad = contract_first(hs, grads).astype(BF16)
    down_t_grad = contract_first(ht, grads).astype(BF16)
    return total[:, :width], total[:, width:], down_s_grad, down_t_grad


def solution(mesh):
    n_seq, n_tok = mesh.shape["seq"], mesh.shape["attn"] * mesh.shape["exp"]

    def run(*args):
        hidden = args[3].shape[1], args[6].shape[1]
        fits = n_tok == 8 and hidden[0] % WIDE == 0 and hidden[1] % WIDE == 0
        fits = fits and hidden[0] >= hidden[1] and args[0].shape == (2, 3 * BLOCK)
        return (by_kernels if fits else by_arrays)(n_seq, n_tok, *args)

    return jax.shard_map(
        run,
        mesh=mesh,
        in_specs=(
            P(TOK, "seq"),
            P(TOK),
            P(TOK, "seq"),
            P("seq", TOK),
            P("seq", TOK),
            P(TOK, "seq"),
            P("seq", TOK),
            P("seq", TOK),
            P(TOK, "seq"),
        ),
        out_specs=(P(TOK, "seq"),) * 4,
        check_vma=False,
    )
```

```python
import functools

import jax
import jax.numpy as jnp
from jax import lax
from jax.experimental import pallas as pl
from jax.experimental.pallas import tpu as pltpu
from jax.sharding import PartitionSpec as P

TOK = ("attn", "exp")
HOPS = (2, 1, 4)
F32 = jnp.float32
BF16 = jnp.bfloat16
MIB = 1 << 20
BLOCK = 512
WIDE = 1024
ROWS = 256
OWN_STEPS = 3
FIRST_STEPS = 8
TEXT_STEPS = 1
PLACES = {"h": pl.ANY, "v": pltpu.VMEM, "s": pltpu.SMEM}


def contract_first(left, right):
    return lax.dot_general(left, right, (((0,), (0,)), ((), ())), preferred_element_type=F32)


def contract_last(left, right):
    return lax.dot_general(left, right, (((1,), (1,)), ((), ())), preferred_element_type=F32)


def times(left, right):
    return jnp.dot(left, right, preferred_element_type=F32)


def size_of(*arrays):
    return sum(a.size * jnp.dtype(a.dtype).itemsize for a in arrays)


def constrain(x, place):
    if place == "s":
        return x
    return pltpu.with_memory_space_constraint(x, pltpu.VMEM if place == "v" else pltpu.HBM)


def call(
    body, name, outs, ins, places, scratch=(), flops=0, traffic=0, limit=4, out_places=None, aliases=None, also=()
):
    out_places = out_places or "v" * len(outs)
    shapes = [pltpu.VMEM(*o) if p == "v" else jax.ShapeDtypeStruct(*o) for o, p in zip(outs, out_places)]
    count = len(ins)

    def seen(*refs):
        body(*refs[:count], *refs[count + len(also) :])

    ins, places = (*ins, *also), places + "v" * len(also)
    return pl.pallas_call(
        seen,
        out_shape=shapes,
        in_specs=[pl.BlockSpec(memory_space=PLACES[p]) for p in places],
        out_specs=[pl.BlockSpec(memory_space=PLACES[p]) for p in out_places],
        scratch_shapes=list(scratch),
        input_output_aliases=aliases or {},
        compiler_params=pltpu.CompilerParams(vmem_limit_bytes=limit * MIB),
        cost_estimate=pl.CostEstimate(flops=flops, bytes_accessed=traffic, transcendentals=0),
        name=name,
    )(*[constrain(x, p) for x, p in zip(ins, places)])


def like(x):
    return x.shape, x.dtype


def parity():
    return lax.rem(lax.axis_index("seq"), 2)


def is_speech(arr_ref):
    return arr_ref[:, arr_ref.shape[1] - 1 :] == 0


def pack_body(kind_hbm, tok_hbm, cot_hbm, wide_ref, tall_ref, out_ref, tok_ref, cot_ref, kind_ref, sems):
    copies = [
        pltpu.make_async_copy(kind_hbm, kind_ref, sems.at[2]),
        pltpu.make_async_copy(tok_hbm, tok_ref, sems.at[0]),
        pltpu.make_async_copy(cot_hbm, cot_ref, sems.at[1]),
    ]
    for copy in copies:
        copy.start()
    width = tok_ref.shape[1]
    row = lax.broadcasted_iota(jnp.int32, (tok_ref.shape[0], 128), 0)
    kind = jnp.zeros(row.shape, F32)
    for copy in copies:
        copy.wait()
    for i in range(tok_ref.shape[0]):
        kind = jnp.where(row == i, kind_ref[i].astype(F32), kind)
    out_ref[:, 2 * width :] = kind.astype(BF16)
    out_ref[:, :width] = tok_ref[...]
    out_ref[:, width : 2 * width] = cot_ref[...]


def join_body(a_ref, b_ref, out_ref):
    both = jnp.concatenate([a_ref[...].astype(F32), b_ref[...].astype(F32)], axis=0)
    out_ref[...] = both.astype(BF16)


def join(a, b, name, also):
    return call(join_body, name, [((2 * a.shape[0], a.shape[1]), BF16)], (a, b), "vv", also=also)[0]


def column_blocks(src, wide, first, cuts):
    rows = src.shape[0] // cuts
    parts = [pl.ds(j * rows, rows) for j in range(cuts)]
    return [
        [(src.at[part, pl.ds(i * WIDE, WIDE)], wide.at[first + i, part]) for part in parts]
        for i in range(src.shape[1] // WIDE)
    ]


def row_blocks(src, tall, first):
    return [
        [(src.at[pl.ds(i, BLOCK)], tall.at[pl.ds(first + i, BLOCK)])] for i in range(0, src.shape[0], BLOCK)
    ]


def started(groups, sems):
    copies, count = [], 0
    for group in groups:
        copies.append([pltpu.make_async_copy(s, d, sems.at[count + i]) for i, (s, d) in enumerate(group)])
        count += len(group)
    for group in copies:
        for copy in group:
            copy.start()
    return copies


def wait(group):
    for copy in group:
        copy.wait()


def load_body(first, after_ref, src_hbm, old_ref, place_ref, sems):
    if place_ref.ndim == 3:
        groups = column_blocks(src_hbm, place_ref, first, 4)
    else:
        groups = row_blocks(src_hbm, place_ref, first)
    for group in started(groups, sems):
        wait(group)


def load(after, src, place, also, first, name):
    return call(
        functools.partial(load_body, first),
        name,
        [like(place)],
        (after, src, place),
        "vhv",
        [pltpu.SemaphoreType.DMA((8,))],
        traffic=size_of(src),
        aliases={2: 0},
        also=also,
    )[0]


def partials_body(
    arr_ref, gs_hbm, us_hbm, ds_hbm, old_wide, old_tall, mine_ref, theirs_ref, wide_ref, tall_ref, part, sems
):
    fs, width = ds_hbm.shape
    ft = tall_ref.shape[0] - fs
    ns, nt = fs // WIDE, ft // WIDE
    groups = column_blocks(gs_hbm, wide_ref, 2 * nt, 2) + column_blocks(us_hbm, wide_ref, 2 * nt + ns, 2)
    copies = started(groups + row_blocks(ds_hbm, tall_ref, 0), sems)
    x = arr_ref[:, :width]
    c = arr_ref[:, width : 2 * width]
    speech = is_speech(arr_ref)

    for k in range(2):
        for i in range(nt):
            part[k, :, i * WIDE : (i + 1) * WIDE] = times(x, wide_ref[k * nt + i])
    for i in range(0, ft, BLOCK):
        part[2, :, i : i + BLOCK] = contract_last(c, tall_ref[fs + i : fs + i + BLOCK, :])
    for k in range(2):
        for i in range(ns):
            wait(copies[k * ns + i])
            value = times(x, wide_ref[2 * nt + k * ns + i])
            cut = slice(i * WIDE, (i + 1) * WIDE)
            if i < nt:
                value = jnp.where(speech, value, part[k, :, cut])
            part[k, :, cut] = value
    for i in range(fs // BLOCK):
        wait(copies[2 * ns + i])
        cut = slice(i * BLOCK, (i + 1) * BLOCK)
        value = contract_last(c, tall_ref[cut, :])
        if i * BLOCK < ft:
            value = jnp.where(speech, value, part[2, :, cut])
        part[2, :, cut] = value
    half = fs // 2
    odd = parity()
    for k in range(3):
        mine_ref[k] = part[k, :, pl.ds(pl.multiple_of(odd * half, half), half)]
        theirs_ref[k] = part[k, :, pl.ds(pl.multiple_of((1 - odd) * half, half), half)]


def partials(arr, gate_s, up_s, down_s, wide, tall):
    rows, fs = arr.shape[0], gate_s.shape[1]
    half = ((3, rows, fs // 2), F32)
    n_sems = 4 * fs // WIDE + fs // BLOCK
    return call(
        partials_body,
        "hidden_partials",
        [half, half, like(wide), like(tall)],
        (arr, gate_s, up_s, down_s, wide, tall),
        "vhhhvv",
        [pltpu.VMEM((3, rows, fs), F32), pltpu.SemaphoreType.DMA((n_sems,))],
        2 * rows * (wide.size + tall.size),
        size_of(gate_s, up_s, down_s),
        aliases={4: 2, 5: 3},
    )


def core_sum_body(mine_ref, got_ref, sum_ref, send_ref):
    total = mine_ref[...] + got_ref[...]
    sum_ref[...] = total
    send_ref[...] = total.astype(BF16)


def hidden_body(sum_ref, got_ref, out_ref):
    total = [sum_ref[k] + got_ref[k].astype(F32) for k in range(3)]
    g, u, dh = total
    sig = jax.nn.sigmoid(g)
    silu = g * sig
    out_ref[0] = (silu * u).astype(BF16)
    out_ref[1] = (dh * u * sig * (1.0 + g * (1.0 - sig))).astype(BF16)
    out_ref[2] = (dh * silu).astype(BF16)


def back_body(
    arr_ref, done_ref, other_ref, wide_ref, tall_ref, after_ref,
    keep_ref, send_ref, hs_ref, ht_ref, dgs, dgt, dus, dut, out,
):
    speech = is_speech(arr_ref)
    fs, ft = hs_ref.shape[1], ht_ref.shape[1]
    ns, nt = fs // WIDE, ft // WIDE
    odd = parity() == 1
    for k, (s, t) in enumerate(((hs_ref, ht_ref), (dgs, dgt), (dus, dut))):
        done, other = done_ref[k], other_ref[k]
        value = jnp.concatenate([jnp.where(odd, other, done), jnp.where(odd, done, other)], axis=1)
        zero = jnp.zeros_like(value)
        s[...] = jnp.where(speech, value, zero)
        t[...] = jnp.where(speech, zero, value)[:, :ft]
    width = tall_ref.shape[1]
    for i in range(0, width, BLOCK):
        cut = slice(i, i + BLOCK)
        out[:, cut] = times(hs_ref[...], tall_ref[:fs, cut]) + times(ht_ref[...], tall_ref[fs:, cut])
    blocks = [(dgt, nt), (dut, nt), (dgs, ns), (dus, ns)]
    blocks = [(ref, i) for ref, n in blocks for i in range(n)]
    size = BLOCK // 2
    for i in range(0, width, size):
        total = jnp.zeros((out.shape[0], size), F32)
        for b, (ref, j) in enumerate(blocks):
            total += contract_last(ref[:, j * WIDE : (j + 1) * WIDE], wide_ref[b, i : i + size, :])
        out[:, width + i : width + i + size] = total
    half = keep_ref.shape[0]
    keep_ref[...] = out[:half]
    send_ref[...] = out[half:].astype(BF16)


def back(arr, done, other, wide, tall, after, fs, ft):
    rows, width = arr.shape[0], tall.shape[1]
    hidden = [((rows, fs), BF16), ((rows, ft), BF16)]
    return call(
        back_body,
        "token_partials",
        [((rows // 2, 2 * width), F32), ((rows // 2, 2 * width), BF16)] + hidden,
        (arr, done, other, wide, tall, after),
        "vvvvvh",
        [pltpu.VMEM(*s) for s in hidden + hidden] + [pltpu.VMEM((rows, 2 * width), F32)],
        2 * rows * (wide.size + tall.size),
    )


def token_sum_body(keep_ref, got_ref, after_ref, next_ref, send_ref):
    total = keep_ref[...] + got_ref[...].astype(F32)
    half = next_ref.shape[0]
    next_ref[...] = total[:half]
    send_ref[...] = total[half:].astype(send_ref.dtype)


def token_sum(keep, got, after, dtype, name):
    rows, width = keep.shape
    outs = [((rows // 2, width), F32), ((rows // 2, width), dtype)]
    return call(token_sum_body, name, outs, (keep, got, after), "vvh")


def last_sum_body(keep_ref, got_ref, mixed_hbm, grad_hbm, mixed_ref, grad_ref, sems):
    total = (keep_ref[...] + got_ref[...].astype(F32)).astype(BF16)
    width = mixed_ref.shape[1]
    mixed_ref[...] = total[:, :width]
    grad_ref[...] = total[:, width:]
    copies = [
        pltpu.make_async_copy(mixed_ref, mixed_hbm, sems.at[0]),
        pltpu.make_async_copy(grad_ref, grad_hbm, sems.at[1]),
    ]
    for copy in copies:
        copy.start()
    for copy in copies:
        copy.wait()


def outer_steps(c, steps, slots, sems):
    copies = []
    for i, (h, place) in enumerate(steps):
        slots[i] = contract_first(h, c).astype(BF16)
        copies.append(pltpu.make_async_copy(slots.at[i], place, sems.at[i]))
        copies[-1].start()
    for copy in copies:
        copy.wait()


def rows_at(ref, start):
    return ref.at[pl.ds(pl.multiple_of(start, ROWS), ROWS)]


def outer_own_body(count, arr_ref, done_ref, out_ref, slots, sems):
    half, width = done_ref.shape[2], out_ref.shape[1]
    c = arr_ref[:, width : 2 * width]
    h = done_ref[0]
    h = jnp.where(is_speech(arr_ref), h, jnp.zeros_like(h))
    base = parity() * half
    steps = [(h[:, i * ROWS : (i + 1) * ROWS], rows_at(out_ref, base + i * ROWS)) for i in range(count)]
    outer_steps(c, steps, slots, sems)


def outer_body(speech, text, after_ref, arr_ref, hs_ref, ht_ref, *refs):
    slots, sems = refs[-2:]
    outs = list(refs[1:-2])
    out_s = outs.pop(0) if len(speech) else None
    out_t = outs.pop(0) if len(text) else None
    width = (out_s if len(speech) else out_t).shape[1]
    c = arr_ref[:, width : 2 * width]
    half = hs_ref.shape[1] // 2
    odd = parity()
    steps = []
    for i in speech:
        side = odd if i * ROWS < half else 1 - odd
        start = side * half + i * ROWS % half
        steps.append((hs_ref[:, pl.ds(pl.multiple_of(start, ROWS), ROWS)], rows_at(out_s, start)))
    for i in text:
        steps.append((ht_ref[:, i * ROWS : (i + 1) * ROWS], rows_at(out_t, i * ROWS)))
    outer_steps(c, steps, slots, sems)


def flip(value, axes, bit, n):
    return lax.ppermute(value, axes, [(i, i ^ bit) for i in range(n)])


def by_kernels(n_seq, n_tok, tokens, modality, cotangent, gate_s, up_s, down_s, gate_t, up_t, down_t):
    rows, width = tokens.shape
    fs, ft = gate_s.shape[1], gate_t.shape[1]
    wide = ((2 * (fs + ft) // WIDE, width, WIDE), BF16)
    tall = ((fs + ft, width), BF16)
    pair = [pltpu.VMEM((rows, width), BF16)] * 2

    packed = ((rows, 2 * width + 128), BF16)
    scratch = pair + [pltpu.SMEM((rows,), jnp.int32), pltpu.SemaphoreType.DMA((3,))]
    wide, tall, arr = call(pack_body, "pack", [wide, tall, packed], (modality, tokens, cotangent), "hhh", scratch)
    got = flip(arr, TOK, HOPS[0], n_tok)
    wide = load(arr, gate_t, wide, (tall,), 0, "load_gate_text")
    arr = join(arr, got, "join_4", (wide, tall))
    got = flip(arr, TOK, HOPS[1], n_tok)
    wide = load(arr, up_t, wide, (tall,), ft // WIDE, "load_up_text")
    arr = join(arr, got, "join_8", (wide, tall))
    got = flip(arr, TOK, HOPS[2], n_tok)
    tall = load(arr, down_t, tall, (wide,), fs, "load_down_text")
    arr = join(arr, got, "join_16", (wide, tall))

    mine, theirs, wide, tall = partials(arr, gate_s, up_s, down_s, wide, tall)
    got = flip(theirs, "seq", 1, n_seq)
    total, send = call(
        core_sum_body, "core_sum", [like(mine), (mine.shape, BF16)], (mine, got), "vv", also=(wide, tall)
    )
    got = flip(send, "seq", 2, n_seq)
    done = call(hidden_body, "hidden", [(mine.shape, BF16)], (total, got), "vv", also=(wide, tall))[0]
    other = flip(done, "seq", 1, n_seq)

    def slots(count):
        return [pltpu.VMEM((count, ROWS, width), BF16), pltpu.SemaphoreType.DMA((count,))]

    def cost(count):
        return 2 * arr.shape[0] * count * ROWS * width, 2 * count * ROWS * width

    own = OWN_STEPS
    down_s_grad = call(
        functools.partial(outer_own_body, own), "down_grad_own", [like(down_s)], (arr, done), "vv", slots(own),
        *cost(own), out_places="h", also=(wide, tall),
    )[0]
    keep, send, hs, ht = back(arr, done, other, wide, tall, down_s_grad, fs, ft)

    got = flip(send, TOK, HOPS[2], n_tok)
    first, second = range(own, FIRST_STEPS), range(FIRST_STEPS, fs // ROWS)
    down_s_grad = call(
        functools.partial(outer_body, first, ()), "down_grad_1", [like(down_s)], (keep, arr, hs, ht, down_s_grad),
        "vvvvh", slots(len(first)), *cost(len(first)), limit=8, out_places="h", aliases={4: 0},
    )[0]
    keep, send = token_sum(keep, got, down_s_grad, BF16, "token_sum_4")

    got = flip(send, TOK, HOPS[1], n_tok)
    text = range(0, TEXT_STEPS)
    count = len(second) + len(text)
    down_s_grad, down_t_grad = call(
        functools.partial(outer_body, second, text), "down_grad_2", [like(down_s), like(down_t)],
        (keep, arr, hs, ht, down_s_grad), "vvvvh", slots(count), *cost(count), limit=8, out_places="hh",
        aliases={4: 0},
    )
    keep, send = token_sum(keep, got, down_t_grad, F32, "token_sum_2")

    got = flip(send, TOK, HOPS[0], n_tok)
    text = range(TEXT_STEPS, ft // ROWS)
    down_t_grad = call(
        functools.partial(outer_body, (), text), "down_grad_3", [like(down_t)], (keep, arr, hs, ht, down_t_grad),
        "vvvvh", slots(len(text)), *cost(len(text)), limit=8, out_places="h", aliases={4: 0},
    )[0]
    outs = [((rows, width), BF16)] * 2
    mixed, token_grad = call(last_sum_body, "token_sum_1", outs, (keep, got), "vv", pair + [pltpu.SemaphoreType.DMA((2,))], out_places="hh")
    return mixed, token_grad, down_s_grad, down_t_grad


def by_arrays(n_seq, n_tok, tokens, modality, cotangent, gate_s, up_s, down_s, gate_t, up_t, down_t):
    width = tokens.shape[1]
    ft = gate_t.shape[1]
    kind = jnp.broadcast_to(modality.astype(BF16)[:, None], (modality.shape[0], 128))
    packed = jnp.concatenate([tokens, cotangent, kind], axis=1)
    arrived = lax.all_gather(packed, TOK, axis=0, tiled=True)
    rows, grads = arrived[:, :width], arrived[:, width : 2 * width]
    speech = arrived[:, 2 * width : 2 * width + 1] == 0

    def pick(s, t):
        return jnp.concatenate([jnp.where(speech, s[:, :ft], t), s[:, ft:]], axis=1)

    def halves(v):
        zero = jnp.zeros((), v.dtype)
        return jnp.where(speech, v, zero), jnp.where(speech, zero, v[:, :ft])

    g = pick(times(rows, gate_s), times(rows, gate_t))
    u = pick(times(rows, up_s), times(rows, up_t))
    dh = pick(contract_last(grads, down_s), contract_last(grads, down_t))
    sums = jnp.stack([g, u, dh])
    sums = sums + flip(sums, "seq", 1, n_seq)
    g, u, dh = sums + flip(sums.astype(BF16), "seq", 2, n_seq).astype(F32)
    sig = jax.nn.sigmoid(g)
    h = (g * sig * u).astype(BF16)
    dg = (dh * u * sig * (1.0 + g * (1.0 - sig))).astype(BF16)
    du = (dh * (g * sig)).astype(BF16)
    (hs, ht), (dgs, dgt), (dus, dut) = halves(h), halves(dg), halves(du)
    mixed = times(hs, down_s) + times(ht, down_t)
    grad = contract_last(dgs, gate_s) + contract_last(dus, up_s)
    grad = grad + contract_last(dgt, gate_t) + contract_last(dut, up_t)
    out = jnp.concatenate([mixed, grad], axis=1).astype(BF16)
    out = out.reshape(n_tok, out.shape[0] // n_tok, out.shape[1])
    out = lax.all_to_all(out, TOK, split_axis=0, concat_axis=0, tiled=True)
    total = jnp.sum(out.astype(F32), axis=0).astype(BF16)
    down_s_grad = contract_first(hs, grads).astype(BF16)
    down_t_grad = contract_first(ht, grads).astype(BF16)
    return total[:, :width], total[:, width:], down_s_grad, down_t_grad


def solution(mesh):
    n_seq, n_tok = mesh.shape["seq"], mesh.shape["attn"] * mesh.shape["exp"]

    def run(*args):
        hidden = args[3].shape[1], args[6].shape[1]
        fits = n_tok == 8 and hidden[0] % WIDE == 0 and hidden[1] % WIDE == 0
        fits = fits and hidden[0] >= hidden[1] and args[0].shape == (2, 3 * BLOCK)
        return (by_kernels if fits else by_arrays)(n_seq, n_tok, *args)

    return jax.shard_map(
        run,
        mesh=mesh,
        in_specs=(
            P(TOK, "seq"),
            P(TOK),
            P(TOK, "seq"),
            P("seq", TOK),
            P("seq", TOK),
            P(TOK, "seq"),
            P("seq", TOK),
            P("seq", TOK),
            P(TOK, "seq"),
        ),
        out_specs=(P(TOK, "seq"),) * 4,
        check_vma=False,
    )
```

```python
import functools

import jax
import jax.numpy as jnp
from jax import lax
from jax.experimental import pallas as pl
from jax.experimental.pallas import tpu as pltpu
from jax.sharding import PartitionSpec as P

TOK = ("attn", "exp")
HOPS = (2, 1, 4)
F32 = jnp.float32
BF16 = jnp.bfloat16
MIB = 1 << 20
BLOCK = 512
ROWS = 256
TURN_FIRST = 2
TURN_SECOND = 6
PLACES = {"h": pl.ANY, "v": pltpu.VMEM, "s": pltpu.SMEM}


def contract_first(left, right):
    return lax.dot_general(left, right, (((0,), (0,)), ((), ())), preferred_element_type=F32)


def contract_last(left, right):
    return lax.dot_general(left, right, (((1,), (1,)), ((), ())), preferred_element_type=F32)


def times(left, right):
    return jnp.dot(left, right, preferred_element_type=F32)


def size_of(*arrays):
    return sum(a.size * jnp.dtype(a.dtype).itemsize for a in arrays)


def constrain(x, place):
    if place == "s":
        return x
    return pltpu.with_memory_space_constraint(x, pltpu.VMEM if place == "v" else pltpu.HBM)


def call(
    body, name, outs, ins, places, scratch=(), flops=0, traffic=0, limit=4, out_places=None, aliases=None, also=()
):
    out_places = out_places or "v" * len(outs)
    shapes = [pltpu.VMEM(*o) if p == "v" else jax.ShapeDtypeStruct(*o) for o, p in zip(outs, out_places)]
    count = len(ins)

    def seen(*refs):
        body(*refs[:count], *refs[count + len(also) :])

    ins, places = (*ins, *also), places + "v" * len(also)
    return pl.pallas_call(
        seen,
        out_shape=shapes,
        in_specs=[pl.BlockSpec(memory_space=PLACES[p]) for p in places],
        out_specs=[pl.BlockSpec(memory_space=PLACES[p]) for p in out_places],
        scratch_shapes=list(scratch),
        input_output_aliases=aliases or {},
        compiler_params=pltpu.CompilerParams(vmem_limit_bytes=limit * MIB),
        cost_estimate=pl.CostEstimate(flops=flops, bytes_accessed=traffic, transcendentals=0),
        name=name,
    )(*[constrain(x, p) for x, p in zip(ins, places)])


def like(x):
    return x.shape, x.dtype


def parity():
    return lax.rem(lax.axis_index("seq"), 2)


def is_speech(arr_ref):
    return arr_ref[:, arr_ref.shape[1] - 1 :] == 0


def pack_body(kind_hbm, tok_hbm, cot_hbm, wide_ref, tall_ref, out_ref, tok_ref, cot_ref, kind_ref, sems):
    copies = [
        pltpu.make_async_copy(kind_hbm, kind_ref, sems.at[2]),
        pltpu.make_async_copy(tok_hbm, tok_ref, sems.at[0]),
        pltpu.make_async_copy(cot_hbm, cot_ref, sems.at[1]),
    ]
    for copy in copies:
        copy.start()
    width = tok_ref.shape[1]
    row = lax.broadcasted_iota(jnp.int32, (tok_ref.shape[0], 128), 0)
    kind = jnp.zeros(row.shape, F32)
    for copy in copies:
        copy.wait()
    for i in range(tok_ref.shape[0]):
        kind = jnp.where(row == i, kind_ref[i].astype(F32), kind)
    out_ref[:, 2 * width :] = kind.astype(BF16)
    out_ref[:, :width] = tok_ref[...]
    out_ref[:, width : 2 * width] = cot_ref[...]


def join_body(a_ref, b_ref, out_ref):
    both = jnp.concatenate([a_ref[...].astype(F32), b_ref[...].astype(F32)], axis=0)
    out_ref[...] = both.astype(BF16)


def join(a, b, name, also):
    return call(join_body, name, [((2 * a.shape[0], a.shape[1]), BF16)], (a, b), "vv", also=also)[0]


def column_blocks(src, wide, first):
    rows = src.shape[0] // BLOCK
    return [
        [
            (src.at[pl.ds(r * BLOCK, BLOCK), pl.ds(i * BLOCK, BLOCK)], wide.at[first + i, r])
            for r in range(rows)
        ]
        for i in range(src.shape[1] // BLOCK)
    ]


def row_blocks(src, tall, first):
    return [
        [(src.at[pl.ds(i, BLOCK)], tall.at[pl.ds(first + i, BLOCK)])] for i in range(0, src.shape[0], BLOCK)
    ]


def started(groups, sems):
    copies, count = [], 0
    for group in groups:
        copies.append([pltpu.make_async_copy(s, d, sems.at[count + i]) for i, (s, d) in enumerate(group)])
        count += len(group)
    for group in copies:
        for copy in group:
            copy.start()
    return copies


def wait(group):
    for copy in group:
        copy.wait()


def load_body(first, after_ref, src_hbm, old_ref, place_ref, sems):
    if place_ref.ndim == 4:
        groups = column_blocks(src_hbm, place_ref, first)
    else:
        groups = row_blocks(src_hbm, place_ref, first)
    for group in started(groups, sems):
        wait(group)


def load(after, src, place, also, first, name):
    return call(
        functools.partial(load_body, first),
        name,
        [like(place)],
        (after, src, place),
        "vhv",
        [pltpu.SemaphoreType.DMA((src.size // BLOCK**2,))],
        traffic=size_of(src),
        aliases={2: 0},
        also=also,
    )[0]


def beside(i, fs, ft):
    side, rest = divmod(i * BLOCK, ft // 2)
    return side * (fs // 2) + rest


def columns(wide_ref, i):
    return wide_ref[i].reshape(-1, BLOCK)


def partials_body(
    arr_ref, gs_hbm, us_hbm, ds_hbm, old_wide, old_tall, mine_ref, theirs_ref, wide_ref, tall_ref, part, sems
):
    fs, width = ds_hbm.shape
    ft = tall_ref.shape[0] - fs
    ns, nt = fs // BLOCK, ft // BLOCK
    groups = column_blocks(gs_hbm, wide_ref, 2 * nt) + column_blocks(us_hbm, wide_ref, 2 * nt + ns)
    copies = started(groups + row_blocks(ds_hbm, tall_ref, 0), sems)
    x = arr_ref[:, :width]
    c = arr_ref[:, width : 2 * width]
    speech = is_speech(arr_ref)

    def put(k, start, value, pick):
        cut = slice(start, start + BLOCK)
        if pick and start % (fs // 2) < ft // 2:
            value = jnp.where(speech, value, part[k, :, cut])
        part[k, :, cut] = value

    for k in range(2):
        for i in range(nt):
            put(k, beside(i, fs, ft), times(x, columns(wide_ref, k * nt + i)), False)
    for i in range(nt):
        rows = slice(fs + i * BLOCK, fs + (i + 1) * BLOCK)
        put(2, beside(i, fs, ft), contract_last(c, tall_ref[rows, :]), False)
    for k in range(2):
        for i in range(ns):
            wait(copies[k * ns + i])
            put(k, i * BLOCK, times(x, columns(wide_ref, 2 * nt + k * ns + i)), True)
    for i in range(ns):
        wait(copies[2 * ns + i])
        put(2, i * BLOCK, contract_last(c, tall_ref[i * BLOCK : (i + 1) * BLOCK, :]), True)
    half = fs // 2
    odd = parity()
    for k in range(3):
        mine_ref[k] = part[k, :, pl.ds(pl.multiple_of(odd * half, half), half)]
        theirs_ref[k] = part[k, :, pl.ds(pl.multiple_of((1 - odd) * half, half), half)]


def partials(arr, gate_s, up_s, down_s, wide, tall):
    rows, fs = arr.shape[0], gate_s.shape[1]
    half = ((3, rows, fs // 2), F32)
    n_sems = 2 * gate_s.size // BLOCK**2 + fs // BLOCK
    return call(
        partials_body,
        "hidden_partials",
        [half, half, like(wide), like(tall)],
        (arr, gate_s, up_s, down_s, wide, tall),
        "vhhhvv",
        [pltpu.VMEM((3, rows, fs), F32), pltpu.SemaphoreType.DMA((n_sems,))],
        2 * rows * (wide.size + tall.size),
        size_of(gate_s, up_s, down_s),
        aliases={4: 2, 5: 3},
    )


def core_sum_body(mine_ref, got_ref, sum_ref, send_ref):
    total = mine_ref[...] + got_ref[...]
    sum_ref[...] = total
    send_ref[...] = total.astype(BF16)


def hidden_body(sum_ref, got_ref, out_ref):
    total = [sum_ref[k] + got_ref[k].astype(F32) for k in range(3)]
    g, u, dh = total
    sig = jax.nn.sigmoid(g)
    silu = g * sig
    out_ref[0] = (silu * u).astype(BF16)
    out_ref[1] = (dh * u * sig * (1.0 + g * (1.0 - sig))).astype(BF16)
    out_ref[2] = (dh * silu).astype(BF16)


def turn_body(first, count, by_product, old_ref, wide_ref):
    row, col = (lax.broadcasted_iota(jnp.int32, (ROWS, ROWS), i) for i in range(2))
    one = (row == col).astype(BF16)
    for i in range(first, first + count):
        for r in range(wide_ref.shape[1]):
            square = wide_ref[i, r]
            if by_product:
                parts = [contract_last(one, square[:, j : j + ROWS]) for j in range(0, BLOCK, ROWS)]
                turned = jnp.concatenate([p.astype(BF16) for p in parts], axis=0)
            else:
                turned = square.T
            wide_ref[i, r] = turned


def turn(wide, tall, first, count, by_product, name):
    return call(
        functools.partial(turn_body, first, count, by_product),
        name,
        [like(wide)],
        (wide,),
        "v",
        traffic=4 * count * wide.shape[1] * BLOCK**2,
        aliases={0: 0},
        also=(tall,),
    )[0]


def mixed_half(h, speech, side, tall_ref, fs):
    half_s, half_t, width = fs // 2, (tall_ref.shape[0] - fs) // 2, tall_ref.shape[1]
    zero = jnp.zeros_like(h)
    hs, ht = jnp.where(speech, h, zero), jnp.where(speech, zero, h)[:, :half_t]
    rows_s = pl.ds(pl.multiple_of(side * half_s, BLOCK), half_s)
    rows_t = pl.ds(pl.multiple_of(fs + side * half_t, BLOCK), half_t)
    cuts = [slice(i, i + BLOCK) for i in range(0, width, BLOCK)]
    return [times(hs, tall_ref[rows_s, cut]) + times(ht, tall_ref[rows_t, cut]) for cut in cuts]


def mixed_own_body(arr_ref, done_ref, tall_ref, out_ref):
    fs = 2 * done_ref.shape[2]
    parts = mixed_half(done_ref[0], is_speech(arr_ref), parity(), tall_ref, fs)
    for i, value in enumerate(parts):
        out_ref[:, i * BLOCK : (i + 1) * BLOCK] = value


def back_body(
    turned, arr_ref, done_ref, other_ref, own_ref, wide_ref, tall_ref,
    keep_ref, send_ref, hs_ref, ht_ref, dgs, dgt, dus, dut, out,
):
    speech = is_speech(arr_ref)
    fs, ft = hs_ref.shape[1], ht_ref.shape[1]
    ns, nt = fs // BLOCK, ft // BLOCK
    odd = parity() == 1
    for k, (s, t) in enumerate(((hs_ref, ht_ref), (dgs, dgt), (dus, dut))):
        done, other = done_ref[k], other_ref[k]
        value = jnp.concatenate([jnp.where(odd, other, done), jnp.where(odd, done, other)], axis=1)
        zero = jnp.zeros_like(value)
        s[...] = jnp.where(speech, value, zero)
        value = jnp.where(speech, zero, value)
        for i in range(nt):
            start = beside(i, fs, ft)
            t[:, i * BLOCK : (i + 1) * BLOCK] = value[:, start : start + BLOCK]
    width = tall_ref.shape[1]
    for i, value in enumerate(mixed_half(other_ref[0], speech, 1 - parity(), tall_ref, fs)):
        cut = slice(i * BLOCK, (i + 1) * BLOCK)
        out[:, cut] = own_ref[:, cut] + value
    blocks = [(dgt, nt), (dut, nt), (dgs, ns), (dus, ns)]
    blocks = [(ref, i) for ref, n in blocks for i in range(n)]
    for r in range(width // BLOCK):
        total = jnp.zeros((out.shape[0], BLOCK), F32)
        for b, (ref, j) in enumerate(blocks):
            product = times if b in turned else contract_last
            total += product(ref[:, j * BLOCK : (j + 1) * BLOCK], wide_ref[b, r])
        start = width + r * BLOCK
        out[:, start : start + BLOCK] = total
    half = keep_ref.shape[0]
    keep_ref[...] = out[:half]
    send_ref[...] = out[half:].astype(BF16)


def back(arr, done, other, own, wide, tall, turned, fs, ft):
    rows, width = arr.shape[0], tall.shape[1]
    hidden = [((rows, fs), BF16), ((rows, ft), BF16)]
    return call(
        functools.partial(back_body, turned),
        "token_partials",
        [((rows // 2, 2 * width), F32), ((rows // 2, 2 * width), BF16)] + hidden,
        (arr, done, other, own, wide, tall),
        "vvvvvv",
        [pltpu.VMEM(*s) for s in hidden + hidden] + [pltpu.VMEM((rows, 2 * width), F32)],
        2 * rows * (wide.size + tall.size),
    )


def token_sum_body(keep_ref, got_ref, after_ref, next_ref, send_ref):
    total = keep_ref[...] + got_ref[...].astype(F32)
    half = next_ref.shape[0]
    next_ref[...] = total[:half]
    send_ref[...] = total[half:].astype(send_ref.dtype)


def token_sum(keep, got, after, dtype, name):
    rows, width = keep.shape
    outs = [((rows // 2, width), F32), ((rows // 2, width), dtype)]
    return call(token_sum_body, name, outs, (keep, got, after), "vvh")


def last_sum_body(keep_ref, got_ref, mixed_hbm, grad_hbm, mixed_ref, grad_ref, sems):
    total = (keep_ref[...] + got_ref[...].astype(F32)).astype(BF16)
    width = mixed_ref.shape[1]
    mixed_ref[...] = total[:, :width]
    grad_ref[...] = total[:, width:]
    copies = [
        pltpu.make_async_copy(mixed_ref, mixed_hbm, sems.at[0]),
        pltpu.make_async_copy(grad_ref, grad_hbm, sems.at[1]),
    ]
    for copy in copies:
        copy.start()
    for copy in copies:
        copy.wait()


def outer_steps(c, steps, slots, sems):
    copies = []
    for i, (h, place) in enumerate(steps):
        slots[i] = contract_first(h, c).astype(BF16)
        copies.append(pltpu.make_async_copy(slots.at[i], place, sems.at[i]))
        copies[-1].start()
    for copy in copies:
        copy.wait()


def outer_body(speech, text, after_ref, arr_ref, hs_ref, ht_ref, *refs):
    slots, sems = refs[-2:]
    outs = list(refs[-2 - bool(speech) - bool(text) : -2])
    width = outs[0].shape[1]
    steps = []
    for h_ref, blocks in ((hs_ref, speech), (ht_ref, text)):
        out = outs.pop(0) if blocks else None
        cuts = [slice(i * ROWS, (i + 1) * ROWS) for i in blocks]
        steps += [(h_ref[:, cut], out.at[cut]) for cut in cuts]
    outer_steps(arr_ref[:, width : 2 * width], steps, slots, sems)


def flip(value, axes, bit, n):
    return lax.ppermute(value, axes, [(i, i ^ bit) for i in range(n)])


def by_kernels(n_seq, n_tok, tokens, modality, cotangent, gate_s, up_s, down_s, gate_t, up_t, down_t):
    rows, width = tokens.shape
    fs, ft = gate_s.shape[1], gate_t.shape[1]
    wide = ((2 * (fs + ft) // BLOCK, width // BLOCK, BLOCK, BLOCK), BF16)
    tall = ((fs + ft, width), BF16)
    pair = [pltpu.VMEM((rows, width), BF16)] * 2

    packed = ((rows, 2 * width + 128), BF16)
    scratch = pair + [pltpu.SMEM((rows,), jnp.int32), pltpu.SemaphoreType.DMA((3,))]
    wide, tall, arr = call(pack_body, "pack", [wide, tall, packed], (modality, tokens, cotangent), "hhh", scratch)
    got = flip(arr, TOK, HOPS[0], n_tok)
    wide = load(arr, gate_t, wide, (tall,), 0, "load_gate_text")
    arr = join(arr, got, "join_4", (wide, tall))
    got = flip(arr, TOK, HOPS[1], n_tok)
    wide = load(arr, up_t, wide, (tall,), ft // BLOCK, "load_up_text")
    arr = join(arr, got, "join_8", (wide, tall))
    got = flip(arr, TOK, HOPS[2], n_tok)
    tall = load(arr, down_t, tall, (wide,), fs, "load_down_text")
    arr = join(arr, got, "join_16", (wide, tall))

    mine, theirs, wide, tall = partials(arr, gate_s, up_s, down_s, wide, tall)
    got = flip(theirs, "seq", 1, n_seq)
    wide = turn(wide, tall, 0, TURN_FIRST, False, "turn_1")
    total, send = call(
        core_sum_body, "core_sum", [like(mine), (mine.shape, BF16)], (mine, got), "vv", also=(wide, tall)
    )
    got = flip(send, "seq", 2, n_seq)
    wide = turn(wide, tall, TURN_FIRST, TURN_SECOND, True, "turn_2")
    done = call(hidden_body, "hidden", [(mine.shape, BF16)], (total, got), "vv", also=(wide, tall))[0]
    other = flip(done, "seq", 1, n_seq)
    own = call(
        mixed_own_body, "mixed_own", [((arr.shape[0], width), F32)], (arr, done, tall), "vvv",
        flops=arr.shape[0] * tall.size, also=(wide,),
    )[0]
    keep, send, hs, ht = back(arr, done, other, own, wide, tall, range(TURN_FIRST + TURN_SECOND), fs, ft)

    def outer(after, speech, text, old, name):
        count = len(speech) + len(text)
        outs = [like(w) for w, blocks in ((down_s, speech), (down_t, text)) if blocks]
        return call(
            functools.partial(outer_body, speech, text), name, outs, (after, arr, hs, ht, *old),
            "vvvv" + "h" * len(old), [pltpu.VMEM((count, ROWS, width), BF16), pltpu.SemaphoreType.DMA((count,))],
            2 * arr.shape[0] * count * ROWS * width, 2 * count * ROWS * width, limit=8,
            out_places="h" * len(outs), aliases={4: 0} if old else None,
        )

    ns, nt = fs // ROWS, ft // ROWS
    got = flip(send, TOK, HOPS[2], n_tok)
    down_s_grad = outer(keep, range(ns // 2), (), (), "down_grad_1")[0]
    keep, send = token_sum(keep, got, down_s_grad, BF16, "token_sum_4")

    got = flip(send, TOK, HOPS[1], n_tok)
    down_s_grad, down_t_grad = outer(keep, range(ns // 2, ns), range(1), (down_s_grad,), "down_grad_2")
    keep, send = token_sum(keep, got, down_t_grad, F32, "token_sum_2")

    got = flip(send, TOK, HOPS[0], n_tok)
    down_t_grad = outer(keep, (), range(1, nt), (down_t_grad,), "down_grad_3")[0]
    outs = [((rows, width), BF16)] * 2
    mixed, token_grad = call(last_sum_body, "token_sum_1", outs, (keep, got), "vv", pair + [pltpu.SemaphoreType.DMA((2,))], out_places="hh")
    return mixed, token_grad, down_s_grad, down_t_grad


def by_arrays(n_seq, n_tok, tokens, modality, cotangent, gate_s, up_s, down_s, gate_t, up_t, down_t):
    width = tokens.shape[1]
    ft = gate_t.shape[1]
    kind = jnp.broadcast_to(modality.astype(BF16)[:, None], (modality.shape[0], 128))
    packed = jnp.concatenate([tokens, cotangent, kind], axis=1)
    arrived = lax.all_gather(packed, TOK, axis=0, tiled=True)
    rows, grads = arrived[:, :width], arrived[:, width : 2 * width]
    speech = arrived[:, 2 * width : 2 * width + 1] == 0

    def pick(s, t):
        return jnp.concatenate([jnp.where(speech, s[:, :ft], t), s[:, ft:]], axis=1)

    def halves(v):
        zero = jnp.zeros((), v.dtype)
        return jnp.where(speech, v, zero), jnp.where(speech, zero, v[:, :ft])

    g = pick(times(rows, gate_s), times(rows, gate_t))
    u = pick(times(rows, up_s), times(rows, up_t))
    dh = pick(contract_last(grads, down_s), contract_last(grads, down_t))
    sums = jnp.stack([g, u, dh])
    sums = sums + flip(sums, "seq", 1, n_seq)
    g, u, dh = sums + flip(sums.astype(BF16), "seq", 2, n_seq).astype(F32)
    sig = jax.nn.sigmoid(g)
    h = (g * sig * u).astype(BF16)
    dg = (dh * u * sig * (1.0 + g * (1.0 - sig))).astype(BF16)
    du = (dh * (g * sig)).astype(BF16)
    (hs, ht), (dgs, dgt), (dus, dut) = halves(h), halves(dg), halves(du)
    mixed = times(hs, down_s) + times(ht, down_t)
    grad = contract_last(dgs, gate_s) + contract_last(dus, up_s)
    grad = grad + contract_last(dgt, gate_t) + contract_last(dut, up_t)
    out = jnp.concatenate([mixed, grad], axis=1).astype(BF16)
    out = out.reshape(n_tok, out.shape[0] // n_tok, out.shape[1])
    out = lax.all_to_all(out, TOK, split_axis=0, concat_axis=0, tiled=True)
    total = jnp.sum(out.astype(F32), axis=0).astype(BF16)
    down_s_grad = contract_first(hs, grads).astype(BF16)
    down_t_grad = contract_first(ht, grads).astype(BF16)
    return total[:, :width], total[:, width:], down_s_grad, down_t_grad


def solution(mesh):
    n_seq, n_tok = mesh.shape["seq"], mesh.shape["attn"] * mesh.shape["exp"]

    def run(*args):
        fs, ft, width = args[3].shape[1], args[6].shape[1], args[0].shape[1]
        fits = n_tok == 8 and args[0].shape[0] == 2 and fs >= ft and ft % (4 * BLOCK) == 0
        fits = fits and fs % (2 * BLOCK) == 0 and width % BLOCK == 0
        return (by_kernels if fits else by_arrays)(n_seq, n_tok, *args)

    return jax.shard_map(
        run,
        mesh=mesh,
        in_specs=(
            P(TOK, "seq"),
            P(TOK),
            P(TOK, "seq"),
            P("seq", TOK),
            P("seq", TOK),
            P(TOK, "seq"),
            P("seq", TOK),
            P("seq", TOK),
            P(TOK, "seq"),
        ),
        out_specs=(P(TOK, "seq"),) * 4,
        check_vma=False,
    )
```

```python
import functools

import jax
import jax.numpy as jnp
from jax import lax
from jax.experimental import pallas as pl
from jax.experimental.pallas import tpu as pltpu
from jax.sharding import PartitionSpec as P

TOK = ("attn", "exp")
HOPS = (2, 1, 4)
F32 = jnp.float32
BF16 = jnp.bfloat16
MIB = 1 << 20
BLOCK = 512
ROWS = 256
TURN_FIRST = 4
TURN_SECOND = 13
PLACES = {"h": pl.ANY, "v": pltpu.VMEM, "s": pltpu.SMEM}


def contract_first(left, right):
    return lax.dot_general(left, right, (((0,), (0,)), ((), ())), preferred_element_type=F32)


def contract_last(left, right):
    return lax.dot_general(left, right, (((1,), (1,)), ((), ())), preferred_element_type=F32)


def times(left, right):
    return jnp.dot(left, right, preferred_element_type=F32)


def size_of(*arrays):
    return sum(a.size * jnp.dtype(a.dtype).itemsize for a in arrays)


def constrain(x, place):
    if place == "s":
        return x
    return pltpu.with_memory_space_constraint(x, pltpu.VMEM if place == "v" else pltpu.HBM)


def call(
    body, name, outs, ins, places, scratch=(), flops=0, traffic=0, limit=4, out_places=None, aliases=None, also=()
):
    out_places = out_places or "v" * len(outs)
    shapes = [pltpu.VMEM(*o) if p == "v" else jax.ShapeDtypeStruct(*o) for o, p in zip(outs, out_places)]
    count = len(ins)

    def seen(*refs):
        body(*refs[:count], *refs[count + len(also) :])

    ins, places = (*ins, *also), places + "v" * len(also)
    return pl.pallas_call(
        seen,
        out_shape=shapes,
        in_specs=[pl.BlockSpec(memory_space=PLACES[p]) for p in places],
        out_specs=[pl.BlockSpec(memory_space=PLACES[p]) for p in out_places],
        scratch_shapes=list(scratch),
        input_output_aliases=aliases or {},
        compiler_params=pltpu.CompilerParams(vmem_limit_bytes=limit * MIB),
        cost_estimate=pl.CostEstimate(flops=flops, bytes_accessed=traffic, transcendentals=0),
        name=name,
    )(*[constrain(x, p) for x, p in zip(ins, places)])


def like(x):
    return x.shape, x.dtype


def parity():
    return lax.rem(lax.axis_index("seq"), 2)


def is_speech(arr_ref):
    return arr_ref[:, arr_ref.shape[1] - 1 :] == 0


def pack_body(kind_hbm, tok_hbm, cot_hbm, wide_ref, tall_ref, out_ref, tok_ref, cot_ref, kind_ref, sems):
    copies = [
        pltpu.make_async_copy(kind_hbm, kind_ref, sems.at[2]),
        pltpu.make_async_copy(tok_hbm, tok_ref, sems.at[0]),
        pltpu.make_async_copy(cot_hbm, cot_ref, sems.at[1]),
    ]
    for copy in copies:
        copy.start()
    width = tok_ref.shape[1]
    row = lax.broadcasted_iota(jnp.int32, (tok_ref.shape[0], 128), 0)
    kind = jnp.zeros(row.shape, F32)
    for copy in copies:
        copy.wait()
    for i in range(tok_ref.shape[0]):
        kind = jnp.where(row == i, kind_ref[i].astype(F32), kind)
    out_ref[:, 2 * width :] = kind.astype(BF16)
    out_ref[:, :width] = tok_ref[...]
    out_ref[:, width : 2 * width] = cot_ref[...]


def join_body(a_ref, b_ref, out_ref):
    both = jnp.concatenate([a_ref[...].astype(F32), b_ref[...].astype(F32)], axis=0)
    out_ref[...] = both.astype(BF16)


def join(a, b, name, also):
    return call(join_body, name, [((2 * a.shape[0], a.shape[1]), BF16)], (a, b), "vv", also=also)[0]


def column_blocks(src, wide, first):
    rows = src.shape[0] // BLOCK
    return [
        [
            (src.at[pl.ds(r * BLOCK, BLOCK), pl.ds(i * BLOCK, BLOCK)], wide.at[first + i, r])
            for r in range(rows)
        ]
        for i in range(src.shape[1] // BLOCK)
    ]


def row_blocks(src, tall, first, rows):
    return [[(src.at[pl.ds(i, BLOCK)], tall.at[pl.ds(first + i, BLOCK)])] for i in range(*rows, BLOCK)]


def started(groups, sems):
    copies, count = [], 0
    for group in groups:
        copies.append([pltpu.make_async_copy(s, d, sems.at[count + i]) for i, (s, d) in enumerate(group)])
        count += len(group)
    for group in copies:
        for copy in group:
            copy.start()
    return copies


def wait(group):
    for copy in group:
        copy.wait()


def load_body(first, rows, after_ref, src_hbm, old_ref, place_ref, sems):
    if place_ref.ndim == 4:
        groups = column_blocks(src_hbm, place_ref, first)
    else:
        groups = row_blocks(src_hbm, place_ref, first, (0, rows))
    for group in started(groups, sems):
        wait(group)


def load(after, src, place, also, first, name, rows=None):
    return call(
        functools.partial(load_body, first, rows or src.shape[0]),
        name,
        [like(place)],
        (after, src, place),
        "vhv",
        [pltpu.SemaphoreType.DMA((src.size // BLOCK**2,))],
        traffic=size_of(src),
        aliases={2: 0},
        also=also,
    )[0]


def beside(i, fs, ft):
    side, rest = divmod(i * BLOCK, ft // 2)
    return side * (fs // 2) + rest


def columns(wide_ref, i):
    return wide_ref[i].reshape(-1, BLOCK)


def partials_body(
    early, arr_ref, ut_ref, gs_hbm, us_hbm, ds_hbm, old_wide, old_tall, mine_ref, theirs_ref, wide_ref, tall_ref, part, sems
):
    fs, width = ds_hbm.shape
    ft = tall_ref.shape[0] - fs
    ns, nt = fs // BLOCK, ft // BLOCK
    groups = column_blocks(gs_hbm, wide_ref, 2 * nt) + column_blocks(us_hbm, wide_ref, 2 * nt + ns)
    copies = started(groups + row_blocks(ds_hbm, tall_ref, 0, (early, fs)) + column_blocks(ut_ref, wide_ref, nt), sems)
    x = arr_ref[:, :width]
    c = arr_ref[:, width : 2 * width]
    speech = is_speech(arr_ref)

    def put(k, start, value, pick):
        cut = slice(start, start + BLOCK)
        if pick and start % (fs // 2) < ft // 2:
            value = jnp.where(speech, value, part[k, :, cut])
        part[k, :, cut] = value

    for k in range(2):
        for i in range(nt):
            block = columns(wide_ref, i) if k == 0 else ut_ref[:, i * BLOCK : (i + 1) * BLOCK]
            put(k, beside(i, fs, ft), times(x, block), False)
    for i in range(nt):
        rows = slice(fs + i * BLOCK, fs + (i + 1) * BLOCK)
        put(2, beside(i, fs, ft), contract_last(c, tall_ref[rows, :]), False)
    for k in range(2):
        for i in range(ns):
            wait(copies[k * ns + i])
            put(k, i * BLOCK, times(x, columns(wide_ref, 2 * nt + k * ns + i)), True)
    for i in range(ns):
        if i * BLOCK >= early:
            wait(copies[2 * ns + i - early // BLOCK])
        put(2, i * BLOCK, contract_last(c, tall_ref[i * BLOCK : (i + 1) * BLOCK, :]), True)
    for group in copies[3 * ns - early // BLOCK :]:
        wait(group)
    half = fs // 2
    odd = parity()
    for k in range(3):
        mine_ref[k] = part[k, :, pl.ds(pl.multiple_of(odd * half, half), half)]
        theirs_ref[k] = part[k, :, pl.ds(pl.multiple_of((1 - odd) * half, half), half)]


def partials(early, arr, up_t, gate_s, up_s, down_s, wide, tall):
    rows, fs = arr.shape[0], gate_s.shape[1]
    half = ((3, rows, fs // 2), F32)
    n_sems = (2 * gate_s.size + up_t.size) // BLOCK**2 + fs // BLOCK
    return call(
        functools.partial(partials_body, early),
        "hidden_partials",
        [half, half, like(wide), like(tall)],
        (arr, up_t, gate_s, up_s, down_s, wide, tall),
        "vvhhhvv",
        [pltpu.VMEM((3, rows, fs), F32), pltpu.SemaphoreType.DMA((n_sems,))],
        2 * rows * (wide.size + tall.size),
        size_of(gate_s, up_s, down_s),
        aliases={5: 2, 6: 3},
    )


def core_sum_body(mine_ref, got_ref, sum_ref, send_ref):
    total = mine_ref[...] + got_ref[...]
    sum_ref[...] = total
    send_ref[...] = total.astype(BF16)


def hidden_body(sum_ref, got_ref, out_ref):
    total = [sum_ref[k] + got_ref[k].astype(F32) for k in range(3)]
    g, u, dh = total
    sig = jax.nn.sigmoid(g)
    silu = g * sig
    out_ref[0] = (silu * u).astype(BF16)
    out_ref[1] = (dh * u * sig * (1.0 + g * (1.0 - sig))).astype(BF16)
    out_ref[2] = (dh * silu).astype(BF16)


def turn_body(first, count, old_ref, wide_ref):
    row, col = (lax.broadcasted_iota(jnp.int32, (ROWS, ROWS), i) for i in range(2))
    one = (row == col).astype(BF16)
    squares = wide_ref.shape[1]
    for n in range(count * squares):
        i, r = first + n // squares, n % squares
        square = wide_ref[i, r]
        if n % 2:
            turned = square.T
        else:
            parts = [contract_last(one, square[:, j : j + ROWS]) for j in range(0, BLOCK, ROWS)]
            turned = jnp.concatenate([p.astype(BF16) for p in parts], axis=0)
        wide_ref[i, r] = turned


def turn(wide, tall, first, count, name):
    return call(
        functools.partial(turn_body, first, count),
        name,
        [like(wide)],
        (wide,),
        "v",
        traffic=4 * count * wide.shape[1] * BLOCK**2,
        aliases={0: 0},
        also=(tall,),
    )[0]


def mixed_half(h, speech, side, tall_ref, fs):
    half_s, half_t, width = fs // 2, (tall_ref.shape[0] - fs) // 2, tall_ref.shape[1]
    zero = jnp.zeros_like(h)
    hs, ht = jnp.where(speech, h, zero), jnp.where(speech, zero, h)[:, :half_t]
    rows_s = pl.ds(pl.multiple_of(side * half_s, BLOCK), half_s)
    rows_t = pl.ds(pl.multiple_of(fs + side * half_t, BLOCK), half_t)
    cuts = [slice(i, i + BLOCK) for i in range(0, width, BLOCK)]
    return [times(hs, tall_ref[rows_s, cut]) + times(ht, tall_ref[rows_t, cut]) for cut in cuts]


def mixed_own_body(arr_ref, done_ref, tall_ref, out_ref):
    fs = 2 * done_ref.shape[2]
    parts = mixed_half(done_ref[0], is_speech(arr_ref), parity(), tall_ref, fs)
    for i, value in enumerate(parts):
        out_ref[:, i * BLOCK : (i + 1) * BLOCK] = value


def back_body(
    turned, arr_ref, done_ref, other_ref, own_ref, wide_ref, tall_ref,
    keep_ref, send_ref, hs_ref, ht_ref, dgs, dgt, dus, dut, out,
):
    speech = is_speech(arr_ref)
    fs, ft = hs_ref.shape[1], ht_ref.shape[1]
    ns, nt = fs // BLOCK, ft // BLOCK
    odd = parity() == 1
    for k, (s, t) in enumerate(((hs_ref, ht_ref), (dgs, dgt), (dus, dut))):
        done, other = done_ref[k], other_ref[k]
        value = jnp.concatenate([jnp.where(odd, other, done), jnp.where(odd, done, other)], axis=1)
        zero = jnp.zeros_like(value)
        s[...] = jnp.where(speech, value, zero)
        value = jnp.where(speech, zero, value)
        for i in range(nt):
            start = beside(i, fs, ft)
            t[:, i * BLOCK : (i + 1) * BLOCK] = value[:, start : start + BLOCK]
    width = tall_ref.shape[1]
    for i, value in enumerate(mixed_half(other_ref[0], speech, 1 - parity(), tall_ref, fs)):
        cut = slice(i * BLOCK, (i + 1) * BLOCK)
        out[:, cut] = own_ref[:, cut] + value
    blocks = [(dgt, nt), (dut, nt), (dgs, ns), (dus, ns)]
    blocks = [(ref, i) for ref, n in blocks for i in range(n)]
    for r in range(width // BLOCK):
        total = jnp.zeros((out.shape[0], BLOCK), F32)
        for b, (ref, j) in enumerate(blocks):
            product = times if b in turned else contract_last
            total += product(ref[:, j * BLOCK : (j + 1) * BLOCK], wide_ref[b, r])
        start = width + r * BLOCK
        out[:, start : start + BLOCK] = total
    half = keep_ref.shape[0]
    keep_ref[...] = out[:half]
    send_ref[...] = out[half:].astype(BF16)


def back(arr, done, other, own, wide, tall, turned, fs, ft):
    rows, width = arr.shape[0], tall.shape[1]
    hidden = [((rows, fs), BF16), ((rows, ft), BF16)]
    return call(
        functools.partial(back_body, turned),
        "token_partials",
        [((rows // 2, 2 * width), F32), ((rows // 2, 2 * width), BF16)] + hidden,
        (arr, done, other, own, wide, tall),
        "vvvvvv",
        [pltpu.VMEM(*s) for s in hidden + hidden] + [pltpu.VMEM((rows, 2 * width), F32)],
        2 * rows * (wide.size + tall.size),
    )


def token_sum_body(keep_ref, got_ref, after_ref, next_ref, send_ref):
    total = keep_ref[...] + got_ref[...].astype(F32)
    half = next_ref.shape[0]
    next_ref[...] = total[:half]
    send_ref[...] = total[half:].astype(send_ref.dtype)


def token_sum(keep, got, after, dtype, name):
    rows, width = keep.shape
    outs = [((rows // 2, width), F32), ((rows // 2, width), dtype)]
    return call(token_sum_body, name, outs, (keep, got, after), "vvh")


def last_sum_body(keep_ref, got_ref, mixed_hbm, grad_hbm, mixed_ref, grad_ref, sems):
    total = (keep_ref[...] + got_ref[...].astype(F32)).astype(BF16)
    width = mixed_ref.shape[1]
    mixed_ref[...] = total[:, :width]
    grad_ref[...] = total[:, width:]
    copies = [
        pltpu.make_async_copy(mixed_ref, mixed_hbm, sems.at[0]),
        pltpu.make_async_copy(grad_ref, grad_hbm, sems.at[1]),
    ]
    for copy in copies:
        copy.start()
    for copy in copies:
        copy.wait()


def outer_steps(c, steps, slots, sems):
    copies = []
    for i, (h, place) in enumerate(steps):
        slots[i] = contract_first(h, c).astype(BF16)
        copies.append(pltpu.make_async_copy(slots.at[i], place, sems.at[i]))
        copies[-1].start()
    for copy in copies:
        copy.wait()


def outer_body(speech, text, after_ref, arr_ref, hs_ref, ht_ref, *refs):
    slots, sems = refs[-2:]
    outs = list(refs[-2 - bool(speech) - bool(text) : -2])
    width = outs[0].shape[1]
    steps = []
    for h_ref, blocks in ((hs_ref, speech), (ht_ref, text)):
        out = outs.pop(0) if blocks else None
        cuts = [slice(i * ROWS, (i + 1) * ROWS) for i in blocks]
        steps += [(h_ref[:, cut], out.at[cut]) for cut in cuts]
    outer_steps(arr_ref[:, width : 2 * width], steps, slots, sems)


def flip(value, axes, bit, n):
    return lax.ppermute(value, axes, [(i, i ^ bit) for i in range(n)])


def by_kernels(n_seq, n_tok, tokens, modality, cotangent, gate_s, up_s, down_s, gate_t, up_t, down_t):
    rows, width = tokens.shape
    fs, ft = gate_s.shape[1], gate_t.shape[1]
    wide = ((2 * (fs + ft) // BLOCK, width // BLOCK, BLOCK, BLOCK), BF16)
    tall = ((fs + ft, width), BF16)
    pair = [pltpu.VMEM((rows, width), BF16)] * 2

    packed = ((rows, 2 * width + 128), BF16)
    scratch = pair + [pltpu.SMEM((rows,), jnp.int32), pltpu.SemaphoreType.DMA((3,))]
    wide, tall, arr = call(pack_body, "pack", [wide, tall, packed], (modality, tokens, cotangent), "hhh", scratch)
    up_t, arr = lax.optimization_barrier((up_t, arr))
    up_t = flip(up_t, "seq", 0, n_seq)
    got = flip(arr, TOK, HOPS[0], n_tok)
    wide = load(arr, gate_t, wide, (tall,), 0, "load_gate_text")
    arr = join(arr, got, "join_4", (wide, tall))
    got = flip(arr, TOK, HOPS[1], n_tok)
    tall = load(arr, down_s, tall, (wide,), 0, "load_down_speech", ft)
    arr = join(arr, got, "join_8", (wide, tall))
    got = flip(arr, TOK, HOPS[2], n_tok)
    tall = load(arr, down_t, tall, (wide,), fs, "load_down_text")
    arr = join(arr, got, "join_16", (wide, tall))

    mine, theirs, wide, tall = partials(ft, arr, up_t, gate_s, up_s, down_s, wide, tall)
    got = flip(theirs, "seq", 1, n_seq)
    wide = turn(wide, tall, 0, TURN_FIRST, "turn_1")
    total, send = call(
        core_sum_body, "core_sum", [like(mine), (mine.shape, BF16)], (mine, got), "vv", also=(wide, tall)
    )
    got = flip(send, "seq", 2, n_seq)
    wide = turn(wide, tall, TURN_FIRST, TURN_SECOND, "turn_2")
    done = call(hidden_body, "hidden", [(mine.shape, BF16)], (total, got), "vv", also=(wide, tall))[0]
    other = flip(done, "seq", 1, n_seq)
    own = call(
        mixed_own_body, "mixed_own", [((arr.shape[0], width), F32)], (arr, done, tall), "vvv",
        flops=arr.shape[0] * tall.size, also=(wide,),
    )[0]
    keep, send, hs, ht = back(arr, done, other, own, wide, tall, range(TURN_FIRST + TURN_SECOND), fs, ft)

    def outer(after, speech, text, old, name):
        count = len(speech) + len(text)
        outs = [like(w) for w, blocks in ((down_s, speech), (down_t, text)) if blocks]
        return call(
            functools.partial(outer_body, speech, text), name, outs, (after, arr, hs, ht, *old),
            "vvvv" + "h" * len(old), [pltpu.VMEM((count, ROWS, width), BF16), pltpu.SemaphoreType.DMA((count,))],
            2 * arr.shape[0] * count * ROWS * width, 2 * count * ROWS * width, limit=8,
            out_places="h" * len(outs), aliases={4: 0} if old else None,
        )

    ns, nt = fs // ROWS, ft // ROWS
    got = flip(send, TOK, HOPS[2], n_tok)
    down_s_grad = outer(keep, range(ns // 2), (), (), "down_grad_1")[0]
    keep, send = token_sum(keep, got, down_s_grad, BF16, "token_sum_4")

    got = flip(send, TOK, HOPS[1], n_tok)
    down_s_grad, down_t_grad = outer(keep, range(ns // 2, ns), range(1), (down_s_grad,), "down_grad_2")
    keep, send = token_sum(keep, got, down_t_grad, F32, "token_sum_2")

    got = flip(send, TOK, HOPS[0], n_tok)
    down_t_grad = outer(keep, (), range(1, nt), (down_t_grad,), "down_grad_3")[0]
    outs = [((rows, width), BF16)] * 2
    mixed, token_grad = call(last_sum_body, "token_sum_1", outs, (keep, got), "vv", pair + [pltpu.SemaphoreType.DMA((2,))], out_places="hh")
    return mixed, token_grad, down_s_grad, down_t_grad


def by_arrays(n_seq, n_tok, tokens, modality, cotangent, gate_s, up_s, down_s, gate_t, up_t, down_t):
    width = tokens.shape[1]
    ft = gate_t.shape[1]
    kind = jnp.broadcast_to(modality.astype(BF16)[:, None], (modality.shape[0], 128))
    packed = jnp.concatenate([tokens, cotangent, kind], axis=1)
    arrived = lax.all_gather(packed, TOK, axis=0, tiled=True)
    rows, grads = arrived[:, :width], arrived[:, width : 2 * width]
    speech = arrived[:, 2 * width : 2 * width + 1] == 0

    def pick(s, t):
        return jnp.concatenate([jnp.where(speech, s[:, :ft], t), s[:, ft:]], axis=1)

    def halves(v):
        zero = jnp.zeros((), v.dtype)
        return jnp.where(speech, v, zero), jnp.where(speech, zero, v[:, :ft])

    g = pick(times(rows, gate_s), times(rows, gate_t))
    u = pick(times(rows, up_s), times(rows, up_t))
    dh = pick(contract_last(grads, down_s), contract_last(grads, down_t))
    sums = jnp.stack([g, u, dh])
    sums = sums + flip(sums, "seq", 1, n_seq)
    g, u, dh = sums + flip(sums.astype(BF16), "seq", 2, n_seq).astype(F32)
    sig = jax.nn.sigmoid(g)
    h = (g * sig * u).astype(BF16)
    dg = (dh * u * sig * (1.0 + g * (1.0 - sig))).astype(BF16)
    du = (dh * (g * sig)).astype(BF16)
    (hs, ht), (dgs, dgt), (dus, dut) = halves(h), halves(dg), halves(du)
    mixed = times(hs, down_s) + times(ht, down_t)
    grad = contract_last(dgs, gate_s) + contract_last(dus, up_s)
    grad = grad + contract_last(dgt, gate_t) + contract_last(dut, up_t)
    out = jnp.concatenate([mixed, grad], axis=1).astype(BF16)
    out = out.reshape(n_tok, out.shape[0] // n_tok, out.shape[1])
    out = lax.all_to_all(out, TOK, split_axis=0, concat_axis=0, tiled=True)
    total = jnp.sum(out.astype(F32), axis=0).astype(BF16)
    down_s_grad = contract_first(hs, grads).astype(BF16)
    down_t_grad = contract_first(ht, grads).astype(BF16)
    return total[:, :width], total[:, width:], down_s_grad, down_t_grad


def solution(mesh):
    n_seq, n_tok = mesh.shape["seq"], mesh.shape["attn"] * mesh.shape["exp"]

    def run(*args):
        fs, ft, width = args[3].shape[1], args[6].shape[1], args[0].shape[1]
        fits = n_tok == 8 and args[0].shape[0] == 2 and fs >= ft and ft % (4 * BLOCK) == 0
        fits = fits and fs % (2 * BLOCK) == 0 and width % BLOCK == 0
        return (by_kernels if fits else by_arrays)(n_seq, n_tok, *args)

    return jax.shard_map(
        run,
        mesh=mesh,
        in_specs=(
            P(TOK, "seq"),
            P(TOK),
            P(TOK, "seq"),
            P("seq", TOK),
            P("seq", TOK),
            P(TOK, "seq"),
            P("seq", TOK),
            P("seq", TOK),
            P(TOK, "seq"),
        ),
        out_specs=(P(TOK, "seq"),) * 4,
        check_vma=False,
    )
```

```python
import functools

import jax
import jax.numpy as jnp
from jax import lax
from jax.experimental import pallas as pl
from jax.experimental.pallas import tpu as pltpu
from jax.sharding import PartitionSpec as P

TOK = ("attn", "exp")
HOPS = (2, 1, 4)
F32 = jnp.float32
BF16 = jnp.bfloat16
MIB = 1 << 20
BLOCK = 512
WIDE = 1024
ROWS = 256
TURN_FIRST = 5
PLACES = {"h": pl.ANY, "v": pltpu.VMEM, "s": pltpu.SMEM}


def contract_first(left, right):
    return lax.dot_general(left, right, (((0,), (0,)), ((), ())), preferred_element_type=F32)


def contract_last(left, right):
    return lax.dot_general(left, right, (((1,), (1,)), ((), ())), preferred_element_type=F32)


def times(left, right):
    return jnp.dot(left, right, preferred_element_type=F32)


def size_of(*arrays):
    return sum(a.size * jnp.dtype(a.dtype).itemsize for a in arrays)


def constrain(x, place):
    if place == "s":
        return x
    return pltpu.with_memory_space_constraint(x, pltpu.VMEM if place == "v" else pltpu.HBM)


def call(
    body, name, outs, ins, places, scratch=(), flops=0, traffic=0, limit=4, out_places=None, aliases=None, also=()
):
    out_places = out_places or "v" * len(outs)
    shapes = [pltpu.VMEM(*o) if p == "v" else jax.ShapeDtypeStruct(*o) for o, p in zip(outs, out_places)]
    count = len(ins)

    def seen(*refs):
        body(*refs[:count], *refs[count + len(also) :])

    ins, places = (*ins, *also), places + "v" * len(also)
    return pl.pallas_call(
        seen,
        out_shape=shapes,
        in_specs=[pl.BlockSpec(memory_space=PLACES[p]) for p in places],
        out_specs=[pl.BlockSpec(memory_space=PLACES[p]) for p in out_places],
        scratch_shapes=list(scratch),
        input_output_aliases=aliases or {},
        compiler_params=pltpu.CompilerParams(vmem_limit_bytes=limit * MIB),
        cost_estimate=pl.CostEstimate(flops=flops, bytes_accessed=traffic, transcendentals=0),
        name=name,
    )(*[constrain(x, p) for x, p in zip(ins, places)])


def like(x):
    return x.shape, x.dtype


def parity():
    return lax.rem(lax.axis_index("seq"), 2)


def is_speech(arr_ref):
    return arr_ref[:, arr_ref.shape[1] - 1 :] == 0


def pack_body(kind_hbm, tok_hbm, cot_hbm, wide_ref, tall_ref, out_ref, tok_ref, cot_ref, kind_ref, sems):
    copies = [
        pltpu.make_async_copy(kind_hbm, kind_ref, sems.at[2]),
        pltpu.make_async_copy(tok_hbm, tok_ref, sems.at[0]),
        pltpu.make_async_copy(cot_hbm, cot_ref, sems.at[1]),
    ]
    for copy in copies:
        copy.start()
    width = tok_ref.shape[1]
    row = lax.broadcasted_iota(jnp.int32, (tok_ref.shape[0], 128), 0)
    kind = jnp.zeros(row.shape, F32)
    for copy in copies:
        copy.wait()
    for i in range(tok_ref.shape[0]):
        kind = jnp.where(row == i, kind_ref[i].astype(F32), kind)
    out_ref[:, 2 * width :] = kind.astype(BF16)
    out_ref[:, :width] = tok_ref[...]
    out_ref[:, width : 2 * width] = cot_ref[...]


def join_body(a_ref, b_ref, out_ref):
    both = jnp.concatenate([a_ref[...].astype(F32), b_ref[...].astype(F32)], axis=0)
    out_ref[...] = both.astype(BF16)


def join(a, b, name, also):
    return call(join_body, name, [((2 * a.shape[0], a.shape[1]), BF16)], (a, b), "vv", also=also)[0]


def column_blocks(src, wide, first, cuts):
    rows = src.shape[0] // cuts
    parts = [pl.ds(j * rows, rows) for j in range(cuts)]
    return [
        [(src.at[part, pl.ds(i * WIDE, WIDE)], wide.at[first + i, part]) for part in parts]
        for i in range(src.shape[1] // WIDE)
    ]


def square_at(wide_ref, i, r):
    per = WIDE // BLOCK
    return wide_ref.at[i // per, pl.ds(r * BLOCK, BLOCK), pl.ds(i % per * BLOCK, BLOCK)]


def row_blocks(src, tall, first):
    return [
        [(src.at[pl.ds(i, BLOCK)], tall.at[pl.ds(first + i, BLOCK)])] for i in range(0, src.shape[0], BLOCK)
    ]


def started(groups, sems):
    copies, count = [], 0
    for group in groups:
        copies.append([pltpu.make_async_copy(s, d, sems.at[count + i]) for i, (s, d) in enumerate(group)])
        count += len(group)
    for group in copies:
        for copy in group:
            copy.start()
    return copies


def wait(group):
    for copy in group:
        copy.wait()


def load_body(first, after_ref, src_hbm, old_ref, place_ref, sems):
    if place_ref.ndim == 3:
        groups = column_blocks(src_hbm, place_ref, first, 4)
    else:
        groups = row_blocks(src_hbm, place_ref, first)
    for group in started(groups, sems):
        wait(group)


def load(after, src, place, also, first, name):
    return call(
        functools.partial(load_body, first),
        name,
        [like(place)],
        (after, src, place),
        "vhv",
        [pltpu.SemaphoreType.DMA((8,))],
        traffic=size_of(src),
        aliases={2: 0},
        also=also,
    )[0]


def beside(i, fs, ft):
    side, rest = divmod(i * BLOCK, ft // 2)
    return side * (fs // 2) + rest


def partials_body(
    arr_ref, gs_hbm, us_hbm, ds_hbm, old_wide, old_tall, mine_ref, theirs_ref, wide_ref, tall_ref, part, sems
):
    fs, width = ds_hbm.shape
    ft = tall_ref.shape[0] - fs
    ns, nt = fs // WIDE, ft // WIDE
    groups = column_blocks(gs_hbm, wide_ref, 2 * nt, 2) + column_blocks(us_hbm, wide_ref, 2 * nt + ns, 2)
    copies = started(groups + row_blocks(ds_hbm, tall_ref, 0), sems)
    x = arr_ref[:, :width]
    c = arr_ref[:, width : 2 * width]
    speech = is_speech(arr_ref)

    def put(k, start, value, pick):
        cut = slice(start, start + BLOCK)
        if pick and start % (fs // 2) < ft // 2:
            value = jnp.where(speech, value, part[k, :, cut])
        part[k, :, cut] = value

    def put_wide(k, start, value, pick):
        for i in range(start, start + WIDE, BLOCK):
            place = i if pick else beside(i // BLOCK, fs, ft)
            put(k, place, value[:, i - start : i - start + BLOCK], pick)

    for k in range(2):
        for i in range(nt):
            put_wide(k, i * WIDE, times(x, wide_ref[k * nt + i]), False)
    for i in range(ft // BLOCK):
        rows = slice(fs + i * BLOCK, fs + (i + 1) * BLOCK)
        put(2, beside(i, fs, ft), contract_last(c, tall_ref[rows, :]), False)
    for k in range(2):
        for i in range(ns):
            wait(copies[k * ns + i])
            put_wide(k, i * WIDE, times(x, wide_ref[2 * nt + k * ns + i]), True)
    for i in range(fs // BLOCK):
        wait(copies[2 * ns + i])
        put(2, i * BLOCK, contract_last(c, tall_ref[i * BLOCK : (i + 1) * BLOCK, :]), True)
    half = fs // 2
    odd = parity()
    for k in range(3):
        mine_ref[k] = part[k, :, pl.ds(pl.multiple_of(odd * half, half), half)]
        theirs_ref[k] = part[k, :, pl.ds(pl.multiple_of((1 - odd) * half, half), half)]


def partials(arr, gate_s, up_s, down_s, wide, tall):
    rows, fs = arr.shape[0], gate_s.shape[1]
    half = ((3, rows, fs // 2), F32)
    n_sems = 4 * fs // WIDE + fs // BLOCK
    return call(
        partials_body,
        "hidden_partials",
        [half, half, like(wide), like(tall)],
        (arr, gate_s, up_s, down_s, wide, tall),
        "vhhhvv",
        [pltpu.VMEM((3, rows, fs), F32), pltpu.SemaphoreType.DMA((n_sems,))],
        2 * rows * (wide.size + tall.size),
        size_of(gate_s, up_s, down_s),
        aliases={4: 2, 5: 3},
    )


def core_sum_body(mine_ref, got_ref, sum_ref, send_ref):
    total = mine_ref[...] + got_ref[...]
    sum_ref[...] = total
    send_ref[...] = total.astype(BF16)


def hidden_body(sum_ref, got_ref, out_ref):
    total = [sum_ref[k] + got_ref[k].astype(F32) for k in range(3)]
    g, u, dh = total
    sig = jax.nn.sigmoid(g)
    silu = g * sig
    out_ref[0] = (silu * u).astype(BF16)
    out_ref[1] = (dh * u * sig * (1.0 + g * (1.0 - sig))).astype(BF16)
    out_ref[2] = (dh * silu).astype(BF16)


def turn_body(first, count, old_ref, wide_ref):
    row, col = (lax.broadcasted_iota(jnp.int32, (ROWS, ROWS), i) for i in range(2))
    one = (row == col).astype(BF16)
    squares = wide_ref.shape[1] // BLOCK
    for n in range(count * squares):
        i, r = first + n // squares, n % squares
        place = square_at(wide_ref, i, r)
        square = place[...]
        if n % 2:
            turned = square.T
        else:
            parts = [contract_last(one, square[:, j : j + ROWS]) for j in range(0, BLOCK, ROWS)]
            turned = jnp.concatenate([p.astype(BF16) for p in parts], axis=0)
        place[...] = turned


def turn(wide, tall, first, count, name):
    return call(
        functools.partial(turn_body, first, count),
        name,
        [like(wide)],
        (wide,),
        "v",
        traffic=4 * count * wide.shape[1] * BLOCK,
        aliases={0: 0},
        also=(tall,),
    )[0]


def mixed_half(h, speech, side, tall_ref, fs):
    half_s, half_t, width = fs // 2, (tall_ref.shape[0] - fs) // 2, tall_ref.shape[1]
    zero = jnp.zeros_like(h)
    hs, ht = jnp.where(speech, h, zero), jnp.where(speech, zero, h)[:, :half_t]
    rows_s = pl.ds(pl.multiple_of(side * half_s, BLOCK), half_s)
    rows_t = pl.ds(pl.multiple_of(fs + side * half_t, BLOCK), half_t)
    cuts = [slice(i, i + BLOCK) for i in range(0, width, BLOCK)]
    return [times(hs, tall_ref[rows_s, cut]) + times(ht, tall_ref[rows_t, cut]) for cut in cuts]


def mixed_own_body(arr_ref, done_ref, tall_ref, out_ref):
    fs = 2 * done_ref.shape[2]
    parts = mixed_half(done_ref[0], is_speech(arr_ref), parity(), tall_ref, fs)
    for i, value in enumerate(parts):
        out_ref[:, i * BLOCK : (i + 1) * BLOCK] = value


def back_body(
    turned, arr_ref, done_ref, other_ref, own_ref, wide_ref, tall_ref,
    keep_ref, send_ref, hs_ref, ht_ref, dgs, dgt, dus, dut, out,
):
    speech = is_speech(arr_ref)
    fs, ft = hs_ref.shape[1], ht_ref.shape[1]
    ns, nt = fs // BLOCK, ft // BLOCK
    odd = parity() == 1
    for k, (s, t) in enumerate(((hs_ref, ht_ref), (dgs, dgt), (dus, dut))):
        done, other = done_ref[k], other_ref[k]
        value = jnp.concatenate([jnp.where(odd, other, done), jnp.where(odd, done, other)], axis=1)
        zero = jnp.zeros_like(value)
        s[...] = jnp.where(speech, value, zero)
        value = jnp.where(speech, zero, value)
        for i in range(nt):
            start = beside(i, fs, ft)
            t[:, i * BLOCK : (i + 1) * BLOCK] = value[:, start : start + BLOCK]
    width = tall_ref.shape[1]
    for i, value in enumerate(mixed_half(other_ref[0], speech, 1 - parity(), tall_ref, fs)):
        cut = slice(i * BLOCK, (i + 1) * BLOCK)
        out[:, cut] = own_ref[:, cut] + value
    blocks = [(dgt, nt), (dut, nt), (dgs, ns), (dus, ns)]
    blocks = [(ref, i) for ref, n in blocks for i in range(n)]
    for r in range(width // BLOCK):
        total = jnp.zeros((out.shape[0], BLOCK), F32)
        for b, (ref, j) in enumerate(blocks):
            product = times if b in turned else contract_last
            total += product(ref[:, j * BLOCK : (j + 1) * BLOCK], square_at(wide_ref, b, r)[...])
        start = width + r * BLOCK
        out[:, start : start + BLOCK] = total
    half = keep_ref.shape[0]
    keep_ref[...] = out[:half]
    send_ref[...] = out[half:].astype(BF16)


def back(arr, done, other, own, wide, tall, turned, fs, ft):
    rows, width = arr.shape[0], tall.shape[1]
    hidden = [((rows, fs), BF16), ((rows, ft), BF16)]
    return call(
        functools.partial(back_body, turned),
        "token_partials",
        [((rows // 2, 2 * width), F32), ((rows // 2, 2 * width), BF16)] + hidden,
        (arr, done, other, own, wide, tall),
        "vvvvvv",
        [pltpu.VMEM(*s) for s in hidden + hidden] + [pltpu.VMEM((rows, 2 * width), F32)],
        2 * rows * (wide.size + tall.size),
    )


def token_sum_body(keep_ref, got_ref, after_ref, next_ref, send_ref):
    total = keep_ref[...] + got_ref[...].astype(F32)
    half = next_ref.shape[0]
    next_ref[...] = total[:half]
    send_ref[...] = total[half:].astype(send_ref.dtype)


def token_sum(keep, got, after, dtype, name):
    rows, width = keep.shape
    outs = [((rows // 2, width), F32), ((rows // 2, width), dtype)]
    return call(token_sum_body, name, outs, (keep, got, after), "vvh")


def last_sum_body(keep_ref, got_ref, mixed_hbm, grad_hbm, mixed_ref, grad_ref, sems):
    total = (keep_ref[...] + got_ref[...].astype(F32)).astype(BF16)
    width = mixed_ref.shape[1]
    mixed_ref[...] = total[:, :width]
    grad_ref[...] = total[:, width:]
    copies = [
        pltpu.make_async_copy(mixed_ref, mixed_hbm, sems.at[0]),
        pltpu.make_async_copy(grad_ref, grad_hbm, sems.at[1]),
    ]
    for copy in copies:
        copy.start()
    for copy in copies:
        copy.wait()


def outer_steps(c, steps, slots, sems):
    copies = []
    for i, (h, place) in enumerate(steps):
        slots[i] = contract_first(h, c).astype(BF16)
        copies.append(pltpu.make_async_copy(slots.at[i], place, sems.at[i]))
        copies[-1].start()
    for copy in copies:
        copy.wait()


def outer_body(speech, text, after_ref, arr_ref, hs_ref, ht_ref, *refs):
    slots, sems = refs[-2:]
    outs = list(refs[-2 - bool(speech) - bool(text) : -2])
    width = outs[0].shape[1]
    steps = []
    for h_ref, blocks in ((hs_ref, speech), (ht_ref, text)):
        out = outs.pop(0) if blocks else None
        cuts = [slice(i * ROWS, (i + 1) * ROWS) for i in blocks]
        steps += [(h_ref[:, cut], out.at[cut]) for cut in cuts]
    outer_steps(arr_ref[:, width : 2 * width], steps, slots, sems)


def flip(value, axes, bit, n):
    return lax.ppermute(value, axes, [(i, i ^ bit) for i in range(n)])


def by_kernels(n_seq, n_tok, tokens, modality, cotangent, gate_s, up_s, down_s, gate_t, up_t, down_t):
    rows, width = tokens.shape
    fs, ft = gate_s.shape[1], gate_t.shape[1]
    wide = ((2 * (fs + ft) // WIDE, width, WIDE), BF16)
    tall = ((fs + ft, width), BF16)
    pair = [pltpu.VMEM((rows, width), BF16)] * 2

    packed = ((rows, 2 * width + 128), BF16)
    scratch = pair + [pltpu.SMEM((rows,), jnp.int32), pltpu.SemaphoreType.DMA((3,))]
    wide, tall, arr = call(pack_body, "pack", [wide, tall, packed], (modality, tokens, cotangent), "hhh", scratch)
    got = flip(arr, TOK, HOPS[0], n_tok)
    wide = load(arr, gate_t, wide, (tall,), 0, "load_gate_text")
    arr = join(arr, got, "join_4", (wide, tall))
    got = flip(arr, TOK, HOPS[1], n_tok)
    wide = load(arr, up_t, wide, (tall,), ft // WIDE, "load_up_text")
    arr = join(arr, got, "join_8", (wide, tall))
    got = flip(arr, TOK, HOPS[2], n_tok)
    tall = load(arr, down_t, tall, (wide,), fs, "load_down_text")
    arr = join(arr, got, "join_16", (wide, tall))

    mine, theirs, wide, tall = partials(arr, gate_s, up_s, down_s, wide, tall)
    blocks = 2 * (fs + ft) // BLOCK
    got = flip(theirs, "seq", 1, n_seq)
    wide = turn(wide, tall, 0, TURN_FIRST, "turn_1")
    total, send = call(
        core_sum_body, "core_sum", [like(mine), (mine.shape, BF16)], (mine, got), "vv", also=(wide, tall)
    )
    got = flip(send, "seq", 2, n_seq)
    wide = turn(wide, tall, TURN_FIRST, blocks - TURN_FIRST, "turn_2")
    done = call(hidden_body, "hidden", [(mine.shape, BF16)], (total, got), "vv", also=(wide, tall))[0]
    other = flip(done, "seq", 1, n_seq)
    own = call(
        mixed_own_body, "mixed_own", [((arr.shape[0], width), F32)], (arr, done, tall), "vvv",
        flops=arr.shape[0] * tall.size, also=(wide,),
    )[0]
    keep, send, hs, ht = back(arr, done, other, own, wide, tall, range(blocks), fs, ft)

    def outer(after, speech, text, old, name):
        count = len(speech) + len(text)
        outs = [like(w) for w, blocks in ((down_s, speech), (down_t, text)) if blocks]
        return call(
            functools.partial(outer_body, speech, text), name, outs, (after, arr, hs, ht, *old),
            "vvvv" + "h" * len(old), [pltpu.VMEM((count, ROWS, width), BF16), pltpu.SemaphoreType.DMA((count,))],
            2 * arr.shape[0] * count * ROWS * width, 2 * count * ROWS * width, limit=8,
            out_places="h" * len(outs), aliases={4: 0} if old else None,
        )

    ns, nt = fs // ROWS, ft // ROWS
    got = flip(send, TOK, HOPS[2], n_tok)
    down_s_grad = outer(keep, range(ns - 5), (), (), "down_grad_1")[0]
    keep, send = token_sum(keep, got, down_s_grad, BF16, "token_sum_4")

    got = flip(send, TOK, HOPS[1], n_tok)
    down_s_grad, down_t_grad = outer(keep, range(ns - 5, ns), range(2), (down_s_grad,), "down_grad_2")
    keep, send = token_sum(keep, got, down_t_grad, BF16, "token_sum_2")

    got = flip(send, TOK, HOPS[0], n_tok)
    down_t_grad = outer(keep, (), range(2, nt), (down_t_grad,), "down_grad_3")[0]
    outs = [((rows, width), BF16)] * 2
    mixed, token_grad = call(last_sum_body, "token_sum_1", outs, (keep, got), "vv", pair + [pltpu.SemaphoreType.DMA((2,))], out_places="hh")
    return mixed, token_grad, down_s_grad, down_t_grad


def by_arrays(n_seq, n_tok, tokens, modality, cotangent, gate_s, up_s, down_s, gate_t, up_t, down_t):
    width = tokens.shape[1]
    ft = gate_t.shape[1]
    kind = jnp.broadcast_to(modality.astype(BF16)[:, None], (modality.shape[0], 128))
    packed = jnp.concatenate([tokens, cotangent, kind], axis=1)
    arrived = lax.all_gather(packed, TOK, axis=0, tiled=True)
    rows, grads = arrived[:, :width], arrived[:, width : 2 * width]
    speech = arrived[:, 2 * width : 2 * width + 1] == 0

    def pick(s, t):
        return jnp.concatenate([jnp.where(speech, s[:, :ft], t), s[:, ft:]], axis=1)

    def halves(v):
        zero = jnp.zeros((), v.dtype)
        return jnp.where(speech, v, zero), jnp.where(speech, zero, v[:, :ft])

    g = pick(times(rows, gate_s), times(rows, gate_t))
    u = pick(times(rows, up_s), times(rows, up_t))
    dh = pick(contract_last(grads, down_s), contract_last(grads, down_t))
    sums = jnp.stack([g, u, dh])
    sums = sums + flip(sums, "seq", 1, n_seq)
    g, u, dh = sums + flip(sums.astype(BF16), "seq", 2, n_seq).astype(F32)
    sig = jax.nn.sigmoid(g)
    h = (g * sig * u).astype(BF16)
    dg = (dh * u * sig * (1.0 + g * (1.0 - sig))).astype(BF16)
    du = (dh * (g * sig)).astype(BF16)
    (hs, ht), (dgs, dgt), (dus, dut) = halves(h), halves(dg), halves(du)
    mixed = times(hs, down_s) + times(ht, down_t)
    grad = contract_last(dgs, gate_s) + contract_last(dus, up_s)
    grad = grad + contract_last(dgt, gate_t) + contract_last(dut, up_t)
    out = jnp.concatenate([mixed, grad], axis=1).astype(BF16)
    out = out.reshape(n_tok, out.shape[0] // n_tok, out.shape[1])
    out = lax.all_to_all(out, TOK, split_axis=0, concat_axis=0, tiled=True)
    total = jnp.sum(out.astype(F32), axis=0).astype(BF16)
    down_s_grad = contract_first(hs, grads).astype(BF16)
    down_t_grad = contract_first(ht, grads).astype(BF16)
    return total[:, :width], total[:, width:], down_s_grad, down_t_grad


def solution(mesh):
    n_seq, n_tok = mesh.shape["seq"], mesh.shape["attn"] * mesh.shape["exp"]

    def run(*args):
        fs, ft, width = args[3].shape[1], args[6].shape[1], args[0].shape[1]
        fits = n_tok == 8 and args[0].shape[0] == 2 and fs >= ft and ft % (2 * WIDE) == 0
        fits = fits and fs % WIDE == 0 and width % BLOCK == 0
        return (by_kernels if fits else by_arrays)(n_seq, n_tok, *args)

    return jax.shard_map(
        run,
        mesh=mesh,
        in_specs=(
            P(TOK, "seq"),
            P(TOK),
            P(TOK, "seq"),
            P("seq", TOK),
            P("seq", TOK),
            P(TOK, "seq"),
            P("seq", TOK),
            P("seq", TOK),
            P(TOK, "seq"),
        ),
        out_specs=(P(TOK, "seq"),) * 4,
        check_vma=False,
    )
```

```python
import functools

import jax
import jax.numpy as jnp
from jax import lax
from jax.experimental import pallas as pl
from jax.experimental.pallas import tpu as pltpu
from jax.sharding import PartitionSpec as P

TOK = ("attn", "exp")
HOPS = (2, 1, 4)
F32 = jnp.float32
BF16 = jnp.bfloat16
MIB = 1 << 20
BLOCK = 512
WIDE = 1024
ROWS = 256
TURN_FIRST = 5
PLACES = {"h": pl.ANY, "v": pltpu.VMEM, "s": pltpu.SMEM}


def contract_first(left, right):
    return lax.dot_general(left, right, (((0,), (0,)), ((), ())), preferred_element_type=F32)


def contract_last(left, right):
    return lax.dot_general(left, right, (((1,), (1,)), ((), ())), preferred_element_type=F32)


def times(left, right):
    return jnp.dot(left, right, preferred_element_type=F32)


def size_of(*arrays):
    return sum(a.size * jnp.dtype(a.dtype).itemsize for a in arrays)


def constrain(x, place):
    if place == "s":
        return x
    return pltpu.with_memory_space_constraint(x, pltpu.VMEM if place == "v" else pltpu.HBM)


def call(
    body, name, outs, ins, places, scratch=(), flops=0, traffic=0, limit=4, out_places=None, aliases=None, also=()
):
    out_places = out_places or "v" * len(outs)
    shapes = [pltpu.VMEM(*o) if p == "v" else jax.ShapeDtypeStruct(*o) for o, p in zip(outs, out_places)]
    count = len(ins)

    def seen(*refs):
        body(*refs[:count], *refs[count + len(also) :])

    ins, places = (*ins, *also), places + "v" * len(also)
    return pl.pallas_call(
        seen,
        out_shape=shapes,
        in_specs=[pl.BlockSpec(memory_space=PLACES[p]) for p in places],
        out_specs=[pl.BlockSpec(memory_space=PLACES[p]) for p in out_places],
        scratch_shapes=list(scratch),
        input_output_aliases=aliases or {},
        compiler_params=pltpu.CompilerParams(vmem_limit_bytes=limit * MIB),
        cost_estimate=pl.CostEstimate(flops=flops, bytes_accessed=traffic, transcendentals=0),
        name=name,
    )(*[constrain(x, p) for x, p in zip(ins, places)])


def like(x):
    return x.shape, x.dtype


def parity():
    return lax.rem(lax.axis_index("seq"), 2)


def is_speech(arr_ref):
    return arr_ref[:, arr_ref.shape[1] - 1 :] == 0


def pack_body(kind_hbm, tok_hbm, cot_hbm, wide_ref, out_ref, tok_ref, cot_ref, kind_ref, sems):
    copies = [
        pltpu.make_async_copy(kind_hbm, kind_ref, sems.at[2]),
        pltpu.make_async_copy(tok_hbm, tok_ref, sems.at[0]),
        pltpu.make_async_copy(cot_hbm, cot_ref, sems.at[1]),
    ]
    for copy in copies:
        copy.start()
    width = tok_ref.shape[1]
    row = lax.broadcasted_iota(jnp.int32, (tok_ref.shape[0], 128), 0)
    kind = jnp.zeros(row.shape, F32)
    for copy in copies:
        copy.wait()
    for i in range(tok_ref.shape[0]):
        kind = jnp.where(row == i, kind_ref[i].astype(F32), kind)
    out_ref[:, 2 * width :] = kind.astype(BF16)
    out_ref[:, :width] = tok_ref[...]
    out_ref[:, width : 2 * width] = cot_ref[...]


def join_body(a_ref, b_ref, out_ref):
    both = jnp.concatenate([a_ref[...].astype(F32), b_ref[...].astype(F32)], axis=0)
    out_ref[...] = both.astype(BF16)


def join(a, b, name, also):
    return call(join_body, name, [((2 * a.shape[0], a.shape[1]), BF16)], (a, b), "vv", also=also)[0]


def column_blocks(src, wide, first, cuts):
    rows = src.shape[0] // cuts
    parts = [pl.ds(j * rows, rows) for j in range(cuts)]
    return [
        [(src.at[part, pl.ds(i * WIDE, WIDE)], wide.at[first + i, part]) for part in parts]
        for i in range(src.shape[1] // WIDE)
    ]


def square_at(wide_ref, i, r):
    per = WIDE // BLOCK
    return wide_ref.at[i // per, pl.ds(r * BLOCK, BLOCK), pl.ds(i % per * BLOCK, BLOCK)]


def started(groups, sems):
    copies, count = [], 0
    for group in groups:
        copies.append([pltpu.make_async_copy(s, d, sems.at[count + i]) for i, (s, d) in enumerate(group)])
        count += len(group)
    for group in copies:
        for copy in group:
            copy.start()
    return copies


def wait(group):
    for copy in group:
        copy.wait()


def load_body(first, after_ref, src_hbm, old_ref, place_ref, sems):
    for group in started(column_blocks(src_hbm, place_ref, first, 4), sems):
        wait(group)


def load(after, src, place, also, first, name):
    return call(
        functools.partial(load_body, first),
        name,
        [like(place)],
        (after, src, place),
        "vhv",
        [pltpu.SemaphoreType.DMA((8,))],
        traffic=size_of(src),
        aliases={2: 0},
        also=also,
    )[0]


def beside(i, fs, ft):
    side, rest = divmod(i * BLOCK, ft // 2)
    return side * (fs // 2) + rest


def partials_body(
    arr_ref, dt_ref, ds_ref, ut_hbm, gs_hbm, us_hbm, old_wide, mine_ref, theirs_ref, wide_ref, part, sems
):
    fs, width = ds_ref.shape
    ft = dt_ref.shape[0]
    ns, nt = fs // WIDE, ft // WIDE
    groups = column_blocks(ut_hbm, wide_ref, nt, 2) + column_blocks(gs_hbm, wide_ref, 2 * nt, 2)
    groups += column_blocks(us_hbm, wide_ref, 2 * nt + ns, 2)
    copies = started(groups, sems)
    x = arr_ref[:, :width]
    c = arr_ref[:, width : 2 * width]
    speech = is_speech(arr_ref)

    def put(k, start, value, pick):
        cut = slice(start, start + BLOCK)
        if pick and start % (fs // 2) < ft // 2:
            value = jnp.where(speech, value, part[k, :, cut])
        part[k, :, cut] = value

    def put_wide(k, start, value, pick):
        for i in range(start, start + WIDE, BLOCK):
            place = i if pick else beside(i // BLOCK, fs, ft)
            put(k, place, value[:, i - start : i - start + BLOCK], pick)

    for k, ref in enumerate((dt_ref, ds_ref)):
        for i in range(0, ref.shape[0], BLOCK):
            place = i if k else beside(i // BLOCK, fs, ft)
            put(2, place, contract_last(c, ref[i : i + BLOCK, :]), k == 1)
    for k in range(2):
        for i in range(nt):
            if k == 1:
                wait(copies[i])
            put_wide(k, i * WIDE, times(x, wide_ref[k * nt + i]), False)
    for k in range(2):
        for i in range(ns):
            wait(copies[nt + k * ns + i])
            put_wide(k, i * WIDE, times(x, wide_ref[2 * nt + k * ns + i]), True)
    half = fs // 2
    odd = parity()
    for k in range(3):
        mine_ref[k] = part[k, :, pl.ds(pl.multiple_of(odd * half, half), half)]
        theirs_ref[k] = part[k, :, pl.ds(pl.multiple_of((1 - odd) * half, half), half)]


def partials(arr, up_t, gate_s, up_s, down_t, down_s, wide):
    rows, fs = arr.shape[0], gate_s.shape[1]
    half = ((3, rows, fs // 2), F32)
    return call(
        partials_body,
        "hidden_partials",
        [half, half, like(wide)],
        (arr, down_t, down_s, up_t, gate_s, up_s, wide),
        "vvvhhhv",
        [pltpu.VMEM((3, rows, fs), F32), pltpu.SemaphoreType.DMA(((4 * fs + 2 * up_t.shape[1]) // WIDE,))],
        2 * rows * (wide.size + down_s.size + down_t.size),
        size_of(up_t, gate_s, up_s),
        aliases={6: 2},
    )


def core_sum_body(mine_ref, got_ref, sum_ref, send_ref):
    total = mine_ref[...] + got_ref[...]
    sum_ref[...] = total
    send_ref[...] = total.astype(BF16)


def hidden_body(sum_ref, got_ref, out_ref):
    total = [sum_ref[k] + got_ref[k].astype(F32) for k in range(3)]
    g, u, dh = total
    sig = jax.nn.sigmoid(g)
    silu = g * sig
    out_ref[0] = (silu * u).astype(BF16)
    out_ref[1] = (dh * u * sig * (1.0 + g * (1.0 - sig))).astype(BF16)
    out_ref[2] = (dh * silu).astype(BF16)


def turn_body(first, count, old_ref, wide_ref):
    row, col = (lax.broadcasted_iota(jnp.int32, (ROWS, ROWS), i) for i in range(2))
    one = (row == col).astype(BF16)
    squares = wide_ref.shape[1] // BLOCK
    for n in range(count * squares):
        i, r = first + n // squares, n % squares
        place = square_at(wide_ref, i, r)
        square = place[...]
        if n % 2:
            turned = square.T
        else:
            parts = [contract_last(one, square[:, j : j + ROWS]) for j in range(0, BLOCK, ROWS)]
            turned = jnp.concatenate([p.astype(BF16) for p in parts], axis=0)
        place[...] = turned


def turn(wide, also, first, count, name):
    return call(
        functools.partial(turn_body, first, count),
        name,
        [like(wide)],
        (wide,),
        "v",
        traffic=4 * count * wide.shape[1] * BLOCK,
        aliases={0: 0},
        also=also,
    )[0]


def mixed_half(h, speech, side, dt_ref, ds_ref):
    half_s, half_t, width = ds_ref.shape[0] // 2, dt_ref.shape[0] // 2, ds_ref.shape[1]
    zero = jnp.zeros_like(h)
    hs, ht = jnp.where(speech, h, zero), jnp.where(speech, zero, h)[:, :half_t]
    rows_s = pl.ds(pl.multiple_of(side * half_s, BLOCK), half_s)
    rows_t = pl.ds(pl.multiple_of(side * half_t, BLOCK), half_t)
    cuts = [slice(i, i + BLOCK) for i in range(0, width, BLOCK)]
    return [times(hs, ds_ref[rows_s, cut]) + times(ht, dt_ref[rows_t, cut]) for cut in cuts]


def mixed_own_body(arr_ref, done_ref, dt_ref, ds_ref, out_ref):
    parts = mixed_half(done_ref[0], is_speech(arr_ref), parity(), dt_ref, ds_ref)
    for i, value in enumerate(parts):
        out_ref[:, i * BLOCK : (i + 1) * BLOCK] = value


def back_body(
    turned, arr_ref, done_ref, other_ref, own_ref, wide_ref, dt_ref, ds_ref,
    keep_ref, send_ref, hs_ref, ht_ref, dgs, dgt, dus, dut, out,
):
    speech = is_speech(arr_ref)
    fs, ft = hs_ref.shape[1], ht_ref.shape[1]
    ns, nt = fs // BLOCK, ft // BLOCK
    odd = parity() == 1
    for k, (s, t) in enumerate(((hs_ref, ht_ref), (dgs, dgt), (dus, dut))):
        done, other = done_ref[k], other_ref[k]
        value = jnp.concatenate([jnp.where(odd, other, done), jnp.where(odd, done, other)], axis=1)
        zero = jnp.zeros_like(value)
        s[...] = jnp.where(speech, value, zero)
        value = jnp.where(speech, zero, value)
        for i in range(nt):
            start = beside(i, fs, ft)
            t[:, i * BLOCK : (i + 1) * BLOCK] = value[:, start : start + BLOCK]
    width = ds_ref.shape[1]
    for i, value in enumerate(mixed_half(other_ref[0], speech, 1 - parity(), dt_ref, ds_ref)):
        cut = slice(i * BLOCK, (i + 1) * BLOCK)
        out[:, cut] = own_ref[:, cut] + value
    blocks = [(dgt, nt), (dut, nt), (dgs, ns), (dus, ns)]
    blocks = [(ref, i) for ref, n in blocks for i in range(n)]
    for r in range(width // BLOCK):
        total = jnp.zeros((out.shape[0], BLOCK), F32)
        for b, (ref, j) in enumerate(blocks):
            product = times if b in turned else contract_last
            total += product(ref[:, j * BLOCK : (j + 1) * BLOCK], square_at(wide_ref, b, r)[...])
        start = width + r * BLOCK
        out[:, start : start + BLOCK] = total
    half = keep_ref.shape[0]
    keep_ref[...] = out[:half]
    send_ref[...] = out[half:].astype(BF16)


def back(arr, done, other, own, wide, down_t, down_s, turned):
    rows, width = arr.shape[0], down_s.shape[1]
    fs, ft = down_s.shape[0], down_t.shape[0]
    hidden = [((rows, fs), BF16), ((rows, ft), BF16)]
    return call(
        functools.partial(back_body, turned),
        "token_partials",
        [((rows // 2, 2 * width), F32), ((rows // 2, 2 * width), BF16)] + hidden,
        (arr, done, other, own, wide, down_t, down_s),
        "vvvvvvv",
        [pltpu.VMEM(*s) for s in hidden + hidden] + [pltpu.VMEM((rows, 2 * width), F32)],
        2 * rows * (wide.size + down_t.size + down_s.size),
    )


def token_sum_body(keep_ref, got_ref, after_ref, next_ref, send_ref):
    total = keep_ref[...] + got_ref[...].astype(F32)
    half = next_ref.shape[0]
    next_ref[...] = total[:half]
    send_ref[...] = total[half:].astype(send_ref.dtype)


def token_sum(keep, got, after, dtype, name):
    rows, width = keep.shape
    outs = [((rows // 2, width), F32), ((rows // 2, width), dtype)]
    return call(token_sum_body, name, outs, (keep, got, after), "vvh")


def last_sum_body(keep_ref, got_ref, mixed_hbm, grad_hbm, mixed_ref, grad_ref, sems):
    total = (keep_ref[...] + got_ref[...].astype(F32)).astype(BF16)
    width = mixed_ref.shape[1]
    mixed_ref[...] = total[:, :width]
    grad_ref[...] = total[:, width:]
    copies = [
        pltpu.make_async_copy(mixed_ref, mixed_hbm, sems.at[0]),
        pltpu.make_async_copy(grad_ref, grad_hbm, sems.at[1]),
    ]
    for copy in copies:
        copy.start()
    for copy in copies:
        copy.wait()


def outer_steps(c, steps, slots, sems):
    copies = []
    for i, (h, place) in enumerate(steps):
        slots[i] = contract_first(h, c).astype(BF16)
        copies.append(pltpu.make_async_copy(slots.at[i], place, sems.at[i]))
        copies[-1].start()
    for copy in copies:
        copy.wait()


def outer_body(speech, text, after_ref, arr_ref, hs_ref, ht_ref, *refs):
    slots, sems = refs[-2:]
    outs = list(refs[-2 - bool(speech) - bool(text) : -2])
    width = outs[0].shape[1]
    steps = []
    for h_ref, blocks in ((hs_ref, speech), (ht_ref, text)):
        out = outs.pop(0) if blocks else None
        cuts = [slice(i * ROWS, (i + 1) * ROWS) for i in blocks]
        steps += [(h_ref[:, cut], out.at[cut]) for cut in cuts]
    outer_steps(arr_ref[:, width : 2 * width], steps, slots, sems)


def flip(value, axes, bit, n):
    return lax.ppermute(value, axes, [(i, i ^ bit) for i in range(n)])


def by_kernels(n_seq, n_tok, tokens, modality, cotangent, gate_s, up_s, down_s, gate_t, up_t, down_t):
    rows, width = tokens.shape
    fs, ft = gate_s.shape[1], gate_t.shape[1]
    wide = ((2 * (fs + ft) // WIDE, width, WIDE), BF16)
    pair = [pltpu.VMEM((rows, width), BF16)] * 2

    packed = ((rows, 2 * width + 128), BF16)
    scratch = pair + [pltpu.SMEM((rows,), jnp.int32), pltpu.SemaphoreType.DMA((3,))]
    wide, arr = call(pack_body, "pack", [wide, packed], (modality, tokens, cotangent), "hhh", scratch)
    got = flip(arr, TOK, HOPS[0], n_tok)
    wide = load(arr, gate_t, wide, (), 0, "load_gate_text")
    arr = join(arr, got, "join_4", (wide,))
    got = flip(arr, TOK, HOPS[1], n_tok)
    arr = join(arr, got, "join_8", (wide,))
    arr = join(arr, flip(arr, TOK, HOPS[2], n_tok), "join_16", (wide, down_t, down_s))

    mine, theirs, wide = partials(arr, up_t, gate_s, up_s, down_t, down_s, wide)
    blocks = 2 * (fs + ft) // BLOCK
    got = flip(theirs, "seq", 1, n_seq)
    wide = turn(wide, (down_t, down_s), 0, TURN_FIRST, "turn_1")
    total, send = call(
        core_sum_body, "core_sum", [like(mine), (mine.shape, BF16)], (mine, got), "vv", also=(wide, down_t, down_s)
    )
    got = flip(send, "seq", 2, n_seq)
    wide = turn(wide, (down_t, down_s), TURN_FIRST, blocks - TURN_FIRST, "turn_2")
    done = call(hidden_body, "hidden", [(mine.shape, BF16)], (total, got), "vv", also=(wide, down_t, down_s))[0]
    other = flip(done, "seq", 1, n_seq)
    own = call(
        mixed_own_body, "mixed_own", [((arr.shape[0], width), F32)], (arr, done, down_t, down_s), "vvvv",
        flops=arr.shape[0] * (down_s.size + down_t.size), also=(wide,),
    )[0]
    keep, send, hs, ht = back(arr, done, other, own, wide, down_t, down_s, range(blocks))

    def outer(after, speech, text, old, name):
        count = len(speech) + len(text)
        outs = [like(w) for w, blocks in ((down_s, speech), (down_t, text)) if blocks]
        return call(
            functools.partial(outer_body, speech, text), name, outs, (after, arr, hs, ht, *old),
            "vvvv" + "h" * len(old), [pltpu.VMEM((count, ROWS, width), BF16), pltpu.SemaphoreType.DMA((count,))],
            2 * arr.shape[0] * count * ROWS * width, 2 * count * ROWS * width, limit=8,
            out_places="h" * len(outs), aliases={4: 0} if old else None,
        )

    ns, nt = fs // ROWS, ft // ROWS
    got = flip(send, TOK, HOPS[2], n_tok)
    down_s_grad = outer(keep, range(ns - 5), (), (), "down_grad_1")[0]
    keep, send = token_sum(keep, got, down_s_grad, BF16, "token_sum_4")

    got = flip(send, TOK, HOPS[1], n_tok)
    down_s_grad, down_t_grad = outer(keep, range(ns - 5, ns), range(2), (down_s_grad,), "down_grad_2")
    keep, send = token_sum(keep, got, down_t_grad, BF16, "token_sum_2")

    got = flip(send, TOK, HOPS[0], n_tok)
    down_t_grad = outer(keep, (), range(2, nt), (down_t_grad,), "down_grad_3")[0]
    outs = [((rows, width), BF16)] * 2
    mixed, token_grad = call(last_sum_body, "token_sum_1", outs, (keep, got), "vv", pair + [pltpu.SemaphoreType.DMA((2,))], out_places="hh")
    return mixed, token_grad, down_s_grad, down_t_grad


def by_arrays(n_seq, n_tok, tokens, modality, cotangent, gate_s, up_s, down_s, gate_t, up_t, down_t):
    width = tokens.shape[1]
    ft = gate_t.shape[1]
    kind = jnp.broadcast_to(modality.astype(BF16)[:, None], (modality.shape[0], 128))
    packed = jnp.concatenate([tokens, cotangent, kind], axis=1)
    arrived = lax.all_gather(packed, TOK, axis=0, tiled=True)
    rows, grads = arrived[:, :width], arrived[:, width : 2 * width]
    speech = arrived[:, 2 * width : 2 * width + 1] == 0

    def pick(s, t):
        return jnp.concatenate([jnp.where(speech, s[:, :ft], t), s[:, ft:]], axis=1)

    def halves(v):
        zero = jnp.zeros((), v.dtype)
        return jnp.where(speech, v, zero), jnp.where(speech, zero, v[:, :ft])

    g = pick(times(rows, gate_s), times(rows, gate_t))
    u = pick(times(rows, up_s), times(rows, up_t))
    dh = pick(contract_last(grads, down_s), contract_last(grads, down_t))
    sums = jnp.stack([g, u, dh])
    sums = sums + flip(sums, "seq", 1, n_seq)
    g, u, dh = sums + flip(sums.astype(BF16), "seq", 2, n_seq).astype(F32)
    sig = jax.nn.sigmoid(g)
    h = (g * sig * u).astype(BF16)
    dg = (dh * u * sig * (1.0 + g * (1.0 - sig))).astype(BF16)
    du = (dh * (g * sig)).astype(BF16)
    (hs, ht), (dgs, dgt), (dus, dut) = halves(h), halves(dg), halves(du)
    mixed = times(hs, down_s) + times(ht, down_t)
    grad = contract_last(dgs, gate_s) + contract_last(dus, up_s)
    grad = grad + contract_last(dgt, gate_t) + contract_last(dut, up_t)
    out = jnp.concatenate([mixed, grad], axis=1).astype(BF16)
    out = out.reshape(n_tok, out.shape[0] // n_tok, out.shape[1])
    out = lax.all_to_all(out, TOK, split_axis=0, concat_axis=0, tiled=True)
    total = jnp.sum(out.astype(F32), axis=0).astype(BF16)
    down_s_grad = contract_first(hs, grads).astype(BF16)
    down_t_grad = contract_first(ht, grads).astype(BF16)
    return total[:, :width], total[:, width:], down_s_grad, down_t_grad


def solution(mesh):
    n_seq, n_tok = mesh.shape["seq"], mesh.shape["attn"] * mesh.shape["exp"]

    def run(*args):
        fs, ft, width = args[3].shape[1], args[6].shape[1], args[0].shape[1]
        fits = n_tok == 8 and args[0].shape[0] == 2 and fs >= ft and ft % (2 * WIDE) == 0
        fits = fits and fs % WIDE == 0 and width % BLOCK == 0
        return (by_kernels if fits else by_arrays)(n_seq, n_tok, *args)

    return jax.shard_map(
        run,
        mesh=mesh,
        in_specs=(
            P(TOK, "seq"),
            P(TOK),
            P(TOK, "seq"),
            P("seq", TOK),
            P("seq", TOK),
            P(TOK, "seq"),
            P("seq", TOK),
            P("seq", TOK),
            P(TOK, "seq"),
        ),
        out_specs=(P(TOK, "seq"),) * 4,
        check_vma=False,
    )
```

```python
import functools

import jax
import jax.numpy as jnp
from jax import lax
from jax.experimental import pallas as pl
from jax.experimental.pallas import tpu as pltpu
from jax.sharding import PartitionSpec as P

TOK = ("attn", "exp")
HOPS = (2, 1, 4)
F32 = jnp.float32
BF16 = jnp.bfloat16
MIB = 1 << 20
LIMIT = 6
BLOCK = 512
WIDE = 1024
ROWS = 256
TURN_FIRST = 5
SLOTS = 4
EARLY_ROWS = 2560
TEXT_FIRST = 3
PLACES = {"h": pl.ANY, "v": pltpu.VMEM, "s": pltpu.SMEM}


def contract_first(left, right):
    return lax.dot_general(left, right, (((0,), (0,)), ((), ())), preferred_element_type=F32)


def contract_last(left, right):
    return lax.dot_general(left, right, (((1,), (1,)), ((), ())), preferred_element_type=F32)


def times(left, right):
    return jnp.dot(left, right, preferred_element_type=F32)


def size_of(*arrays):
    return sum(a.size * jnp.dtype(a.dtype).itemsize for a in arrays)


def constrain(x, place):
    if place == "s":
        return x
    return pltpu.with_memory_space_constraint(x, pltpu.VMEM if place == "v" else pltpu.HBM)


def call(
    body, name, outs, ins, places, scratch=(), flops=0, traffic=0, limit=LIMIT, out_places=None, aliases=None, also=()
):
    out_places = out_places or "v" * len(outs)
    shapes = [pltpu.VMEM(*o) if p == "v" else jax.ShapeDtypeStruct(*o) for o, p in zip(outs, out_places)]
    count = len(ins)

    def seen(*refs):
        body(*refs[:count], *refs[count + len(also) :])

    ins, places = (*ins, *also), places + "v" * len(also)
    return pl.pallas_call(
        seen,
        out_shape=shapes,
        in_specs=[pl.BlockSpec(memory_space=PLACES[p]) for p in places],
        out_specs=[pl.BlockSpec(memory_space=PLACES[p]) for p in out_places],
        scratch_shapes=list(scratch),
        input_output_aliases=aliases or {},
        compiler_params=pltpu.CompilerParams(vmem_limit_bytes=limit * MIB),
        cost_estimate=pl.CostEstimate(flops=flops, bytes_accessed=traffic, transcendentals=0),
        name=name,
    )(*[constrain(x, p) for x, p in zip(ins, places)])


def like(x):
    return x.shape, x.dtype


def parity():
    return lax.rem(lax.axis_index("seq"), 2)


def is_speech(arr_ref):
    return arr_ref[:, arr_ref.shape[1] - 1 :] == 0


def pack_body(kind_hbm, tok_hbm, cot_hbm, wide_ref, out_ref, tok_ref, cot_ref, kind_ref, sems):
    copies = [
        pltpu.make_async_copy(kind_hbm, kind_ref, sems.at[2]),
        pltpu.make_async_copy(tok_hbm, tok_ref, sems.at[0]),
        pltpu.make_async_copy(cot_hbm, cot_ref, sems.at[1]),
    ]
    for copy in copies:
        copy.start()
    width = tok_ref.shape[1]
    row = lax.broadcasted_iota(jnp.int32, (tok_ref.shape[0], 128), 0)
    kind = jnp.zeros(row.shape, F32)
    for copy in copies:
        copy.wait()
    for i in range(tok_ref.shape[0]):
        kind = jnp.where(row == i, kind_ref[i].astype(F32), kind)
    out_ref[:, 2 * width :] = kind.astype(BF16)
    out_ref[:, :width] = tok_ref[...]
    out_ref[:, width : 2 * width] = cot_ref[...]


def join_body(a_ref, b_ref, out_ref):
    both = jnp.concatenate([a_ref[...].astype(F32), b_ref[...].astype(F32)], axis=0)
    out_ref[...] = both.astype(BF16)


def join(a, b, name, also):
    return call(join_body, name, [((2 * a.shape[0], a.shape[1]), BF16)], (a, b), "vv", also=also)[0]


def column_blocks(src, wide, first, cuts):
    rows = src.shape[0] // cuts
    parts = [pl.ds(j * rows, rows) for j in range(cuts)]
    return [
        [(src.at[part, pl.ds(i * WIDE, WIDE)], wide.at[first + i, part]) for part in parts]
        for i in range(src.shape[1] // WIDE)
    ]


def square_at(wide_ref, i, r):
    per = WIDE // BLOCK
    return wide_ref.at[i // per, pl.ds(r * BLOCK, BLOCK), pl.ds(i % per * BLOCK, BLOCK)]


def started(groups, sems):
    copies, count = [], 0
    for group in groups:
        copies.append([pltpu.make_async_copy(s, d, sems.at[count + i]) for i, (s, d) in enumerate(group)])
        count += len(group)
    for group in copies:
        for copy in group:
            copy.start()
    return copies


def wait(group):
    for copy in group:
        copy.wait()


def load_body(first, after_ref, src_hbm, old_ref, place_ref, sems):
    for group in started(column_blocks(src_hbm, place_ref, first, 4), sems):
        wait(group)


def load(after, src, place, also, first, name):
    return call(
        functools.partial(load_body, first),
        name,
        [like(place)],
        (after, src, place),
        "vhv",
        [pltpu.SemaphoreType.DMA((8,))],
        traffic=size_of(src),
        aliases={2: 0},
        also=also,
    )[0]


def beside(i, fs, ft):
    side, rest = divmod(i * BLOCK, ft // 2)
    return side * (fs // 2) + rest


def partials_body(
    arr_ref, dt_ref, ds_ref, ut_hbm, gs_hbm, us_hbm, old_wide, mine_ref, theirs_ref, wide_ref, part, sems
):
    fs, width = ds_ref.shape
    ft = dt_ref.shape[0]
    ns, nt = fs // WIDE, ft // WIDE
    groups = column_blocks(ut_hbm, wide_ref, nt, 2) + column_blocks(gs_hbm, wide_ref, 2 * nt, 2)
    groups += column_blocks(us_hbm, wide_ref, 2 * nt + ns, 2)
    copies = started(groups, sems)
    x = arr_ref[:, :width]
    c = arr_ref[:, width : 2 * width]
    speech = is_speech(arr_ref)

    def put(k, start, value, pick):
        cut = slice(start, start + BLOCK)
        if pick and start % (fs // 2) < ft // 2:
            value = jnp.where(speech, value, part[k, :, cut])
        part[k, :, cut] = value

    def put_wide(k, start, value, pick):
        for i in range(start, start + WIDE, BLOCK):
            place = i if pick else beside(i // BLOCK, fs, ft)
            put(k, place, value[:, i - start : i - start + BLOCK], pick)

    for k, ref in enumerate((dt_ref, ds_ref)):
        for i in range(0, ref.shape[0], BLOCK):
            place = i if k else beside(i // BLOCK, fs, ft)
            put(2, place, contract_last(c, ref[i : i + BLOCK, :]), k == 1)
    for k in range(2):
        for i in range(nt):
            if k == 1:
                wait(copies[i])
            put_wide(k, i * WIDE, times(x, wide_ref[k * nt + i]), False)
    for k in range(2):
        for i in range(ns):
            wait(copies[nt + k * ns + i])
            put_wide(k, i * WIDE, times(x, wide_ref[2 * nt + k * ns + i]), True)
    half = fs // 2
    odd = parity()
    for k in range(3):
        mine_ref[k] = part[k, :, pl.ds(pl.multiple_of(odd * half, half), half)]
        theirs_ref[k] = part[k, :, pl.ds(pl.multiple_of((1 - odd) * half, half), half)]


def partials(arr, up_t, gate_s, up_s, down_t, down_s, wide):
    rows, fs = arr.shape[0], gate_s.shape[1]
    half = ((3, rows, fs // 2), F32)
    return call(
        partials_body,
        "hidden_partials",
        [half, half, like(wide)],
        (arr, down_t, down_s, up_t, gate_s, up_s, wide),
        "vvvhhhv",
        [pltpu.VMEM((3, rows, fs), F32), pltpu.SemaphoreType.DMA(((4 * fs + 2 * up_t.shape[1]) // WIDE,))],
        2 * rows * (wide.size + down_s.size + down_t.size),
        size_of(up_t, gate_s, up_s),
        aliases={6: 2},
    )


def core_sum_body(mine_ref, got_ref, sum_ref, send_ref):
    total = mine_ref[...] + got_ref[...]
    sum_ref[...] = total
    send_ref[...] = total.astype(BF16)


def hidden_body(sum_ref, got_ref, out_ref):
    total = [sum_ref[k] + got_ref[k].astype(F32) for k in range(3)]
    g, u, dh = total
    sig = jax.nn.sigmoid(g)
    silu = g * sig
    out_ref[0] = (silu * u).astype(BF16)
    out_ref[1] = (dh * u * sig * (1.0 + g * (1.0 - sig))).astype(BF16)
    out_ref[2] = (dh * silu).astype(BF16)


def turn_body(first, count, old_ref, wide_ref):
    row, col = (lax.broadcasted_iota(jnp.int32, (ROWS, ROWS), i) for i in range(2))
    one = (row == col).astype(BF16)
    squares = wide_ref.shape[1] // BLOCK
    for n in range(count * squares):
        i, r = first + n // squares, n % squares
        place = square_at(wide_ref, i, r)
        square = place[...]
        if n % 2:
            turned = square.T
        else:
            parts = [contract_last(one, square[:, j : j + ROWS]) for j in range(0, BLOCK, ROWS)]
            turned = jnp.concatenate([p.astype(BF16) for p in parts], axis=0)
        place[...] = turned


def turn(wide, also, first, count, name):
    return call(
        functools.partial(turn_body, first, count),
        name,
        [like(wide)],
        (wide,),
        "v",
        traffic=4 * count * wide.shape[1] * BLOCK,
        aliases={0: 0},
        also=also,
    )[0]


def mixed_half(h, speech, side, dt_ref, ds_ref):
    half_s, half_t, width = ds_ref.shape[0] // 2, dt_ref.shape[0] // 2, ds_ref.shape[1]
    zero = jnp.zeros_like(h)
    hs, ht = jnp.where(speech, h, zero), jnp.where(speech, zero, h)[:, :half_t]
    rows_s = pl.ds(pl.multiple_of(side * half_s, BLOCK), half_s)
    rows_t = pl.ds(pl.multiple_of(side * half_t, BLOCK), half_t)
    cuts = [slice(i, i + BLOCK) for i in range(0, width, BLOCK)]
    return [times(hs, ds_ref[rows_s, cut]) + times(ht, dt_ref[rows_t, cut]) for cut in cuts]


def mixed_own_body(arr_ref, done_ref, dt_ref, ds_ref, out_ref):
    parts = mixed_half(done_ref[0], is_speech(arr_ref), parity(), dt_ref, ds_ref)
    for i, value in enumerate(parts):
        out_ref[:, i * BLOCK : (i + 1) * BLOCK] = value


def back_body(
    turned, grad_rows, arr_ref, done_ref, other_ref, own_ref, wide_ref, dt_ref, ds_ref,
    keep_ref, send_ref, hs_ref, ht_ref, grad_hbm, dgs, dgt, dus, dut, out, slots, sems,
):
    speech = is_speech(arr_ref)
    fs, ft = hs_ref.shape[1], ht_ref.shape[1]
    ns, nt = fs // BLOCK, ft // BLOCK
    odd = parity() == 1
    for k, (s, t) in enumerate(((hs_ref, ht_ref), (dgs, dgt), (dus, dut))):
        done, other = done_ref[k], other_ref[k]
        value = jnp.concatenate([jnp.where(odd, other, done), jnp.where(odd, done, other)], axis=1)
        zero = jnp.zeros_like(value)
        s[...] = jnp.where(speech, value, zero)
        value = jnp.where(speech, zero, value)
        for i in range(nt):
            start = beside(i, fs, ft)
            t[:, i * BLOCK : (i + 1) * BLOCK] = value[:, start : start + BLOCK]
    width = ds_ref.shape[1]
    for i, value in enumerate(mixed_half(other_ref[0], speech, 1 - parity(), dt_ref, ds_ref)):
        cut = slice(i * BLOCK, (i + 1) * BLOCK)
        out[:, cut] = own_ref[:, cut] + value
    blocks = [(dgt, nt), (dut, nt), (dgs, ns), (dus, ns)]
    blocks = [(ref, i) for ref, n in blocks for i in range(n)]
    c = arr_ref[:, width : 2 * width]
    count, n_slots = grad_rows // ROWS, slots.shape[0]
    squares = [(r, b) for r in range(width // BLOCK) for b in range(len(blocks))]
    copies, total = [], None
    for n, (r, b) in enumerate(squares):
        ref, j = blocks[b]
        product = times if b in turned else contract_last
        value = product(ref[:, j * BLOCK : (j + 1) * BLOCK], square_at(wide_ref, b, r)[...])
        total = value if b == 0 else total + value
        if b == len(blocks) - 1:
            start = width + r * BLOCK
            out[:, start : start + BLOCK] = total
        while len(copies) * len(squares) < (n + 1) * count:
            i = len(copies)
            if i >= n_slots:
                copies[i - n_slots].wait()
            cut = slice(i * ROWS, (i + 1) * ROWS)
            slots[i % n_slots] = contract_first(hs_ref[:, cut], c).astype(BF16)
            copies.append(pltpu.make_async_copy(slots.at[i % n_slots], grad_hbm.at[cut], sems.at[i % n_slots]))
            copies[i].start()
    for copy in copies[-n_slots:]:
        copy.wait()
    half = keep_ref.shape[0]
    keep_ref[...] = out[:half]
    send_ref[...] = out[half:].astype(BF16)


def back(arr, done, other, own, wide, down_t, down_s, turned, grad_rows):
    rows, width = arr.shape[0], down_s.shape[1]
    fs, ft = down_s.shape[0], down_t.shape[0]
    hidden = [((rows, fs), BF16), ((rows, ft), BF16)]
    scratch = [pltpu.VMEM(*s) for s in hidden + hidden] + [pltpu.VMEM((rows, 2 * width), F32)]
    scratch += [pltpu.VMEM((SLOTS, ROWS, width), BF16), pltpu.SemaphoreType.DMA((SLOTS,))]
    return call(
        functools.partial(back_body, turned, grad_rows),
        "token_partials",
        [((rows // 2, 2 * width), F32), ((rows // 2, 2 * width), BF16)] + hidden + [like(down_s)],
        (arr, done, other, own, wide, down_t, down_s),
        "vvvvvvv",
        scratch,
        2 * rows * (wide.size + down_t.size + down_s.size),
        out_places="vvvvh",
    )


def token_sum_body(keep_ref, got_ref, after_ref, next_ref, *send_refs):
    total = keep_ref[...] + got_ref[...].astype(F32)
    own = next_ref.shape[0]
    next_ref[...] = total[:own]
    for i, ref in enumerate(send_refs):
        ref[...] = total[(i + 1) * own : (i + 2) * own].astype(ref.dtype)


def token_sum(keep, got, after, own, name):
    rows, width = keep.shape
    outs = [((own, width), F32)] + [((own, width), BF16)] * (rows // own - 1)
    return call(token_sum_body, name, outs, (keep, got, after), "vvh")


def last_sum_body(keep_ref, got_a, got_b, got_c, mixed_hbm, grad_hbm, mixed_ref, grad_ref, sems):
    total = keep_ref[...] + got_a[...].astype(F32)
    total = (total + got_b[...].astype(F32) + got_c[...].astype(F32)).astype(BF16)
    width = mixed_ref.shape[1]
    mixed_ref[...] = total[:, :width]
    grad_ref[...] = total[:, width:]
    copies = [
        pltpu.make_async_copy(mixed_ref, mixed_hbm, sems.at[0]),
        pltpu.make_async_copy(grad_ref, grad_hbm, sems.at[1]),
    ]
    for copy in copies:
        copy.start()
    for copy in copies:
        copy.wait()


def outer_steps(c, steps, slots, sems):
    copies = []
    for i, (h, place) in enumerate(steps):
        slots[i] = contract_first(h, c).astype(BF16)
        copies.append(pltpu.make_async_copy(slots.at[i], place, sems.at[i]))
        copies[-1].start()
    for copy in copies:
        copy.wait()


def outer_body(speech, text, after_ref, arr_ref, hs_ref, ht_ref, *refs):
    slots, sems = refs[-2:]
    outs = list(refs[-2 - bool(speech) - bool(text) : -2])
    width = outs[0].shape[1]
    steps = []
    for h_ref, blocks in ((hs_ref, speech), (ht_ref, text)):
        out = outs.pop(0) if blocks else None
        cuts = [slice(i * ROWS, (i + 1) * ROWS) for i in blocks]
        steps += [(h_ref[:, cut], out.at[cut]) for cut in cuts]
    outer_steps(arr_ref[:, width : 2 * width], steps, slots, sems)


def flip(value, axes, bit, n):
    return lax.ppermute(value, axes, [(i, i ^ bit) for i in range(n)])


def by_kernels(n_seq, n_tok, tokens, modality, cotangent, gate_s, up_s, down_s, gate_t, up_t, down_t):
    rows, width = tokens.shape
    fs, ft = gate_s.shape[1], gate_t.shape[1]
    wide = ((2 * (fs + ft) // WIDE, width, WIDE), BF16)
    pair = [pltpu.VMEM((rows, width), BF16)] * 2

    packed = ((rows, 2 * width + 128), BF16)
    scratch = pair + [pltpu.SMEM((rows,), jnp.int32), pltpu.SemaphoreType.DMA((3,))]
    wide, arr = call(pack_body, "pack", [wide, packed], (modality, tokens, cotangent), "hhh", scratch)
    got = flip(arr, TOK, HOPS[0], n_tok)
    wide = load(arr, gate_t, wide, (), 0, "load_gate_text")
    arr = join(arr, got, "join_4", (wide,))
    got = flip(arr, TOK, HOPS[1], n_tok)
    arr = join(arr, got, "join_8", (wide,))
    arr = join(arr, flip(arr, TOK, HOPS[2], n_tok), "join_16", (wide, down_t, down_s))

    mine, theirs, wide = partials(arr, up_t, gate_s, up_s, down_t, down_s, wide)
    blocks = 2 * (fs + ft) // BLOCK
    got = flip(theirs, "seq", 1, n_seq)
    wide = turn(wide, (down_t, down_s), 0, TURN_FIRST, "turn_1")
    total, send = call(
        core_sum_body, "core_sum", [like(mine), (mine.shape, BF16)], (mine, got), "vv", also=(wide, down_t, down_s)
    )
    got = flip(send, "seq", 2, n_seq)
    wide = turn(wide, (down_t, down_s), TURN_FIRST, blocks - TURN_FIRST, "turn_2")
    done = call(hidden_body, "hidden", [(mine.shape, BF16)], (total, got), "vv", also=(wide, down_t, down_s))[0]
    other = flip(done, "seq", 1, n_seq)
    own = call(
        mixed_own_body, "mixed_own", [((arr.shape[0], width), F32)], (arr, done, down_t, down_s), "vvvv",
        flops=arr.shape[0] * (down_s.size + down_t.size), also=(wide,),
    )[0]
    early = EARLY_ROWS
    keep, send, hs, ht, down_s_grad = back(arr, done, other, own, wide, down_t, down_s, range(blocks), early)

    def outer(after, speech, text, old, name):
        count = len(speech) + len(text)
        outs = [like(w) for w, blocks in ((down_s, speech), (down_t, text)) if blocks]
        return call(
            functools.partial(outer_body, speech, text), name, outs, (after, arr, hs, ht, *old),
            "vvvv" + "h" * len(old), [pltpu.VMEM((count, ROWS, width), BF16), pltpu.SemaphoreType.DMA((count,))],
            2 * arr.shape[0] * count * ROWS * width, 2 * count * ROWS * width, limit=8,
            out_places="h" * len(outs), aliases={4: 0} if old else None,
        )

    ns, nt = fs // ROWS, ft // ROWS
    got = flip(send, TOK, HOPS[2], n_tok)
    down_s_grad, down_t_grad = outer(keep, range(early // ROWS, ns), range(TEXT_FIRST), (down_s_grad,), "down_grad_1")
    keep, *sends = token_sum(keep, got, down_t_grad, rows, "token_sum_4")
    bits = (HOPS[0], HOPS[1], HOPS[0] ^ HOPS[1])
    gots = [flip(send, TOK, bit, n_tok) for send, bit in zip(sends, bits)]
    down_t_grad = outer(keep, (), range(TEXT_FIRST, nt), (down_t_grad,), "down_grad_2")[0]
    outs = [((rows, width), BF16)] * 2
    mixed, token_grad = call(
        last_sum_body, "token_sum_1", outs, (keep, *gots), "vvvv", pair + [pltpu.SemaphoreType.DMA((2,))],
        out_places="hh",
    )
    return mixed, token_grad, down_s_grad, down_t_grad


def by_arrays(n_seq, n_tok, tokens, modality, cotangent, gate_s, up_s, down_s, gate_t, up_t, down_t):
    width = tokens.shape[1]
    ft = gate_t.shape[1]
    kind = jnp.broadcast_to(modality.astype(BF16)[:, None], (modality.shape[0], 128))
    packed = jnp.concatenate([tokens, cotangent, kind], axis=1)
    arrived = lax.all_gather(packed, TOK, axis=0, tiled=True)
    rows, grads = arrived[:, :width], arrived[:, width : 2 * width]
    speech = arrived[:, 2 * width : 2 * width + 1] == 0

    def pick(s, t):
        return jnp.concatenate([jnp.where(speech, s[:, :ft], t), s[:, ft:]], axis=1)

    def halves(v):
        zero = jnp.zeros((), v.dtype)
        return jnp.where(speech, v, zero), jnp.where(speech, zero, v[:, :ft])

    g = pick(times(rows, gate_s), times(rows, gate_t))
    u = pick(times(rows, up_s), times(rows, up_t))
    dh = pick(contract_last(grads, down_s), contract_last(grads, down_t))
    sums = jnp.stack([g, u, dh])
    sums = sums + flip(sums, "seq", 1, n_seq)
    g, u, dh = sums + flip(sums.astype(BF16), "seq", 2, n_seq).astype(F32)
    sig = jax.nn.sigmoid(g)
    h = (g * sig * u).astype(BF16)
    dg = (dh * u * sig * (1.0 + g * (1.0 - sig))).astype(BF16)
    du = (dh * (g * sig)).astype(BF16)
    (hs, ht), (dgs, dgt), (dus, dut) = halves(h), halves(dg), halves(du)
    mixed = times(hs, down_s) + times(ht, down_t)
    grad = contract_last(dgs, gate_s) + contract_last(dus, up_s)
    grad = grad + contract_last(dgt, gate_t) + contract_last(dut, up_t)
    out = jnp.concatenate([mixed, grad], axis=1).astype(BF16)
    out = out.reshape(n_tok, out.shape[0] // n_tok, out.shape[1])
    out = lax.all_to_all(out, TOK, split_axis=0, concat_axis=0, tiled=True)
    total = jnp.sum(out.astype(F32), axis=0).astype(BF16)
    down_s_grad = contract_first(hs, grads).astype(BF16)
    down_t_grad = contract_first(ht, grads).astype(BF16)
    return total[:, :width], total[:, width:], down_s_grad, down_t_grad


def solution(mesh):
    n_seq, n_tok = mesh.shape["seq"], mesh.shape["attn"] * mesh.shape["exp"]

    def run(*args):
        fs, ft, width = args[3].shape[1], args[6].shape[1], args[0].shape[1]
        fits = n_tok == 8 and args[0].shape[0] == 2 and fs >= ft and ft % (2 * WIDE) == 0
        fits = fits and fs % WIDE == 0 and width % BLOCK == 0
        return (by_kernels if fits else by_arrays)(n_seq, n_tok, *args)

    return jax.shard_map(
        run,
        mesh=mesh,
        in_specs=(
            P(TOK, "seq"),
            P(TOK),
            P(TOK, "seq"),
            P("seq", TOK),
            P("seq", TOK),
            P(TOK, "seq"),
            P("seq", TOK),
            P("seq", TOK),
            P(TOK, "seq"),
        ),
        out_specs=(P(TOK, "seq"),) * 4,
        check_vma=False,
    )
```

```python
import functools

import jax
import jax.numpy as jnp
from jax import lax
from jax.experimental import pallas as pl
from jax.experimental.pallas import tpu as pltpu
from jax.sharding import PartitionSpec as P

TOK = ("attn", "exp")
HOPS = (2, 1, 4)
F32 = jnp.float32
BF16 = jnp.bfloat16
MIB = 1 << 20
LIMIT = 6
BLOCK = 512
WIDE = 1024
ROWS = 256
TILE = 128
TURN_FIRST = 5
SLOTS = 4
EARLY_ROWS = 2048
TEXT_FIRST = 2
PLACES = {"h": pl.ANY, "v": pltpu.VMEM, "s": pltpu.SMEM}


def contract_first(left, right):
    return lax.dot_general(left, right, (((0,), (0,)), ((), ())), preferred_element_type=F32)


def contract_last(left, right):
    return lax.dot_general(left, right, (((1,), (1,)), ((), ())), preferred_element_type=F32)


def times(left, right):
    return jnp.dot(left, right, preferred_element_type=F32)


def size_of(*arrays):
    return sum(a.size * jnp.dtype(a.dtype).itemsize for a in arrays)


def constrain(x, place):
    if place == "s":
        return x
    return pltpu.with_memory_space_constraint(x, pltpu.VMEM if place == "v" else pltpu.HBM)


def call(
    body, name, outs, ins, places, scratch=(), flops=0, traffic=0, limit=LIMIT, out_places=None, aliases=None, also=()
):
    out_places = out_places or "v" * len(outs)
    shapes = [pltpu.VMEM(*o) if p == "v" else jax.ShapeDtypeStruct(*o) for o, p in zip(outs, out_places)]
    count = len(ins)

    def seen(*refs):
        body(*refs[:count], *refs[count + len(also) :])

    ins, places = (*ins, *also), places + "v" * len(also)
    return pl.pallas_call(
        seen,
        out_shape=shapes,
        in_specs=[pl.BlockSpec(memory_space=PLACES[p]) for p in places],
        out_specs=[pl.BlockSpec(memory_space=PLACES[p]) for p in out_places],
        scratch_shapes=list(scratch),
        input_output_aliases=aliases or {},
        compiler_params=pltpu.CompilerParams(vmem_limit_bytes=limit * MIB),
        cost_estimate=pl.CostEstimate(flops=flops, bytes_accessed=traffic, transcendentals=0),
        name=name,
    )(*[constrain(x, p) for x, p in zip(ins, places)])


def like(x):
    return x.shape, x.dtype


def parity():
    return lax.rem(lax.axis_index("seq"), 2)


def is_speech(arr_ref):
    return arr_ref[:, arr_ref.shape[1] - 1 :] == 0


def pack_body(kind_hbm, tok_hbm, cot_hbm, wide_ref, out_ref, tok_ref, cot_ref, kind_ref, sems):
    copies = [
        pltpu.make_async_copy(kind_hbm, kind_ref, sems.at[2]),
        pltpu.make_async_copy(tok_hbm, tok_ref, sems.at[0]),
        pltpu.make_async_copy(cot_hbm, cot_ref, sems.at[1]),
    ]
    for copy in copies:
        copy.start()
    width = tok_ref.shape[1]
    row = lax.broadcasted_iota(jnp.int32, (tok_ref.shape[0], 128), 0)
    kind = jnp.zeros(row.shape, F32)
    for copy in copies:
        copy.wait()
    for i in range(tok_ref.shape[0]):
        kind = jnp.where(row == i, kind_ref[i].astype(F32), kind)
    out_ref[:, 2 * width :] = kind.astype(BF16)
    out_ref[:, :width] = tok_ref[...]
    out_ref[:, width : 2 * width] = cot_ref[...]


def join_body(a_ref, b_ref, out_ref):
    both = jnp.concatenate([a_ref[...].astype(F32), b_ref[...].astype(F32)], axis=0)
    out_ref[...] = both.astype(BF16)


def join(a, b, name, also):
    return call(join_body, name, [((2 * a.shape[0], a.shape[1]), BF16)], (a, b), "vv", also=also)[0]


def column_blocks(src, wide, first, cuts):
    rows = src.shape[0] // cuts
    parts = [pl.ds(j * rows, rows) for j in range(cuts)]
    return [
        [(src.at[part, pl.ds(i * WIDE, WIDE)], wide.at[first + i, part]) for part in parts]
        for i in range(src.shape[1] // WIDE)
    ]


def square_at(wide_ref, i, r):
    per = WIDE // BLOCK
    return wide_ref.at[i // per, pl.ds(r * BLOCK, BLOCK), pl.ds(i % per * BLOCK, BLOCK)]


def started(groups, sems):
    copies, count = [], 0
    for group in groups:
        copies.append([pltpu.make_async_copy(s, d, sems.at[count + i]) for i, (s, d) in enumerate(group)])
        count += len(group)
    for group in copies:
        for copy in group:
            copy.start()
    return copies


def wait(group):
    for copy in group:
        copy.wait()


def load_body(first, after_ref, src_hbm, old_ref, place_ref, sems):
    for group in started(column_blocks(src_hbm, place_ref, first, 4), sems):
        wait(group)


def load(after, src, place, also, first, name):
    return call(
        functools.partial(load_body, first),
        name,
        [like(place)],
        (after, src, place),
        "vhv",
        [pltpu.SemaphoreType.DMA((8,))],
        traffic=size_of(src),
        aliases={2: 0},
        also=also,
    )[0]


def beside(i, fs, ft):
    side, rest = divmod(i * BLOCK, ft // 2)
    return side * (fs // 2) + rest


def partials_body(
    arr_ref, dt_ref, ds_ref, ut_hbm, gs_hbm, us_hbm, old_wide, mine_ref, theirs_ref, wide_ref, part, sems
):
    fs, width = ds_ref.shape
    ft = dt_ref.shape[0]
    ns, nt = fs // WIDE, ft // WIDE
    groups = column_blocks(ut_hbm, wide_ref, nt, 2) + column_blocks(gs_hbm, wide_ref, 2 * nt, 2)
    groups += column_blocks(us_hbm, wide_ref, 2 * nt + ns, 2)
    copies = started(groups, sems)
    x = arr_ref[:, :width]
    c = arr_ref[:, width : 2 * width]
    speech = is_speech(arr_ref)

    def put(k, start, value, pick):
        cut = slice(start, start + BLOCK)
        if pick and start % (fs // 2) < ft // 2:
            value = jnp.where(speech, value, part[k, :, cut])
        part[k, :, cut] = value

    def put_wide(k, start, value, pick):
        for i in range(start, start + WIDE, BLOCK):
            place = i if pick else beside(i // BLOCK, fs, ft)
            put(k, place, value[:, i - start : i - start + BLOCK], pick)

    for k, ref in enumerate((dt_ref, ds_ref)):
        for i in range(0, ref.shape[0], BLOCK):
            place = i if k else beside(i // BLOCK, fs, ft)
            put(2, place, contract_last(c, ref[i : i + BLOCK, :]), k == 1)
    for k in range(2):
        for i in range(nt):
            if k == 1:
                wait(copies[i])
            put_wide(k, i * WIDE, times(x, wide_ref[k * nt + i]), False)
    for k in range(2):
        for i in range(ns):
            wait(copies[nt + k * ns + i])
            put_wide(k, i * WIDE, times(x, wide_ref[2 * nt + k * ns + i]), True)
    half = fs // 2
    odd = parity()
    for k in range(3):
        mine_ref[k] = part[k, :, pl.ds(pl.multiple_of(odd * half, half), half)]
        theirs_ref[k] = part[k, :, pl.ds(pl.multiple_of((1 - odd) * half, half), half)]


def partials(arr, up_t, gate_s, up_s, down_t, down_s, wide):
    rows, fs = arr.shape[0], gate_s.shape[1]
    half = ((3, rows, fs // 2), F32)
    return call(
        partials_body,
        "hidden_partials",
        [half, half, like(wide)],
        (arr, down_t, down_s, up_t, gate_s, up_s, wide),
        "vvvhhhv",
        [pltpu.VMEM((3, rows, fs), F32), pltpu.SemaphoreType.DMA(((4 * fs + 2 * up_t.shape[1]) // WIDE,))],
        2 * rows * (wide.size + down_s.size + down_t.size),
        size_of(up_t, gate_s, up_s),
        aliases={6: 2},
    )


def core_sum_body(mine_ref, got_ref, sum_ref, send_ref):
    total = mine_ref[...] + got_ref[...]
    sum_ref[...] = total
    send_ref[...] = total.astype(BF16)


def hidden_body(sum_ref, got_ref, out_ref):
    total = [sum_ref[k] + got_ref[k].astype(F32) for k in range(3)]
    g, u, dh = total
    sig = jax.nn.sigmoid(g)
    silu = g * sig
    out_ref[0] = (silu * u).astype(BF16)
    out_ref[1] = (dh * u * sig * (1.0 + g * (1.0 - sig))).astype(BF16)
    out_ref[2] = (dh * silu).astype(BF16)


def turn_body(first, count, old_ref, wide_ref):
    row, col = (lax.broadcasted_iota(jnp.int32, (ROWS, ROWS), i) for i in range(2))
    one = (row == col).astype(BF16)
    squares = wide_ref.shape[1] // BLOCK
    for n in range(count * squares):
        i, r = first + n // squares, n % squares
        place = square_at(wide_ref, i, r)
        square = place[...]
        if n % 2:
            turned = square.T
        else:
            parts = [contract_last(one, square[:, j : j + ROWS]) for j in range(0, BLOCK, ROWS)]
            turned = jnp.concatenate([p.astype(BF16) for p in parts], axis=0)
        place[...] = turned


def turn(wide, also, first, count, name):
    return call(
        functools.partial(turn_body, first, count),
        name,
        [like(wide)],
        (wide,),
        "v",
        traffic=4 * count * wide.shape[1] * BLOCK,
        aliases={0: 0},
        also=also,
    )[0]


def mixed_half(h, speech, side, dt_ref, ds_ref):
    half_s, half_t, width = ds_ref.shape[0] // 2, dt_ref.shape[0] // 2, ds_ref.shape[1]
    zero = jnp.zeros_like(h)
    hs, ht = jnp.where(speech, h, zero), jnp.where(speech, zero, h)[:, :half_t]
    rows_s = pl.ds(pl.multiple_of(side * half_s, BLOCK), half_s)
    rows_t = pl.ds(pl.multiple_of(side * half_t, BLOCK), half_t)
    cuts = [slice(i, i + BLOCK) for i in range(0, width, BLOCK)]
    return [times(hs, ds_ref[rows_s, cut]) + times(ht, dt_ref[rows_t, cut]) for cut in cuts]


def mixed_own_body(arr_ref, done_ref, dt_ref, ds_ref, out_ref):
    parts = mixed_half(done_ref[0], is_speech(arr_ref), parity(), dt_ref, ds_ref)
    for i, value in enumerate(parts):
        out_ref[:, i * BLOCK : (i + 1) * BLOCK] = value


def back_body(
    turned, grad_rows, arr_ref, done_ref, other_ref, own_ref, wide_ref, dt_ref, ds_ref,
    keep_ref, send_ref, hs_ref, ht_ref, grad_hbm, dgs, dgt, dus, dut, out, slots, sems,
):
    speech = is_speech(arr_ref)
    fs, ft = hs_ref.shape[1], ht_ref.shape[1]
    ns, nt = fs // BLOCK, ft // BLOCK
    odd = parity() == 1
    for k, (s, t) in enumerate(((hs_ref, ht_ref), (dgs, dgt), (dus, dut))):
        done, other = done_ref[k], other_ref[k]
        value = jnp.concatenate([jnp.where(odd, other, done), jnp.where(odd, done, other)], axis=1)
        zero = jnp.zeros_like(value)
        s[...] = jnp.where(speech, value, zero)
        value = jnp.where(speech, zero, value)
        for i in range(nt):
            start = beside(i, fs, ft)
            t[:, i * BLOCK : (i + 1) * BLOCK] = value[:, start : start + BLOCK]
    width = ds_ref.shape[1]
    for i, value in enumerate(mixed_half(other_ref[0], speech, 1 - parity(), dt_ref, ds_ref)):
        cut = slice(i * BLOCK, (i + 1) * BLOCK)
        out[:, cut] = own_ref[:, cut] + value
    blocks = [(dgt, nt), (dut, nt), (dgs, ns), (dus, ns)]
    blocks = [(ref, i) for ref, n in blocks for i in range(n)]
    c = arr_ref[:, width : 2 * width]
    count, n_slots = grad_rows // ROWS, slots.shape[0]
    squares = [(r, b) for r in range(width // BLOCK) for b in range(len(blocks))]
    copies, total = [], None
    for n, (r, b) in enumerate(squares):
        ref, j = blocks[b]
        product = times if b in turned else contract_last
        value = product(ref[:, j * BLOCK : (j + 1) * BLOCK], square_at(wide_ref, b, r)[...])
        total = value if b == 0 else total + value
        if b == len(blocks) - 1:
            start = width + r * BLOCK
            out[:, start : start + BLOCK] = total
        while len(copies) * len(squares) < (n + 1) * count:
            i = len(copies)
            if i >= n_slots:
                copies[i - n_slots].wait()
            cut = slice(i * ROWS, (i + 1) * ROWS)
            outer_block(hs_ref[:, cut], c, slots.at[i % n_slots])
            copies.append(pltpu.make_async_copy(slots.at[i % n_slots], grad_hbm.at[cut], sems.at[i % n_slots]))
            copies[i].start()
    for copy in copies[-n_slots:]:
        copy.wait()
    half = keep_ref.shape[0]
    keep_ref[...] = out[:half]
    send_ref[...] = out[half:].astype(BF16)


def back(arr, done, other, own, wide, down_t, down_s, turned, grad_rows):
    rows, width = arr.shape[0], down_s.shape[1]
    fs, ft = down_s.shape[0], down_t.shape[0]
    hidden = [((rows, fs), BF16), ((rows, ft), BF16)]
    scratch = [pltpu.VMEM(*s) for s in hidden + hidden] + [pltpu.VMEM((rows, 2 * width), F32)]
    scratch += [pltpu.VMEM((SLOTS, ROWS, width), BF16), pltpu.SemaphoreType.DMA((SLOTS,))]
    return call(
        functools.partial(back_body, turned, grad_rows),
        "token_partials",
        [((rows // 2, 2 * width), F32), ((rows // 2, 2 * width), BF16)] + hidden + [like(down_s)],
        (arr, done, other, own, wide, down_t, down_s),
        "vvvvvvv",
        scratch,
        2 * rows * (wide.size + down_t.size + down_s.size),
        out_places="vvvvh",
    )


def token_sum_body(keep_ref, got_ref, after_ref, next_ref, *send_refs):
    total = keep_ref[...] + got_ref[...].astype(F32)
    own = next_ref.shape[0]
    next_ref[...] = total[:own]
    for i, ref in enumerate(send_refs):
        ref[...] = total[(i + 1) * own : (i + 2) * own].astype(ref.dtype)


def token_sum(keep, got, after, own, name):
    rows, width = keep.shape
    outs = [((own, width), F32)] + [((own, width), BF16)] * (rows // own - 1)
    return call(token_sum_body, name, outs, (keep, got, after), "vvh")


def last_sum_body(keep_ref, got_a, got_b, got_c, mixed_hbm, grad_hbm, mixed_ref, grad_ref, sems):
    total = keep_ref[...] + got_a[...].astype(F32)
    total = (total + got_b[...].astype(F32) + got_c[...].astype(F32)).astype(BF16)
    width = mixed_ref.shape[1]
    mixed_ref[...] = total[:, :width]
    grad_ref[...] = total[:, width:]
    copies = [
        pltpu.make_async_copy(mixed_ref, mixed_hbm, sems.at[0]),
        pltpu.make_async_copy(grad_ref, grad_hbm, sems.at[1]),
    ]
    for copy in copies:
        copy.start()
    for copy in copies:
        copy.wait()


def outer_block(h, c, place):
    for i in range(0, h.shape[1], TILE):
        turned = h[:, i : i + TILE].T
        for j in range(0, c.shape[1], 2 * TILE):
            place[i : i + TILE, j : j + 2 * TILE] = times(turned, c[:, j : j + 2 * TILE]).astype(BF16)


def outer_steps(c, steps, slots, sems):
    copies = []
    for i, (h, place) in enumerate(steps):
        outer_block(h, c, slots.at[i])
        copies.append(pltpu.make_async_copy(slots.at[i], place, sems.at[i]))
        copies[-1].start()
    for copy in copies:
        copy.wait()


def outer_body(speech, text, after_ref, arr_ref, hs_ref, ht_ref, *refs):
    slots, sems = refs[-2:]
    outs = list(refs[-2 - bool(speech) - bool(text) : -2])
    width = outs[0].shape[1]
    steps = []
    for h_ref, blocks in ((hs_ref, speech), (ht_ref, text)):
        out = outs.pop(0) if blocks else None
        cuts = [slice(i * ROWS, (i + 1) * ROWS) for i in blocks]
        steps += [(h_ref[:, cut], out.at[cut]) for cut in cuts]
    outer_steps(arr_ref[:, width : 2 * width], steps, slots, sems)


def flip(value, axes, bit, n):
    return lax.ppermute(value, axes, [(i, i ^ bit) for i in range(n)])


def by_kernels(n_seq, n_tok, tokens, modality, cotangent, gate_s, up_s, down_s, gate_t, up_t, down_t):
    rows, width = tokens.shape
    fs, ft = gate_s.shape[1], gate_t.shape[1]
    wide = ((2 * (fs + ft) // WIDE, width, WIDE), BF16)
    pair = [pltpu.VMEM((rows, width), BF16)] * 2

    packed = ((rows, 2 * width + 128), BF16)
    scratch = pair + [pltpu.SMEM((rows,), jnp.int32), pltpu.SemaphoreType.DMA((3,))]
    wide, arr = call(pack_body, "pack", [wide, packed], (modality, tokens, cotangent), "hhh", scratch)
    got = flip(arr, TOK, HOPS[0], n_tok)
    wide = load(arr, gate_t, wide, (), 0, "load_gate_text")
    arr = join(arr, got, "join_4", (wide,))
    got = flip(arr, TOK, HOPS[1], n_tok)
    arr = join(arr, got, "join_8", (wide,))
    arr = join(arr, flip(arr, TOK, HOPS[2], n_tok), "join_16", (wide, down_t, down_s))

    mine, theirs, wide = partials(arr, up_t, gate_s, up_s, down_t, down_s, wide)
    blocks = 2 * (fs + ft) // BLOCK
    got = flip(theirs, "seq", 1, n_seq)
    wide = turn(wide, (down_t, down_s), 0, TURN_FIRST, "turn_1")
    total, send = call(
        core_sum_body, "core_sum", [like(mine), (mine.shape, BF16)], (mine, got), "vv", also=(wide, down_t, down_s)
    )
    got = flip(send, "seq", 2, n_seq)
    wide = turn(wide, (down_t, down_s), TURN_FIRST, blocks - TURN_FIRST, "turn_2")
    done = call(hidden_body, "hidden", [(mine.shape, BF16)], (total, got), "vv", also=(wide, down_t, down_s))[0]
    other = flip(done, "seq", 1, n_seq)
    own = call(
        mixed_own_body, "mixed_own", [((arr.shape[0], width), F32)], (arr, done, down_t, down_s), "vvvv",
        flops=arr.shape[0] * (down_s.size + down_t.size), also=(wide,),
    )[0]
    early = EARLY_ROWS
    keep, send, hs, ht, down_s_grad = back(arr, done, other, own, wide, down_t, down_s, range(blocks), early)

    def outer(after, speech, text, old, name):
        count = len(speech) + len(text)
        outs = [like(w) for w, blocks in ((down_s, speech), (down_t, text)) if blocks]
        return call(
            functools.partial(outer_body, speech, text), name, outs, (after, arr, hs, ht, *old),
            "vvvv" + "h" * len(old), [pltpu.VMEM((count, ROWS, width), BF16), pltpu.SemaphoreType.DMA((count,))],
            2 * arr.shape[0] * count * ROWS * width, 2 * count * ROWS * width, limit=8,
            out_places="h" * len(outs), aliases={4: 0} if old else None,
        )

    ns, nt = fs // ROWS, ft // ROWS
    got = flip(send, TOK, HOPS[2], n_tok)
    down_s_grad, down_t_grad = outer(keep, range(early // ROWS, ns), range(TEXT_FIRST), (down_s_grad,), "down_grad_1")
    keep, *sends = token_sum(keep, got, down_t_grad, rows, "token_sum_4")
    bits = (HOPS[0], HOPS[1], HOPS[0] ^ HOPS[1])
    gots = [flip(sends[i], TOK, bits[i], n_tok) for i in (2, 0, 1)]
    down_t_grad = outer(keep, (), range(TEXT_FIRST, nt), (down_t_grad,), "down_grad_2")[0]
    outs = [((rows, width), BF16)] * 2
    mixed, token_grad = call(
        last_sum_body, "token_sum_1", outs, (keep, *gots), "vvvv", pair + [pltpu.SemaphoreType.DMA((2,))],
        out_places="hh",
    )
    return mixed, token_grad, down_s_grad, down_t_grad


def by_arrays(n_seq, n_tok, tokens, modality, cotangent, gate_s, up_s, down_s, gate_t, up_t, down_t):
    width = tokens.shape[1]
    ft = gate_t.shape[1]
    kind = jnp.broadcast_to(modality.astype(BF16)[:, None], (modality.shape[0], 128))
    packed = jnp.concatenate([tokens, cotangent, kind], axis=1)
    arrived = lax.all_gather(packed, TOK, axis=0, tiled=True)
    rows, grads = arrived[:, :width], arrived[:, width : 2 * width]
    speech = arrived[:, 2 * width : 2 * width + 1] == 0

    def pick(s, t):
        return jnp.concatenate([jnp.where(speech, s[:, :ft], t), s[:, ft:]], axis=1)

    def halves(v):
        zero = jnp.zeros((), v.dtype)
        return jnp.where(speech, v, zero), jnp.where(speech, zero, v[:, :ft])

    g = pick(times(rows, gate_s), times(rows, gate_t))
    u = pick(times(rows, up_s), times(rows, up_t))
    dh = pick(contract_last(grads, down_s), contract_last(grads, down_t))
    sums = jnp.stack([g, u, dh])
    sums = sums + flip(sums, "seq", 1, n_seq)
    g, u, dh = sums + flip(sums.astype(BF16), "seq", 2, n_seq).astype(F32)
    sig = jax.nn.sigmoid(g)
    h = (g * sig * u).astype(BF16)
    dg = (dh * u * sig * (1.0 + g * (1.0 - sig))).astype(BF16)
    du = (dh * (g * sig)).astype(BF16)
    (hs, ht), (dgs, dgt), (dus, dut) = halves(h), halves(dg), halves(du)
    mixed = times(hs, down_s) + times(ht, down_t)
    grad = contract_last(dgs, gate_s) + contract_last(dus, up_s)
    grad = grad + contract_last(dgt, gate_t) + contract_last(dut, up_t)
    out = jnp.concatenate([mixed, grad], axis=1).astype(BF16)
    out = out.reshape(n_tok, out.shape[0] // n_tok, out.shape[1])
    out = lax.all_to_all(out, TOK, split_axis=0, concat_axis=0, tiled=True)
    total = jnp.sum(out.astype(F32), axis=0).astype(BF16)
    down_s_grad = contract_first(hs, grads).astype(BF16)
    down_t_grad = contract_first(ht, grads).astype(BF16)
    return total[:, :width], total[:, width:], down_s_grad, down_t_grad


def solution(mesh):
    n_seq, n_tok = mesh.shape["seq"], mesh.shape["attn"] * mesh.shape["exp"]

    def run(*args):
        fs, ft, width = args[3].shape[1], args[6].shape[1], args[0].shape[1]
        fits = n_tok == 8 and args[0].shape[0] == 2 and fs >= ft and ft % (2 * WIDE) == 0
        fits = fits and fs % WIDE == 0 and width % BLOCK == 0
        return (by_kernels if fits else by_arrays)(n_seq, n_tok, *args)

    return jax.shard_map(
        run,
        mesh=mesh,
        in_specs=(
            P(TOK, "seq"),
            P(TOK),
            P(TOK, "seq"),
            P("seq", TOK),
            P("seq", TOK),
            P(TOK, "seq"),
            P("seq", TOK),
            P("seq", TOK),
            P(TOK, "seq"),
        ),
        out_specs=(P(TOK, "seq"),) * 4,
        check_vma=False,
    )
```

```python
import functools

import jax
import jax.numpy as jnp
from jax import lax
from jax.experimental import pallas as pl
from jax.experimental.pallas import tpu as pltpu
from jax.sharding import PartitionSpec as P

TOK = ("attn", "exp")
HOPS = (2, 1, 4)
F32 = jnp.float32
BF16 = jnp.bfloat16
MIB = 1 << 20
LIMIT = 8
BLOCK = 512
WIDE = 1024
ROWS = 256
TILE = 128
TURN_FIRST = 5
EARLY_ROWS = 2048
TEXT_FIRST = 2
PLACES = {"h": pl.ANY, "v": pltpu.VMEM, "s": pltpu.SMEM}


def contract_first(left, right):
    return lax.dot_general(left, right, (((0,), (0,)), ((), ())), preferred_element_type=F32)


def contract_last(left, right):
    return lax.dot_general(left, right, (((1,), (1,)), ((), ())), preferred_element_type=F32)


def times(left, right):
    return jnp.dot(left, right, preferred_element_type=F32)


def size_of(*arrays):
    return sum(a.size * jnp.dtype(a.dtype).itemsize for a in arrays)


def constrain(x, place):
    if place == "s":
        return x
    return pltpu.with_memory_space_constraint(x, pltpu.VMEM if place == "v" else pltpu.HBM)


def call(
    body, name, outs, ins, places, scratch=(), flops=0, traffic=0, limit=LIMIT, out_places=None, aliases=None, also=()
):
    out_places = out_places or "v" * len(outs)
    shapes = [pltpu.VMEM(*o) if p == "v" else jax.ShapeDtypeStruct(*o) for o, p in zip(outs, out_places)]
    count = len(ins)

    def seen(*refs):
        body(*refs[:count], *refs[count + len(also) :])

    ins, places = (*ins, *also), places + "v" * len(also)
    return pl.pallas_call(
        seen,
        out_shape=shapes,
        in_specs=[pl.BlockSpec(memory_space=PLACES[p]) for p in places],
        out_specs=[pl.BlockSpec(memory_space=PLACES[p]) for p in out_places],
        scratch_shapes=list(scratch),
        input_output_aliases=aliases or {},
        compiler_params=pltpu.CompilerParams(vmem_limit_bytes=limit * MIB),
        cost_estimate=pl.CostEstimate(flops=flops, bytes_accessed=traffic, transcendentals=0),
        name=name,
    )(*[constrain(x, p) for x, p in zip(ins, places)])


def like(x):
    return x.shape, x.dtype


def parity():
    return lax.rem(lax.axis_index("seq"), 2)


def is_speech(arr_ref):
    return arr_ref[:, arr_ref.shape[1] - 1 :] == 0


def pack_body(kind_hbm, tok_hbm, cot_hbm, wide_ref, out_ref, tok_ref, cot_ref, kind_ref, sems):
    copies = [
        pltpu.make_async_copy(kind_hbm, kind_ref, sems.at[2]),
        pltpu.make_async_copy(tok_hbm, tok_ref, sems.at[0]),
        pltpu.make_async_copy(cot_hbm, cot_ref, sems.at[1]),
    ]
    for copy in copies:
        copy.start()
    width = tok_ref.shape[1]
    row = lax.broadcasted_iota(jnp.int32, (tok_ref.shape[0], 128), 0)
    kind = jnp.zeros(row.shape, F32)
    for copy in copies:
        copy.wait()
    for i in range(tok_ref.shape[0]):
        kind = jnp.where(row == i, kind_ref[i].astype(F32), kind)
    out_ref[:, 2 * width :] = kind.astype(BF16)
    out_ref[:, :width] = tok_ref[...]
    out_ref[:, width : 2 * width] = cot_ref[...]


def join_body(a_ref, b_ref, out_ref):
    both = jnp.concatenate([a_ref[...].astype(F32), b_ref[...].astype(F32)], axis=0)
    out_ref[...] = both.astype(BF16)


def join(a, b, name, also):
    return call(join_body, name, [((2 * a.shape[0], a.shape[1]), BF16)], (a, b), "vv", also=also)[0]


def column_blocks(src, wide, first, cuts):
    rows = src.shape[0] // cuts
    parts = [pl.ds(j * rows, rows) for j in range(cuts)]
    return [
        [(src.at[part, pl.ds(i * WIDE, WIDE)], wide.at[first + i, part]) for part in parts]
        for i in range(src.shape[1] // WIDE)
    ]


def square_at(wide_ref, i, r):
    per = WIDE // BLOCK
    return wide_ref.at[i // per, pl.ds(r * BLOCK, BLOCK), pl.ds(i % per * BLOCK, BLOCK)]


def started(groups, sems):
    copies, count = [], 0
    for group in groups:
        copies.append([pltpu.make_async_copy(s, d, sems.at[count + i]) for i, (s, d) in enumerate(group)])
        count += len(group)
    for group in copies:
        for copy in group:
            copy.start()
    return copies


def wait(group):
    for copy in group:
        copy.wait()


def load_body(first, after_ref, src_hbm, old_ref, place_ref, sems):
    for group in started(column_blocks(src_hbm, place_ref, first, 4), sems):
        wait(group)


def load(after, src, place, also, first, name):
    return call(
        functools.partial(load_body, first),
        name,
        [like(place)],
        (after, src, place),
        "vhv",
        [pltpu.SemaphoreType.DMA((8,))],
        traffic=size_of(src),
        aliases={2: 0},
        also=also,
    )[0]


def beside(i, fs, ft):
    side, rest = divmod(i * BLOCK, ft // 2)
    return side * (fs // 2) + rest


def partials_body(
    arr_ref, dt_ref, ds_ref, ut_hbm, gs_hbm, us_hbm, old_wide, mine_ref, theirs_ref, wide_ref, part, sems
):
    fs, width = ds_ref.shape
    ft = dt_ref.shape[0]
    ns, nt = fs // WIDE, ft // WIDE
    groups = column_blocks(ut_hbm, wide_ref, nt, 2) + column_blocks(gs_hbm, wide_ref, 2 * nt, 2)
    groups += column_blocks(us_hbm, wide_ref, 2 * nt + ns, 2)
    copies = started(groups, sems)
    x = arr_ref[:, :width]
    c = arr_ref[:, width : 2 * width]
    speech = is_speech(arr_ref)

    def put(k, start, value, pick):
        cut = slice(start, start + BLOCK)
        if pick and start % (fs // 2) < ft // 2:
            value = jnp.where(speech, value, part[k, :, cut])
        part[k, :, cut] = value

    def put_wide(k, start, value, pick):
        for i in range(start, start + WIDE, BLOCK):
            place = i if pick else beside(i // BLOCK, fs, ft)
            put(k, place, value[:, i - start : i - start + BLOCK], pick)

    for k, ref in enumerate((dt_ref, ds_ref)):
        for i in range(0, ref.shape[0], BLOCK):
            place = i if k else beside(i // BLOCK, fs, ft)
            put(2, place, contract_last(c, ref[i : i + BLOCK, :]), k == 1)
    for k in range(2):
        for i in range(nt):
            if k == 1:
                wait(copies[i])
            put_wide(k, i * WIDE, times(x, wide_ref[k * nt + i]), False)
    for k in range(2):
        for i in range(ns):
            wait(copies[nt + k * ns + i])
            put_wide(k, i * WIDE, times(x, wide_ref[2 * nt + k * ns + i]), True)
    half = fs // 2
    odd = parity()
    for k in range(3):
        mine_ref[k] = part[k, :, pl.ds(pl.multiple_of(odd * half, half), half)]
        theirs_ref[k] = part[k, :, pl.ds(pl.multiple_of((1 - odd) * half, half), half)]


def partials(arr, up_t, gate_s, up_s, down_t, down_s, wide):
    rows, fs = arr.shape[0], gate_s.shape[1]
    half = ((3, rows, fs // 2), F32)
    return call(
        partials_body,
        "hidden_partials",
        [half, half, like(wide)],
        (arr, down_t, down_s, up_t, gate_s, up_s, wide),
        "vvvhhhv",
        [pltpu.VMEM((3, rows, fs), F32), pltpu.SemaphoreType.DMA(((4 * fs + 2 * up_t.shape[1]) // WIDE,))],
        2 * rows * (wide.size + down_s.size + down_t.size),
        size_of(up_t, gate_s, up_s),
        aliases={6: 2},
    )


def core_sum_body(mine_ref, got_ref, sum_ref, send_ref):
    total = mine_ref[...] + got_ref[...]
    sum_ref[...] = total
    send_ref[...] = total.astype(BF16)


def hidden_body(sum_ref, got_ref, out_ref):
    total = [sum_ref[k] + got_ref[k].astype(F32) for k in range(3)]
    g, u, dh = total
    sig = jax.nn.sigmoid(g)
    silu = g * sig
    out_ref[0] = (silu * u).astype(BF16)
    out_ref[1] = (dh * u * sig * (1.0 + g * (1.0 - sig))).astype(BF16)
    out_ref[2] = (dh * silu).astype(BF16)


def turn_body(first, count, old_ref, wide_ref):
    row, col = (lax.broadcasted_iota(jnp.int32, (ROWS, ROWS), i) for i in range(2))
    one = (row == col).astype(BF16)
    squares = wide_ref.shape[1] // BLOCK
    for n in range(count * squares):
        i, r = first + n // squares, n % squares
        place = square_at(wide_ref, i, r)
        square = place[...]
        if n % 2:
            turned = square.T
        else:
            parts = [contract_last(one, square[:, j : j + ROWS]) for j in range(0, BLOCK, ROWS)]
            turned = jnp.concatenate([p.astype(BF16) for p in parts], axis=0)
        place[...] = turned


def turn(wide, also, first, count, name):
    return call(
        functools.partial(turn_body, first, count),
        name,
        [like(wide)],
        (wide,),
        "v",
        traffic=4 * count * wide.shape[1] * BLOCK,
        aliases={0: 0},
        also=also,
    )[0]


def mixed_half(h, speech, side, dt_ref, ds_ref):
    half_s, half_t, width = ds_ref.shape[0] // 2, dt_ref.shape[0] // 2, ds_ref.shape[1]
    zero = jnp.zeros_like(h)
    hs, ht = jnp.where(speech, h, zero), jnp.where(speech, zero, h)[:, :half_t]
    rows_s = pl.ds(pl.multiple_of(side * half_s, BLOCK), half_s)
    rows_t = pl.ds(pl.multiple_of(side * half_t, BLOCK), half_t)
    cuts = [slice(i, i + BLOCK) for i in range(0, width, BLOCK)]
    return [times(hs, ds_ref[rows_s, cut]) + times(ht, dt_ref[rows_t, cut]) for cut in cuts]


def mixed_own_body(arr_ref, done_ref, dt_ref, ds_ref, out_ref):
    parts = mixed_half(done_ref[0], is_speech(arr_ref), parity(), dt_ref, ds_ref)
    for i, value in enumerate(parts):
        out_ref[:, i * BLOCK : (i + 1) * BLOCK] = value


def back_body(
    turned, grad_rows, arr_ref, done_ref, other_ref, own_ref, wide_ref, dt_ref, ds_ref,
    keep_ref, send_ref, hs_ref, ht_ref, grad_hbm, dgs, dgt, dus, dut, out, slots, sems,
):
    speech = is_speech(arr_ref)
    fs, ft = hs_ref.shape[1], ht_ref.shape[1]
    ns, nt = fs // BLOCK, ft // BLOCK
    odd = parity() == 1
    for k, (s, t) in enumerate(((hs_ref, ht_ref), (dgs, dgt), (dus, dut))):
        done, other = done_ref[k], other_ref[k]
        value = jnp.concatenate([jnp.where(odd, other, done), jnp.where(odd, done, other)], axis=1)
        zero = jnp.zeros_like(value)
        s[...] = jnp.where(speech, value, zero)
        value = jnp.where(speech, zero, value)
        for i in range(nt):
            start = beside(i, fs, ft)
            t[:, i * BLOCK : (i + 1) * BLOCK] = value[:, start : start + BLOCK]
    width = ds_ref.shape[1]
    for i, value in enumerate(mixed_half(other_ref[0], speech, 1 - parity(), dt_ref, ds_ref)):
        cut = slice(i * BLOCK, (i + 1) * BLOCK)
        out[:, cut] = own_ref[:, cut] + value
    blocks = [(dgt, nt), (dut, nt), (dgs, ns), (dus, ns)]
    blocks = [(ref, i) for ref, n in blocks for i in range(n)]
    c = arr_ref[:, width : 2 * width]
    copies = []
    for i in range(grad_rows // ROWS):
        cut = slice(i * ROWS, (i + 1) * ROWS)
        outer_block(hs_ref[:, cut], c, slots.at[i])
        copies.append(pltpu.make_async_copy(slots.at[i], grad_hbm.at[cut], sems.at[i]))
    for copy in copies:
        copy.start()
    for r in range(width // BLOCK):
        total = jnp.zeros((out.shape[0], BLOCK), F32)
        for b, (ref, j) in enumerate(blocks):
            product = times if b in turned else contract_last
            total += product(ref[:, j * BLOCK : (j + 1) * BLOCK], square_at(wide_ref, b, r)[...])
        start = width + r * BLOCK
        out[:, start : start + BLOCK] = total
    for copy in copies:
        copy.wait()
    half = keep_ref.shape[0]
    keep_ref[...] = out[:half]
    send_ref[...] = out[half:].astype(BF16)


def back(arr, done, other, own, wide, down_t, down_s, turned, grad_rows):
    rows, width = arr.shape[0], down_s.shape[1]
    fs, ft = down_s.shape[0], down_t.shape[0]
    count = grad_rows // ROWS
    hidden = [((rows, fs), BF16), ((rows, ft), BF16)]
    scratch = [pltpu.VMEM(*s) for s in hidden + hidden] + [pltpu.VMEM((rows, 2 * width), F32)]
    scratch += [pltpu.VMEM((count, ROWS, width), BF16), pltpu.SemaphoreType.DMA((count,))]
    return call(
        functools.partial(back_body, turned, grad_rows),
        "token_partials",
        [((rows // 2, 2 * width), F32), ((rows // 2, 2 * width), BF16)] + hidden + [like(down_s)],
        (arr, done, other, own, wide, down_t, down_s),
        "vvvvvvv",
        scratch,
        2 * rows * (wide.size + down_t.size + down_s.size),
        out_places="vvvvh",
    )


def token_sum_body(keep_ref, got_ref, after_ref, next_ref, *send_refs):
    total = keep_ref[...] + got_ref[...].astype(F32)
    own = next_ref.shape[0]
    next_ref[...] = total[:own]
    for i, ref in enumerate(send_refs):
        ref[...] = total[(i + 1) * own : (i + 2) * own].astype(ref.dtype)


def token_sum(keep, got, after, own, name):
    rows, width = keep.shape
    outs = [((own, width), F32)] + [((own, width), BF16)] * (rows // own - 1)
    return call(token_sum_body, name, outs, (keep, got, after), "vvh")


def last_sum_body(keep_ref, got_a, got_b, got_c, mixed_hbm, grad_hbm, mixed_ref, grad_ref, sems):
    total = keep_ref[...] + got_a[...].astype(F32)
    total = (total + got_b[...].astype(F32) + got_c[...].astype(F32)).astype(BF16)
    width = mixed_ref.shape[1]
    mixed_ref[...] = total[:, :width]
    grad_ref[...] = total[:, width:]
    copies = [
        pltpu.make_async_copy(mixed_ref, mixed_hbm, sems.at[0]),
        pltpu.make_async_copy(grad_ref, grad_hbm, sems.at[1]),
    ]
    for copy in copies:
        copy.start()
    for copy in copies:
        copy.wait()


def outer_block(h, c, place):
    for i in range(0, h.shape[1], TILE):
        turned = h[:, i : i + TILE].T
        for j in range(0, c.shape[1], 2 * TILE):
            place[i : i + TILE, j : j + 2 * TILE] = times(turned, c[:, j : j + 2 * TILE]).astype(BF16)


def outer_steps(c, steps, slots, sems):
    copies = []
    for i, (h, place) in enumerate(steps):
        outer_block(h, c, slots.at[i])
        copies.append(pltpu.make_async_copy(slots.at[i], place, sems.at[i]))
        copies[-1].start()
    for copy in copies:
        copy.wait()


def outer_body(speech, text, after_ref, arr_ref, hs_ref, ht_ref, *refs):
    slots, sems = refs[-2:]
    outs = list(refs[-2 - bool(speech) - bool(text) : -2])
    width = outs[0].shape[1]
    steps = []
    for h_ref, blocks in ((hs_ref, speech), (ht_ref, text)):
        out = outs.pop(0) if blocks else None
        cuts = [slice(i * ROWS, (i + 1) * ROWS) for i in blocks]
        steps += [(h_ref[:, cut], out.at[cut]) for cut in cuts]
    outer_steps(arr_ref[:, width : 2 * width], steps, slots, sems)


def flip(value, axes, bit, n):
    return lax.ppermute(value, axes, [(i, i ^ bit) for i in range(n)])


def by_kernels(n_seq, n_tok, tokens, modality, cotangent, gate_s, up_s, down_s, gate_t, up_t, down_t):
    rows, width = tokens.shape
    fs, ft = gate_s.shape[1], gate_t.shape[1]
    wide = ((2 * (fs + ft) // WIDE, width, WIDE), BF16)
    pair = [pltpu.VMEM((rows, width), BF16)] * 2

    packed = ((rows, 2 * width + 128), BF16)
    scratch = pair + [pltpu.SMEM((rows,), jnp.int32), pltpu.SemaphoreType.DMA((3,))]
    wide, arr = call(pack_body, "pack", [wide, packed], (modality, tokens, cotangent), "hhh", scratch)
    got = flip(arr, TOK, HOPS[0], n_tok)
    wide = load(arr, gate_t, wide, (), 0, "load_gate_text")
    arr = join(arr, got, "join_4", (wide,))
    got = flip(arr, TOK, HOPS[1], n_tok)
    arr = join(arr, got, "join_8", (wide,))
    arr = join(arr, flip(arr, TOK, HOPS[2], n_tok), "join_16", (wide, down_t, down_s))

    mine, theirs, wide = partials(arr, up_t, gate_s, up_s, down_t, down_s, wide)
    blocks = 2 * (fs + ft) // BLOCK
    got = flip(theirs, "seq", 1, n_seq)
    wide = turn(wide, (down_t, down_s), 0, TURN_FIRST, "turn_1")
    total, send = call(
        core_sum_body, "core_sum", [like(mine), (mine.shape, BF16)], (mine, got), "vv", also=(wide, down_t, down_s)
    )
    got = flip(send, "seq", 2, n_seq)
    wide = turn(wide, (down_t, down_s), TURN_FIRST, blocks - TURN_FIRST, "turn_2")
    done = call(hidden_body, "hidden", [(mine.shape, BF16)], (total, got), "vv", also=(wide, down_t, down_s))[0]
    other = flip(done, "seq", 1, n_seq)
    own = call(
        mixed_own_body, "mixed_own", [((arr.shape[0], width), F32)], (arr, done, down_t, down_s), "vvvv",
        flops=arr.shape[0] * (down_s.size + down_t.size), also=(wide,),
    )[0]
    early = EARLY_ROWS
    keep, send, hs, ht, down_s_grad = back(arr, done, other, own, wide, down_t, down_s, range(blocks), early)

    def outer(after, speech, text, old, name):
        count = len(speech) + len(text)
        outs = [like(w) for w, blocks in ((down_s, speech), (down_t, text)) if blocks]
        return call(
            functools.partial(outer_body, speech, text), name, outs, (after, arr, hs, ht, *old),
            "vvvv" + "h" * len(old), [pltpu.VMEM((count, ROWS, width), BF16), pltpu.SemaphoreType.DMA((count,))],
            2 * arr.shape[0] * count * ROWS * width, 2 * count * ROWS * width, limit=8,
            out_places="h" * len(outs), aliases={4: 0} if old else None,
        )

    ns, nt = fs // ROWS, ft // ROWS
    got = flip(send, TOK, HOPS[2], n_tok)
    down_s_grad, down_t_grad = outer(keep, range(early // ROWS, ns), range(TEXT_FIRST), (down_s_grad,), "down_grad_1")
    keep, *sends = token_sum(keep, got, down_t_grad, rows, "token_sum_4")
    bits = (HOPS[0], HOPS[1], HOPS[0] ^ HOPS[1])
    gots = [flip(sends[i], TOK, bits[i], n_tok) for i in (2, 0, 1)]
    down_t_grad = outer(keep, (), range(TEXT_FIRST, nt), (down_t_grad,), "down_grad_2")[0]
    outs = [((rows, width), BF16)] * 2
    mixed, token_grad = call(
        last_sum_body, "token_sum_1", outs, (keep, *gots), "vvvv", pair + [pltpu.SemaphoreType.DMA((2,))],
        out_places="hh",
    )
    return mixed, token_grad, down_s_grad, down_t_grad


def by_arrays(n_seq, n_tok, tokens, modality, cotangent, gate_s, up_s, down_s, gate_t, up_t, down_t):
    width = tokens.shape[1]
    ft = gate_t.shape[1]
    kind = jnp.broadcast_to(modality.astype(BF16)[:, None], (modality.shape[0], 128))
    packed = jnp.concatenate([tokens, cotangent, kind], axis=1)
    arrived = lax.all_gather(packed, TOK, axis=0, tiled=True)
    rows, grads = arrived[:, :width], arrived[:, width : 2 * width]
    speech = arrived[:, 2 * width : 2 * width + 1] == 0

    def pick(s, t):
        return jnp.concatenate([jnp.where(speech, s[:, :ft], t), s[:, ft:]], axis=1)

    def halves(v):
        zero = jnp.zeros((), v.dtype)
        return jnp.where(speech, v, zero), jnp.where(speech, zero, v[:, :ft])

    g = pick(times(rows, gate_s), times(rows, gate_t))
    u = pick(times(rows, up_s), times(rows, up_t))
    dh = pick(contract_last(grads, down_s), contract_last(grads, down_t))
    sums = jnp.stack([g, u, dh])
    sums = sums + flip(sums, "seq", 1, n_seq)
    g, u, dh = sums + flip(sums.astype(BF16), "seq", 2, n_seq).astype(F32)
    sig = jax.nn.sigmoid(g)
    h = (g * sig * u).astype(BF16)
    dg = (dh * u * sig * (1.0 + g * (1.0 - sig))).astype(BF16)
    du = (dh * (g * sig)).astype(BF16)
    (hs, ht), (dgs, dgt), (dus, dut) = halves(h), halves(dg), halves(du)
    mixed = times(hs, down_s) + times(ht, down_t)
    grad = contract_last(dgs, gate_s) + contract_last(dus, up_s)
    grad = grad + contract_last(dgt, gate_t) + contract_last(dut, up_t)
    out = jnp.concatenate([mixed, grad], axis=1).astype(BF16)
    out = out.reshape(n_tok, out.shape[0] // n_tok, out.shape[1])
    out = lax.all_to_all(out, TOK, split_axis=0, concat_axis=0, tiled=True)
    total = jnp.sum(out.astype(F32), axis=0).astype(BF16)
    down_s_grad = contract_first(hs, grads).astype(BF16)
    down_t_grad = contract_first(ht, grads).astype(BF16)
    return total[:, :width], total[:, width:], down_s_grad, down_t_grad


def solution(mesh):
    n_seq, n_tok = mesh.shape["seq"], mesh.shape["attn"] * mesh.shape["exp"]

    def run(*args):
        fs, ft, width = args[3].shape[1], args[6].shape[1], args[0].shape[1]
        fits = n_tok == 8 and args[0].shape[0] == 2 and fs >= ft and ft % (2 * WIDE) == 0
        fits = fits and fs % WIDE == 0 and width % BLOCK == 0
        return (by_kernels if fits else by_arrays)(n_seq, n_tok, *args)

    return jax.shard_map(
        run,
        mesh=mesh,
        in_specs=(
            P(TOK, "seq"),
            P(TOK),
            P(TOK, "seq"),
            P("seq", TOK),
            P("seq", TOK),
            P(TOK, "seq"),
            P("seq", TOK),
            P("seq", TOK),
            P(TOK, "seq"),
        ),
        out_specs=(P(TOK, "seq"),) * 4,
        check_vma=False,
    )
```

```python
import functools

import jax
import jax.numpy as jnp
from jax import lax
from jax.experimental import pallas as pl
from jax.experimental.pallas import tpu as pltpu
from jax.sharding import PartitionSpec as P

TOK = ("attn", "exp")
HOPS = (2, 1, 4)
F32 = jnp.float32
BF16 = jnp.bfloat16
MIB = 1 << 20
LIMIT = 8
BLOCK = 512
WIDE = 1024
ROWS = 256
TILE = 128
TURN_FIRST = 5
EARLY_BLOCKS = 1
EARLY_ROWS = 2048
TEXT_FIRST = 2
PLACES = {"h": pl.ANY, "v": pltpu.VMEM, "s": pltpu.SMEM}


def contract_first(left, right):
    return lax.dot_general(left, right, (((0,), (0,)), ((), ())), preferred_element_type=F32)


def contract_last(left, right):
    return lax.dot_general(left, right, (((1,), (1,)), ((), ())), preferred_element_type=F32)


def times(left, right):
    return jnp.dot(left, right, preferred_element_type=F32)


def size_of(*arrays):
    return sum(a.size * jnp.dtype(a.dtype).itemsize for a in arrays)


def constrain(x, place):
    if place == "s":
        return x
    return pltpu.with_memory_space_constraint(x, pltpu.VMEM if place == "v" else pltpu.HBM)


def call(
    body, name, outs, ins, places, scratch=(), flops=0, traffic=0, limit=LIMIT, out_places=None, aliases=None, also=()
):
    out_places = out_places or "v" * len(outs)
    shapes = [pltpu.VMEM(*o) if p == "v" else jax.ShapeDtypeStruct(*o) for o, p in zip(outs, out_places)]
    count = len(ins)

    def seen(*refs):
        body(*refs[:count], *refs[count + len(also) :])

    ins, places = (*ins, *also), places + "v" * len(also)
    return pl.pallas_call(
        seen,
        out_shape=shapes,
        in_specs=[pl.BlockSpec(memory_space=PLACES[p]) for p in places],
        out_specs=[pl.BlockSpec(memory_space=PLACES[p]) for p in out_places],
        scratch_shapes=list(scratch),
        input_output_aliases=aliases or {},
        compiler_params=pltpu.CompilerParams(vmem_limit_bytes=limit * MIB),
        cost_estimate=pl.CostEstimate(flops=flops, bytes_accessed=traffic, transcendentals=0),
        name=name,
    )(*[constrain(x, p) for x, p in zip(ins, places)])


def like(x):
    return x.shape, x.dtype


def parity():
    return lax.rem(lax.axis_index("seq"), 2)


def is_speech(arr_ref):
    return arr_ref[:, arr_ref.shape[1] - 1 :] == 0


def pack_body(kind_hbm, tok_hbm, cot_hbm, wide_ref, out_ref, tok_ref, cot_ref, kind_ref, sems):
    copies = [
        pltpu.make_async_copy(kind_hbm, kind_ref, sems.at[2]),
        pltpu.make_async_copy(tok_hbm, tok_ref, sems.at[0]),
        pltpu.make_async_copy(cot_hbm, cot_ref, sems.at[1]),
    ]
    for copy in copies:
        copy.start()
    width = tok_ref.shape[1]
    row = lax.broadcasted_iota(jnp.int32, (tok_ref.shape[0], 128), 0)
    kind = jnp.zeros(row.shape, F32)
    for copy in copies:
        copy.wait()
    for i in range(tok_ref.shape[0]):
        kind = jnp.where(row == i, kind_ref[i].astype(F32), kind)
    out_ref[:, 2 * width :] = kind.astype(BF16)
    out_ref[:, :width] = tok_ref[...]
    out_ref[:, width : 2 * width] = cot_ref[...]


def join_body(*refs):
    *parts, out_ref = refs
    out_ref[...] = jnp.concatenate([part[...].astype(F32) for part in parts], axis=0).astype(BF16)


def join(parts, name, also):
    rows, width = parts[0].shape
    outs = [((len(parts) * rows, width), BF16)]
    return call(join_body, name, outs, parts, "v" * len(parts), also=also)[0]


def column_blocks(src, wide, first, cuts):
    rows = src.shape[0] // cuts
    parts = [pl.ds(j * rows, rows) for j in range(cuts)]
    return [
        [(src.at[part, pl.ds(i * WIDE, WIDE)], wide.at[first + i, part]) for part in parts]
        for i in range(src.shape[1] // WIDE)
    ]


def square_at(wide_ref, i, r):
    per = WIDE // BLOCK
    return wide_ref.at[i // per, pl.ds(r * BLOCK, BLOCK), pl.ds(i % per * BLOCK, BLOCK)]


def started(groups, sems):
    copies, count = [], 0
    for group in groups:
        copies.append([pltpu.make_async_copy(s, d, sems.at[count + i]) for i, (s, d) in enumerate(group)])
        count += len(group)
    for group in copies:
        for copy in group:
            copy.start()
    return copies


def wait(group):
    for copy in group:
        copy.wait()


def load_body(first, count, after_ref, src_hbm, old_ref, place_ref, sems):
    for group in started(column_blocks(src_hbm, place_ref, first, 4)[:count], sems):
        wait(group)


def load(after, src, place, also, first, count, name):
    return call(
        functools.partial(load_body, first, count),
        name,
        [like(place)],
        (after, src, place),
        "vhv",
        [pltpu.SemaphoreType.DMA((8,))],
        traffic=size_of(src),
        aliases={2: 0},
        also=also,
    )[0]


def beside(i, fs, ft):
    side, rest = divmod(i * BLOCK, ft // 2)
    return side * (fs // 2) + rest


def partials_body(
    arr_ref, dt_ref, ds_ref, gt_hbm, ut_hbm, gs_hbm, us_hbm, old_wide, mine_ref, theirs_ref, wide_ref, part, sems
):
    fs, width = ds_ref.shape
    ft = dt_ref.shape[0]
    ns, nt = fs // WIDE, ft // WIDE
    groups = column_blocks(gt_hbm, wide_ref, 0, 2)[EARLY_BLOCKS:] + column_blocks(ut_hbm, wide_ref, nt, 2)
    groups += column_blocks(gs_hbm, wide_ref, 2 * nt, 2)
    groups += column_blocks(us_hbm, wide_ref, 2 * nt + ns, 2)
    copies = started(groups, sems)
    x = arr_ref[:, :width]
    c = arr_ref[:, width : 2 * width]
    speech = is_speech(arr_ref)

    def put(k, start, value, pick):
        cut = slice(start, start + BLOCK)
        if pick and start % (fs // 2) < ft // 2:
            value = jnp.where(speech, value, part[k, :, cut])
        part[k, :, cut] = value

    def put_wide(k, start, value, pick):
        for i in range(start, start + WIDE, BLOCK):
            place = i if pick else beside(i // BLOCK, fs, ft)
            put(k, place, value[:, i - start : i - start + BLOCK], pick)

    for k, ref in enumerate((dt_ref, ds_ref)):
        for i in range(0, ref.shape[0], BLOCK):
            place = i if k else beside(i // BLOCK, fs, ft)
            put(2, place, contract_last(c, ref[i : i + BLOCK, :]), k == 1)
    for k in range(2):
        for i in range(nt):
            if k * nt + i >= EARLY_BLOCKS:
                wait(copies[k * nt + i - EARLY_BLOCKS])
            put_wide(k, i * WIDE, times(x, wide_ref[k * nt + i]), False)
    for k in range(2):
        for i in range(ns):
            wait(copies[2 * nt - EARLY_BLOCKS + k * ns + i])
            put_wide(k, i * WIDE, times(x, wide_ref[2 * nt + k * ns + i]), True)
    half = fs // 2
    odd = parity()
    for k in range(3):
        mine_ref[k] = part[k, :, pl.ds(pl.multiple_of(odd * half, half), half)]
        theirs_ref[k] = part[k, :, pl.ds(pl.multiple_of((1 - odd) * half, half), half)]


def partials(arr, gate_t, up_t, gate_s, up_s, down_t, down_s, wide):
    rows, fs = arr.shape[0], gate_s.shape[1]
    half = ((3, rows, fs // 2), F32)
    return call(
        partials_body,
        "hidden_partials",
        [half, half, like(wide)],
        (arr, down_t, down_s, gate_t, up_t, gate_s, up_s, wide),
        "vvvhhhhv",
        [pltpu.VMEM((3, rows, fs), F32), pltpu.SemaphoreType.DMA((4 * (fs + up_t.shape[1]) // WIDE,))],
        2 * rows * (wide.size + down_s.size + down_t.size),
        size_of(up_t, gate_s, up_s),
        aliases={7: 2},
    )


def core_sum_body(mine_ref, got_ref, sum_ref, send_ref):
    total = mine_ref[...] + got_ref[...]
    sum_ref[...] = total
    send_ref[...] = total.astype(BF16)


def hidden_body(sum_ref, got_ref, out_ref):
    total = [sum_ref[k] + got_ref[k].astype(F32) for k in range(3)]
    g, u, dh = total
    sig = jax.nn.sigmoid(g)
    silu = g * sig
    out_ref[0] = (silu * u).astype(BF16)
    out_ref[1] = (dh * u * sig * (1.0 + g * (1.0 - sig))).astype(BF16)
    out_ref[2] = (dh * silu).astype(BF16)


def turn_body(first, count, old_ref, wide_ref):
    row, col = (lax.broadcasted_iota(jnp.int32, (ROWS, ROWS), i) for i in range(2))
    one = (row == col).astype(BF16)
    squares = wide_ref.shape[1] // BLOCK
    for n in range(count * squares):
        i, r = first + n // squares, n % squares
        place = square_at(wide_ref, i, r)
        square = place[...]
        if n % 2:
            turned = square.T
        else:
            parts = [contract_last(one, square[:, j : j + ROWS]) for j in range(0, BLOCK, ROWS)]
            turned = jnp.concatenate([p.astype(BF16) for p in parts], axis=0)
        place[...] = turned


def turn(wide, also, first, count, name):
    return call(
        functools.partial(turn_body, first, count),
        name,
        [like(wide)],
        (wide,),
        "v",
        traffic=4 * count * wide.shape[1] * BLOCK,
        aliases={0: 0},
        also=also,
    )[0]


def mixed_half(h, speech, side, dt_ref, ds_ref):
    half_s, half_t, width = ds_ref.shape[0] // 2, dt_ref.shape[0] // 2, ds_ref.shape[1]
    zero = jnp.zeros_like(h)
    hs, ht = jnp.where(speech, h, zero), jnp.where(speech, zero, h)[:, :half_t]
    rows_s = pl.ds(pl.multiple_of(side * half_s, BLOCK), half_s)
    rows_t = pl.ds(pl.multiple_of(side * half_t, BLOCK), half_t)
    cuts = [slice(i, i + BLOCK) for i in range(0, width, BLOCK)]
    return [times(hs, ds_ref[rows_s, cut]) + times(ht, dt_ref[rows_t, cut]) for cut in cuts]


def mixed_own_body(arr_ref, done_ref, dt_ref, ds_ref, out_ref):
    parts = mixed_half(done_ref[0], is_speech(arr_ref), parity(), dt_ref, ds_ref)
    for i, value in enumerate(parts):
        out_ref[:, i * BLOCK : (i + 1) * BLOCK] = value


def back_body(
    turned, grad_rows, arr_ref, done_ref, other_ref, own_ref, wide_ref, dt_ref, ds_ref,
    keep_ref, send_ref, hs_ref, ht_ref, grad_hbm, dgs, dgt, dus, dut, out, slots, sems,
):
    speech = is_speech(arr_ref)
    fs, ft = hs_ref.shape[1], ht_ref.shape[1]
    ns, nt = fs // BLOCK, ft // BLOCK
    odd = parity() == 1
    for k, (s, t) in enumerate(((hs_ref, ht_ref), (dgs, dgt), (dus, dut))):
        done, other = done_ref[k], other_ref[k]
        value = jnp.concatenate([jnp.where(odd, other, done), jnp.where(odd, done, other)], axis=1)
        zero = jnp.zeros_like(value)
        s[...] = jnp.where(speech, value, zero)
        value = jnp.where(speech, zero, value)
        for i in range(nt):
            start = beside(i, fs, ft)
            t[:, i * BLOCK : (i + 1) * BLOCK] = value[:, start : start + BLOCK]
    width = ds_ref.shape[1]
    for i, value in enumerate(mixed_half(other_ref[0], speech, 1 - parity(), dt_ref, ds_ref)):
        cut = slice(i * BLOCK, (i + 1) * BLOCK)
        out[:, cut] = own_ref[:, cut] + value
    blocks = [(dgt, nt), (dut, nt), (dgs, ns), (dus, ns)]
    blocks = [(ref, i) for ref, n in blocks for i in range(n)]
    c = arr_ref[:, width : 2 * width]
    copies = []
    for i in range(grad_rows // ROWS):
        cut = slice(i * ROWS, (i + 1) * ROWS)
        outer_block(hs_ref[:, cut], c, slots.at[i])
        copies.append(pltpu.make_async_copy(slots.at[i], grad_hbm.at[cut], sems.at[i]))
    for copy in copies:
        copy.start()
    for r in range(width // BLOCK):
        total = jnp.zeros((out.shape[0], BLOCK), F32)
        for b, (ref, j) in enumerate(blocks):
            product = times if b in turned else contract_last
            total += product(ref[:, j * BLOCK : (j + 1) * BLOCK], square_at(wide_ref, b, r)[...])
        start = width + r * BLOCK
        out[:, start : start + BLOCK] = total
    for copy in copies:
        copy.wait()
    half = keep_ref.shape[0]
    keep_ref[...] = out[:half]
    send_ref[...] = out[half:].astype(BF16)


def back(arr, done, other, own, wide, down_t, down_s, turned, grad_rows):
    rows, width = arr.shape[0], down_s.shape[1]
    fs, ft = down_s.shape[0], down_t.shape[0]
    count = grad_rows // ROWS
    hidden = [((rows, fs), BF16), ((rows, ft), BF16)]
    scratch = [pltpu.VMEM(*s) for s in hidden + hidden] + [pltpu.VMEM((rows, 2 * width), F32)]
    scratch += [pltpu.VMEM((count, ROWS, width), BF16), pltpu.SemaphoreType.DMA((count,))]
    return call(
        functools.partial(back_body, turned, grad_rows),
        "token_partials",
        [((rows // 2, 2 * width), F32), ((rows // 2, 2 * width), BF16)] + hidden + [like(down_s)],
        (arr, done, other, own, wide, down_t, down_s),
        "vvvvvvv",
        scratch,
        2 * rows * (wide.size + down_t.size + down_s.size),
        out_places="vvvvh",
    )


def token_sum_body(keep_ref, got_ref, after_ref, next_ref, *send_refs):
    total = keep_ref[...] + got_ref[...].astype(F32)
    own = next_ref.shape[0]
    next_ref[...] = total[:own]
    for i, ref in enumerate(send_refs):
        ref[...] = total[(i + 1) * own : (i + 2) * own].astype(ref.dtype)


def token_sum(keep, got, after, own, name):
    rows, width = keep.shape
    outs = [((own, width), F32)] + [((own, width), BF16)] * (rows // own - 1)
    return call(token_sum_body, name, outs, (keep, got, after), "vvh")


def last_sum_body(keep_ref, got_a, got_b, got_c, mixed_hbm, grad_hbm, mixed_ref, grad_ref, sems):
    total = keep_ref[...] + got_a[...].astype(F32)
    total = (total + got_b[...].astype(F32) + got_c[...].astype(F32)).astype(BF16)
    width = mixed_ref.shape[1]
    mixed_ref[...] = total[:, :width]
    grad_ref[...] = total[:, width:]
    copies = [
        pltpu.make_async_copy(mixed_ref, mixed_hbm, sems.at[0]),
        pltpu.make_async_copy(grad_ref, grad_hbm, sems.at[1]),
    ]
    for copy in copies:
        copy.start()
    for copy in copies:
        copy.wait()


def outer_block(h, c, place):
    for i in range(0, h.shape[1], TILE):
        turned = h[:, i : i + TILE].T
        for j in range(0, c.shape[1], 2 * TILE):
            place[i : i + TILE, j : j + 2 * TILE] = times(turned, c[:, j : j + 2 * TILE]).astype(BF16)


def outer_steps(c, steps, slots, sems):
    copies = []
    for i, (h, place) in enumerate(steps):
        outer_block(h, c, slots.at[i])
        copies.append(pltpu.make_async_copy(slots.at[i], place, sems.at[i]))
        copies[-1].start()
    for copy in copies:
        copy.wait()


def outer_body(speech, text, after_ref, arr_ref, hs_ref, ht_ref, *refs):
    slots, sems = refs[-2:]
    outs = list(refs[-2 - bool(speech) - bool(text) : -2])
    width = outs[0].shape[1]
    steps = []
    for h_ref, blocks in ((hs_ref, speech), (ht_ref, text)):
        out = outs.pop(0) if blocks else None
        cuts = [slice(i * ROWS, (i + 1) * ROWS) for i in blocks]
        steps += [(h_ref[:, cut], out.at[cut]) for cut in cuts]
    outer_steps(arr_ref[:, width : 2 * width], steps, slots, sems)


def flip(value, axes, bit, n):
    return lax.ppermute(value, axes, [(i, i ^ bit) for i in range(n)])


def by_kernels(n_seq, n_tok, tokens, modality, cotangent, gate_s, up_s, down_s, gate_t, up_t, down_t):
    rows, width = tokens.shape
    fs, ft = gate_s.shape[1], gate_t.shape[1]
    wide = ((2 * (fs + ft) // WIDE, width, WIDE), BF16)
    pair = [pltpu.VMEM((rows, width), BF16)] * 2

    packed = ((rows, 2 * width + 128), BF16)
    scratch = pair + [pltpu.SMEM((rows,), jnp.int32), pltpu.SemaphoreType.DMA((3,))]
    wide, arr = call(pack_body, "pack", [wide, packed], (modality, tokens, cotangent), "hhh", scratch)
    bits = (HOPS[0], HOPS[1], HOPS[0] ^ HOPS[1])
    far, *near = [flip(arr, TOK, bits[i], n_tok) for i in (2, 0, 1)]
    wide = load(arr, gate_t, wide, (), 0, EARLY_BLOCKS, "load_gate_text")
    arr = join((arr, *near, far), "join_8", (wide,))
    arr = join((arr, flip(arr, TOK, HOPS[2], n_tok)), "join_16", (wide, down_t, down_s))

    mine, theirs, wide = partials(arr, gate_t, up_t, gate_s, up_s, down_t, down_s, wide)
    blocks = 2 * (fs + ft) // BLOCK
    got = flip(theirs, "seq", 1, n_seq)
    wide = turn(wide, (down_t, down_s), 0, TURN_FIRST, "turn_1")
    total, send = call(
        core_sum_body, "core_sum", [like(mine), (mine.shape, BF16)], (mine, got), "vv", also=(wide, down_t, down_s)
    )
    got = flip(send, "seq", 2, n_seq)
    wide = turn(wide, (down_t, down_s), TURN_FIRST, blocks - TURN_FIRST, "turn_2")
    done = call(hidden_body, "hidden", [(mine.shape, BF16)], (total, got), "vv", also=(wide, down_t, down_s))[0]
    other = flip(done, "seq", 1, n_seq)
    own = call(
        mixed_own_body, "mixed_own", [((arr.shape[0], width), F32)], (arr, done, down_t, down_s), "vvvv",
        flops=arr.shape[0] * (down_s.size + down_t.size), also=(wide,),
    )[0]
    early = EARLY_ROWS
    keep, send, hs, ht, down_s_grad = back(arr, done, other, own, wide, down_t, down_s, range(blocks), early)

    def outer(after, speech, text, old, name):
        count = len(speech) + len(text)
        outs = [like(w) for w, blocks in ((down_s, speech), (down_t, text)) if blocks]
        return call(
            functools.partial(outer_body, speech, text), name, outs, (after, arr, hs, ht, *old),
            "vvvv" + "h" * len(old), [pltpu.VMEM((count, ROWS, width), BF16), pltpu.SemaphoreType.DMA((count,))],
            2 * arr.shape[0] * count * ROWS * width, 2 * count * ROWS * width, limit=8,
            out_places="h" * len(outs), aliases={4: 0} if old else None,
        )

    ns, nt = fs // ROWS, ft // ROWS
    got = flip(send, TOK, HOPS[2], n_tok)
    down_s_grad, down_t_grad = outer(keep, range(early // ROWS, ns), range(TEXT_FIRST), (down_s_grad,), "down_grad_1")
    keep, *sends = token_sum(keep, got, down_t_grad, rows, "token_sum_4")
    gots = [flip(sends[i], TOK, bits[i], n_tok) for i in (2, 0, 1)]
    down_t_grad = outer(keep, (), range(TEXT_FIRST, nt), (down_t_grad,), "down_grad_2")[0]
    outs = [((rows, width), BF16)] * 2
    mixed, token_grad = call(
        last_sum_body, "token_sum_1", outs, (keep, *gots), "vvvv", pair + [pltpu.SemaphoreType.DMA((2,))],
        out_places="hh",
    )
    return mixed, token_grad, down_s_grad, down_t_grad


def by_arrays(n_seq, n_tok, tokens, modality, cotangent, gate_s, up_s, down_s, gate_t, up_t, down_t):
    width = tokens.shape[1]
    ft = gate_t.shape[1]
    kind = jnp.broadcast_to(modality.astype(BF16)[:, None], (modality.shape[0], 128))
    packed = jnp.concatenate([tokens, cotangent, kind], axis=1)
    arrived = lax.all_gather(packed, TOK, axis=0, tiled=True)
    rows, grads = arrived[:, :width], arrived[:, width : 2 * width]
    speech = arrived[:, 2 * width : 2 * width + 1] == 0

    def pick(s, t):
        return jnp.concatenate([jnp.where(speech, s[:, :ft], t), s[:, ft:]], axis=1)

    def halves(v):
        zero = jnp.zeros((), v.dtype)
        return jnp.where(speech, v, zero), jnp.where(speech, zero, v[:, :ft])

    g = pick(times(rows, gate_s), times(rows, gate_t))
    u = pick(times(rows, up_s), times(rows, up_t))
    dh = pick(contract_last(grads, down_s), contract_last(grads, down_t))
    sums = jnp.stack([g, u, dh])
    sums = sums + flip(sums, "seq", 1, n_seq)
    g, u, dh = sums + flip(sums.astype(BF16), "seq", 2, n_seq).astype(F32)
    sig = jax.nn.sigmoid(g)
    h = (g * sig * u).astype(BF16)
    dg = (dh * u * sig * (1.0 + g * (1.0 - sig))).astype(BF16)
    du = (dh * (g * sig)).astype(BF16)
    (hs, ht), (dgs, dgt), (dus, dut) = halves(h), halves(dg), halves(du)
    mixed = times(hs, down_s) + times(ht, down_t)
    grad = contract_last(dgs, gate_s) + contract_last(dus, up_s)
    grad = grad + contract_last(dgt, gate_t) + contract_last(dut, up_t)
    out = jnp.concatenate([mixed, grad], axis=1).astype(BF16)
    out = out.reshape(n_tok, out.shape[0] // n_tok, out.shape[1])
    out = lax.all_to_all(out, TOK, split_axis=0, concat_axis=0, tiled=True)
    total = jnp.sum(out.astype(F32), axis=0).astype(BF16)
    down_s_grad = contract_first(hs, grads).astype(BF16)
    down_t_grad = contract_first(ht, grads).astype(BF16)
    return total[:, :width], total[:, width:], down_s_grad, down_t_grad


def solution(mesh):
    n_seq, n_tok = mesh.shape["seq"], mesh.shape["attn"] * mesh.shape["exp"]

    def run(*args):
        fs, ft, width = args[3].shape[1], args[6].shape[1], args[0].shape[1]
        fits = n_tok == 8 and args[0].shape[0] == 2 and fs >= ft and ft % (2 * WIDE) == 0
        fits = fits and fs % WIDE == 0 and width % BLOCK == 0
        return (by_kernels if fits else by_arrays)(n_seq, n_tok, *args)

    return jax.shard_map(
        run,
        mesh=mesh,
        in_specs=(
            P(TOK, "seq"),
            P(TOK),
            P(TOK, "seq"),
            P("seq", TOK),
            P("seq", TOK),
            P(TOK, "seq"),
            P("seq", TOK),
            P("seq", TOK),
            P(TOK, "seq"),
        ),
        out_specs=(P(TOK, "seq"),) * 4,
        check_vma=False,
    )
```

```python
import functools

import jax
import jax.numpy as jnp
from jax import lax
from jax.experimental import pallas as pl
from jax.experimental.pallas import tpu as pltpu
from jax.sharding import PartitionSpec as P

TOK = ("attn", "exp")
HOPS = (2, 1, 4)
F32 = jnp.float32
BF16 = jnp.bfloat16
MIB = 1 << 20
LIMIT = 8
BLOCK = 512
WIDE = 1024
ROWS = 256
TILE = 128
TURN_FIRST = 5
EARLY_ROWS = 2048
TEXT_FIRST = 2
PLACES = {"h": pl.ANY, "v": pltpu.VMEM, "s": pltpu.SMEM}


def contract_first(left, right):
    return lax.dot_general(left, right, (((0,), (0,)), ((), ())), preferred_element_type=F32)


def contract_last(left, right):
    return lax.dot_general(left, right, (((1,), (1,)), ((), ())), preferred_element_type=F32)


def times(left, right):
    return jnp.dot(left, right, preferred_element_type=F32)


def size_of(*arrays):
    return sum(a.size * jnp.dtype(a.dtype).itemsize for a in arrays)


def constrain(x, place):
    if place == "s":
        return x
    return pltpu.with_memory_space_constraint(x, pltpu.VMEM if place == "v" else pltpu.HBM)


def call(
    body, name, outs, ins, places, scratch=(), flops=0, traffic=0, limit=LIMIT, out_places=None, aliases=None, also=()
):
    out_places = out_places or "v" * len(outs)
    shapes = [pltpu.VMEM(*o) if p == "v" else jax.ShapeDtypeStruct(*o) for o, p in zip(outs, out_places)]
    count = len(ins)

    def seen(*refs):
        body(*refs[:count], *refs[count + len(also) :])

    ins, places = (*ins, *also), places + "v" * len(also)
    return pl.pallas_call(
        seen,
        out_shape=shapes,
        in_specs=[pl.BlockSpec(memory_space=PLACES[p]) for p in places],
        out_specs=[pl.BlockSpec(memory_space=PLACES[p]) for p in out_places],
        scratch_shapes=list(scratch),
        input_output_aliases=aliases or {},
        compiler_params=pltpu.CompilerParams(vmem_limit_bytes=limit * MIB),
        cost_estimate=pl.CostEstimate(flops=flops, bytes_accessed=traffic, transcendentals=0),
        name=name,
    )(*[constrain(x, p) for x, p in zip(ins, places)])


def like(x):
    return x.shape, x.dtype


def parity():
    return lax.rem(lax.axis_index("seq"), 2)


def is_speech(arr_ref):
    return arr_ref[:, arr_ref.shape[1] - 1 :] == 0


def pack_body(kind_hbm, tok_hbm, cot_hbm, wide_ref, out_ref, tok_ref, cot_ref, kind_ref, sems):
    copies = [
        pltpu.make_async_copy(kind_hbm, kind_ref, sems.at[2]),
        pltpu.make_async_copy(tok_hbm, tok_ref, sems.at[0]),
        pltpu.make_async_copy(cot_hbm, cot_ref, sems.at[1]),
    ]
    for copy in copies:
        copy.start()
    width = tok_ref.shape[1]
    row = lax.broadcasted_iota(jnp.int32, (tok_ref.shape[0], 128), 0)
    kind = jnp.zeros(row.shape, F32)
    for copy in copies:
        copy.wait()
    for i in range(tok_ref.shape[0]):
        kind = jnp.where(row == i, kind_ref[i].astype(F32), kind)
    out_ref[:, 2 * width :] = kind.astype(BF16)
    out_ref[:, :width] = tok_ref[...]
    out_ref[:, width : 2 * width] = cot_ref[...]


def join_body(*refs):
    *parts, out_ref = refs
    out_ref[...] = jnp.concatenate([part[...].astype(F32) for part in parts], axis=0).astype(BF16)


def join(parts, name, also):
    rows, width = parts[0].shape
    outs = [((len(parts) * rows, width), BF16)]
    return call(join_body, name, outs, parts, "v" * len(parts), also=also)[0]


def column_blocks(src, wide, first, cuts):
    rows = src.shape[0] // cuts
    parts = [pl.ds(j * rows, rows) for j in range(cuts)]
    return [
        [(src.at[part, pl.ds(i * WIDE, WIDE)], wide.at[first + i, part]) for part in parts]
        for i in range(src.shape[1] // WIDE)
    ]


def square_at(wide_ref, i, r):
    per = WIDE // BLOCK
    return wide_ref.at[i // per, pl.ds(r * BLOCK, BLOCK), pl.ds(i % per * BLOCK, BLOCK)]


def started(groups, sems):
    copies, count = [], 0
    for group in groups:
        copies.append([pltpu.make_async_copy(s, d, sems.at[count + i]) for i, (s, d) in enumerate(group)])
        count += len(group)
    for group in copies:
        for copy in group:
            copy.start()
    return copies


def wait(group):
    for copy in group:
        copy.wait()


def load_body(first, after_ref, src_hbm, old_ref, place_ref, sems):
    for group in started(column_blocks(src_hbm, place_ref, first, 4), sems):
        wait(group)


def load(after, src, place, also, first, name):
    return call(
        functools.partial(load_body, first),
        name,
        [like(place)],
        (after, src, place),
        "vhv",
        [pltpu.SemaphoreType.DMA((8,))],
        traffic=size_of(src),
        aliases={2: 0},
        also=also,
    )[0]


def beside(i, fs, ft):
    side, rest = divmod(i * BLOCK, ft // 2)
    return side * (fs // 2) + rest


def partials_body(
    arr_ref, dt_ref, ds_ref, ut_hbm, gs_hbm, us_hbm, old_wide, mine_ref, theirs_ref, wide_ref, part, sems
):
    fs, width = ds_ref.shape
    ft = dt_ref.shape[0]
    ns, nt = fs // WIDE, ft // WIDE
    groups = column_blocks(ut_hbm, wide_ref, nt, 2) + column_blocks(gs_hbm, wide_ref, 2 * nt, 2)
    groups += column_blocks(us_hbm, wide_ref, 2 * nt + ns, 2)
    copies = started(groups, sems)
    x = arr_ref[:, :width]
    c = arr_ref[:, width : 2 * width]
    speech = is_speech(arr_ref)

    def put(k, start, value, pick):
        cut = slice(start, start + BLOCK)
        if pick and start % (fs // 2) < ft // 2:
            value = jnp.where(speech, value, part[k, :, cut])
        part[k, :, cut] = value

    def put_wide(k, start, value, pick):
        for i in range(start, start + WIDE, BLOCK):
            place = i if pick else beside(i // BLOCK, fs, ft)
            put(k, place, value[:, i - start : i - start + BLOCK], pick)

    for k, ref in enumerate((dt_ref, ds_ref)):
        for i in range(0, ref.shape[0], BLOCK):
            place = i if k else beside(i // BLOCK, fs, ft)
            put(2, place, contract_last(c, ref[i : i + BLOCK, :]), k == 1)
    for k in range(2):
        for i in range(nt):
            if k == 1:
                wait(copies[i])
            put_wide(k, i * WIDE, times(x, wide_ref[k * nt + i]), False)
    for k in range(2):
        for i in range(ns):
            wait(copies[nt + k * ns + i])
            put_wide(k, i * WIDE, times(x, wide_ref[2 * nt + k * ns + i]), True)
    half = fs // 2
    odd = parity()
    for k in range(3):
        mine_ref[k] = part[k, :, pl.ds(pl.multiple_of(odd * half, half), half)]
        theirs_ref[k] = part[k, :, pl.ds(pl.multiple_of((1 - odd) * half, half), half)]


def partials(arr, up_t, gate_s, up_s, down_t, down_s, wide):
    rows, fs = arr.shape[0], gate_s.shape[1]
    half = ((3, rows, fs // 2), F32)
    return call(
        partials_body,
        "hidden_partials",
        [half, half, like(wide)],
        (arr, down_t, down_s, up_t, gate_s, up_s, wide),
        "vvvhhhv",
        [pltpu.VMEM((3, rows, fs), F32), pltpu.SemaphoreType.DMA(((4 * fs + 2 * up_t.shape[1]) // WIDE,))],
        2 * rows * (wide.size + down_s.size + down_t.size),
        size_of(up_t, gate_s, up_s),
        aliases={6: 2},
    )


def core_sum_body(mine_ref, got_ref, sum_ref, send_ref):
    total = mine_ref[...] + got_ref[...]
    sum_ref[...] = total
    send_ref[...] = total.astype(BF16)


def hidden_body(sum_ref, got_ref, out_ref):
    total = [sum_ref[k] + got_ref[k].astype(F32) for k in range(3)]
    g, u, dh = total
    sig = jax.nn.sigmoid(g)
    silu = g * sig
    out_ref[0] = (silu * u).astype(BF16)
    out_ref[1] = (dh * u * sig * (1.0 + g * (1.0 - sig))).astype(BF16)
    out_ref[2] = (dh * silu).astype(BF16)


def turn_body(first, count, old_ref, wide_ref):
    row, col = (lax.broadcasted_iota(jnp.int32, (ROWS, ROWS), i) for i in range(2))
    one = (row == col).astype(BF16)
    squares = wide_ref.shape[1] // BLOCK
    for n in range(count * squares):
        i, r = first + n // squares, n % squares
        place = square_at(wide_ref, i, r)
        square = place[...]
        if n % 2:
            turned = square.T
        else:
            parts = [contract_last(one, square[:, j : j + ROWS]) for j in range(0, BLOCK, ROWS)]
            turned = jnp.concatenate([p.astype(BF16) for p in parts], axis=0)
        place[...] = turned


def turn(wide, also, first, count, name):
    return call(
        functools.partial(turn_body, first, count),
        name,
        [like(wide)],
        (wide,),
        "v",
        traffic=4 * count * wide.shape[1] * BLOCK,
        aliases={0: 0},
        also=also,
    )[0]


def mixed_half(h, speech, side, dt_ref, ds_ref):
    half_s, half_t, width = ds_ref.shape[0] // 2, dt_ref.shape[0] // 2, ds_ref.shape[1]
    zero = jnp.zeros_like(h)
    hs, ht = jnp.where(speech, h, zero), jnp.where(speech, zero, h)[:, :half_t]
    rows_s = pl.ds(pl.multiple_of(side * half_s, BLOCK), half_s)
    rows_t = pl.ds(pl.multiple_of(side * half_t, BLOCK), half_t)
    cuts = [slice(i, i + BLOCK) for i in range(0, width, BLOCK)]
    return [times(hs, ds_ref[rows_s, cut]) + times(ht, dt_ref[rows_t, cut]) for cut in cuts]


def mixed_own_body(arr_ref, done_ref, dt_ref, ds_ref, out_ref):
    parts = mixed_half(done_ref[0], is_speech(arr_ref), parity(), dt_ref, ds_ref)
    for i, value in enumerate(parts):
        out_ref[:, i * BLOCK : (i + 1) * BLOCK] = value


def back_body(
    turned, grad_rows, arr_ref, done_ref, other_ref, own_ref, wide_ref, dt_ref, ds_ref,
    keep_ref, send_ref, hs_ref, ht_ref, grad_hbm, dgs, dgt, dus, dut, out, slots, sems,
):
    speech = is_speech(arr_ref)
    fs, ft = hs_ref.shape[1], ht_ref.shape[1]
    ns, nt = fs // BLOCK, ft // BLOCK
    odd = parity() == 1
    for k, (s, t) in enumerate(((hs_ref, ht_ref), (dgs, dgt), (dus, dut))):
        done, other = done_ref[k], other_ref[k]
        value = jnp.concatenate([jnp.where(odd, other, done), jnp.where(odd, done, other)], axis=1)
        zero = jnp.zeros_like(value)
        s[...] = jnp.where(speech, value, zero)
        value = jnp.where(speech, zero, value)
        for i in range(nt):
            start = beside(i, fs, ft)
            t[:, i * BLOCK : (i + 1) * BLOCK] = value[:, start : start + BLOCK]
    width = ds_ref.shape[1]
    for i, value in enumerate(mixed_half(other_ref[0], speech, 1 - parity(), dt_ref, ds_ref)):
        cut = slice(i * BLOCK, (i + 1) * BLOCK)
        out[:, cut] = own_ref[:, cut] + value
    blocks = [(dgt, nt), (dut, nt), (dgs, ns), (dus, ns)]
    blocks = [(ref, i) for ref, n in blocks for i in range(n)]
    c = arr_ref[:, width : 2 * width]
    copies = []
    for i in range(grad_rows // ROWS):
        cut = slice(i * ROWS, (i + 1) * ROWS)
        outer_block(hs_ref[:, cut], c, slots.at[i])
        copies.append(pltpu.make_async_copy(slots.at[i], grad_hbm.at[cut], sems.at[i]))
    for copy in copies:
        copy.start()
    for r in range(width // BLOCK):
        total = jnp.zeros((out.shape[0], BLOCK), F32)
        for b, (ref, j) in enumerate(blocks):
            product = times if b in turned else contract_last
            total += product(ref[:, j * BLOCK : (j + 1) * BLOCK], square_at(wide_ref, b, r)[...])
        start = width + r * BLOCK
        out[:, start : start + BLOCK] = total
    for copy in copies:
        copy.wait()
    half = keep_ref.shape[0]
    keep_ref[...] = out[:half]
    send_ref[...] = out[half:].astype(BF16)


def back(arr, done, other, own, wide, down_t, down_s, turned, grad_rows):
    rows, width = arr.shape[0], down_s.shape[1]
    fs, ft = down_s.shape[0], down_t.shape[0]
    count = grad_rows // ROWS
    hidden = [((rows, fs), BF16), ((rows, ft), BF16)]
    scratch = [pltpu.VMEM(*s) for s in hidden + hidden] + [pltpu.VMEM((rows, 2 * width), F32)]
    scratch += [pltpu.VMEM((count, ROWS, width), BF16), pltpu.SemaphoreType.DMA((count,))]
    return call(
        functools.partial(back_body, turned, grad_rows),
        "token_partials",
        [((rows // 2, 2 * width), F32), ((rows // 2, 2 * width), BF16)] + hidden + [like(down_s)],
        (arr, done, other, own, wide, down_t, down_s),
        "vvvvvvv",
        scratch,
        2 * rows * (wide.size + down_t.size + down_s.size),
        out_places="vvvvh",
    )


def token_sum_body(keep_ref, got_ref, after_ref, next_ref, *send_refs):
    total = keep_ref[...] + got_ref[...].astype(F32)
    own = next_ref.shape[0]
    next_ref[...] = total[:own]
    for i, ref in enumerate(send_refs):
        ref[...] = total[(i + 1) * own : (i + 2) * own].astype(ref.dtype)


def token_sum(keep, got, after, own, name):
    rows, width = keep.shape
    outs = [((own, width), F32)] + [((own, width), BF16)] * (rows // own - 1)
    return call(token_sum_body, name, outs, (keep, got, after), "vvh")


def last_sum_body(keep_ref, got_a, got_b, got_c, mixed_hbm, grad_hbm, mixed_ref, grad_ref, sems):
    total = keep_ref[...] + got_a[...].astype(F32)
    total = (total + got_b[...].astype(F32) + got_c[...].astype(F32)).astype(BF16)
    width = mixed_ref.shape[1]
    mixed_ref[...] = total[:, :width]
    grad_ref[...] = total[:, width:]
    copies = [
        pltpu.make_async_copy(mixed_ref, mixed_hbm, sems.at[0]),
        pltpu.make_async_copy(grad_ref, grad_hbm, sems.at[1]),
    ]
    for copy in copies:
        copy.start()
    for copy in copies:
        copy.wait()


def outer_block(h, c, place):
    for i in range(0, h.shape[1], TILE):
        turned = h[:, i : i + TILE].T
        for j in range(0, c.shape[1], 2 * TILE):
            place[i : i + TILE, j : j + 2 * TILE] = times(turned, c[:, j : j + 2 * TILE]).astype(BF16)


def outer_steps(c, steps, slots, sems):
    copies = []
    for i, (h, place) in enumerate(steps):
        outer_block(h, c, slots.at[i])
        copies.append(pltpu.make_async_copy(slots.at[i], place, sems.at[i]))
        copies[-1].start()
    for copy in copies:
        copy.wait()


def outer_body(speech, text, after_ref, arr_ref, hs_ref, ht_ref, *refs):
    slots, sems = refs[-2:]
    outs = list(refs[-2 - bool(speech) - bool(text) : -2])
    width = outs[0].shape[1]
    steps = []
    for h_ref, blocks in ((hs_ref, speech), (ht_ref, text)):
        out = outs.pop(0) if blocks else None
        cuts = [slice(i * ROWS, (i + 1) * ROWS) for i in blocks]
        steps += [(h_ref[:, cut], out.at[cut]) for cut in cuts]
    outer_steps(arr_ref[:, width : 2 * width], steps, slots, sems)


def flip(value, axes, bit, n):
    return lax.ppermute(value, axes, [(i, i ^ bit) for i in range(n)])


def by_kernels(n_seq, n_tok, tokens, modality, cotangent, gate_s, up_s, down_s, gate_t, up_t, down_t):
    rows, width = tokens.shape
    fs, ft = gate_s.shape[1], gate_t.shape[1]
    wide = ((2 * (fs + ft) // WIDE, width, WIDE), BF16)
    pair = [pltpu.VMEM((rows, width), BF16)] * 2

    packed = ((rows, 2 * width + 128), BF16)
    scratch = pair + [pltpu.SMEM((rows,), jnp.int32), pltpu.SemaphoreType.DMA((3,))]
    wide, arr = call(pack_body, "pack", [wide, packed], (modality, tokens, cotangent), "hhh", scratch)
    bits = (HOPS[0], HOPS[1], HOPS[0] ^ HOPS[1])
    far, *near = [flip(arr, TOK, bits[i], n_tok) for i in (2, 0, 1)]
    wide = load(arr, gate_t, wide, (), 0, "load_gate_text")
    arr = join((arr, *near, far), "join_8", (wide,))
    arr = join((arr, flip(arr, TOK, HOPS[2], n_tok)), "join_16", (wide, down_t, down_s))

    mine, theirs, wide = partials(arr, up_t, gate_s, up_s, down_t, down_s, wide)
    blocks = 2 * (fs + ft) // BLOCK
    got = flip(theirs, "seq", 1, n_seq)
    wide = turn(wide, (down_t, down_s), 0, TURN_FIRST, "turn_1")
    total, send = call(
        core_sum_body, "core_sum", [like(mine), (mine.shape, BF16)], (mine, got), "vv", also=(wide, down_t, down_s)
    )
    got = flip(send, "seq", 2, n_seq)
    wide = turn(wide, (down_t, down_s), TURN_FIRST, blocks - TURN_FIRST, "turn_2")
    done = call(hidden_body, "hidden", [(mine.shape, BF16)], (total, got), "vv", also=(wide, down_t, down_s))[0]
    other = flip(done, "seq", 1, n_seq)
    own = call(
        mixed_own_body, "mixed_own", [((arr.shape[0], width), F32)], (arr, done, down_t, down_s), "vvvv",
        flops=arr.shape[0] * (down_s.size + down_t.size), also=(wide,),
    )[0]
    early = EARLY_ROWS
    keep, send, hs, ht, down_s_grad = back(arr, done, other, own, wide, down_t, down_s, range(blocks), early)

    def outer(after, speech, text, old, name):
        count = len(speech) + len(text)
        outs = [like(w) for w, blocks in ((down_s, speech), (down_t, text)) if blocks]
        return call(
            functools.partial(outer_body, speech, text), name, outs, (after, arr, hs, ht, *old),
            "vvvv" + "h" * len(old), [pltpu.VMEM((count, ROWS, width), BF16), pltpu.SemaphoreType.DMA((count,))],
            2 * arr.shape[0] * count * ROWS * width, 2 * count * ROWS * width, limit=8,
            out_places="h" * len(outs), aliases={4: 0} if old else None,
        )

    ns, nt = fs // ROWS, ft // ROWS
    got = flip(send, TOK, HOPS[2], n_tok)
    down_s_grad, down_t_grad = outer(keep, range(early // ROWS, ns), range(TEXT_FIRST), (down_s_grad,), "down_grad_1")
    keep, *sends = token_sum(keep, got, down_t_grad, rows, "token_sum_4")
    gots = [flip(sends[i], TOK, bits[i], n_tok) for i in (2, 0, 1)]
    down_t_grad = outer(keep, (), range(TEXT_FIRST, nt), (down_t_grad,), "down_grad_2")[0]
    outs = [((rows, width), BF16)] * 2
    mixed, token_grad = call(
        last_sum_body, "token_sum_1", outs, (keep, *gots), "vvvv", pair + [pltpu.SemaphoreType.DMA((2,))],
        out_places="hh",
    )
    return mixed, token_grad, down_s_grad, down_t_grad


def by_arrays(n_seq, n_tok, tokens, modality, cotangent, gate_s, up_s, down_s, gate_t, up_t, down_t):
    width = tokens.shape[1]
    ft = gate_t.shape[1]
    kind = jnp.broadcast_to(modality.astype(BF16)[:, None], (modality.shape[0], 128))
    packed = jnp.concatenate([tokens, cotangent, kind], axis=1)
    arrived = lax.all_gather(packed, TOK, axis=0, tiled=True)
    rows, grads = arrived[:, :width], arrived[:, width : 2 * width]
    speech = arrived[:, 2 * width : 2 * width + 1] == 0

    def pick(s, t):
        return jnp.concatenate([jnp.where(speech, s[:, :ft], t), s[:, ft:]], axis=1)

    def halves(v):
        zero = jnp.zeros((), v.dtype)
        return jnp.where(speech, v, zero), jnp.where(speech, zero, v[:, :ft])

    g = pick(times(rows, gate_s), times(rows, gate_t))
    u = pick(times(rows, up_s), times(rows, up_t))
    dh = pick(contract_last(grads, down_s), contract_last(grads, down_t))
    sums = jnp.stack([g, u, dh])
    sums = sums + flip(sums, "seq", 1, n_seq)
    g, u, dh = sums + flip(sums.astype(BF16), "seq", 2, n_seq).astype(F32)
    sig = jax.nn.sigmoid(g)
    h = (g * sig * u).astype(BF16)
    dg = (dh * u * sig * (1.0 + g * (1.0 - sig))).astype(BF16)
    du = (dh * (g * sig)).astype(BF16)
    (hs, ht), (dgs, dgt), (dus, dut) = halves(h), halves(dg), halves(du)
    mixed = times(hs, down_s) + times(ht, down_t)
    grad = contract_last(dgs, gate_s) + contract_last(dus, up_s)
    grad = grad + contract_last(dgt, gate_t) + contract_last(dut, up_t)
    out = jnp.concatenate([mixed, grad], axis=1).astype(BF16)
    out = out.reshape(n_tok, out.shape[0] // n_tok, out.shape[1])
    out = lax.all_to_all(out, TOK, split_axis=0, concat_axis=0, tiled=True)
    total = jnp.sum(out.astype(F32), axis=0).astype(BF16)
    down_s_grad = contract_first(hs, grads).astype(BF16)
    down_t_grad = contract_first(ht, grads).astype(BF16)
    return total[:, :width], total[:, width:], down_s_grad, down_t_grad


def solution(mesh):
    n_seq, n_tok = mesh.shape["seq"], mesh.shape["attn"] * mesh.shape["exp"]

    def run(*args):
        fs, ft, width = args[3].shape[1], args[6].shape[1], args[0].shape[1]
        fits = n_tok == 8 and args[0].shape[0] == 2 and fs >= ft and ft % (2 * WIDE) == 0
        fits = fits and fs % WIDE == 0 and width % BLOCK == 0
        return (by_kernels if fits else by_arrays)(n_seq, n_tok, *args)

    return jax.shard_map(
        run,
        mesh=mesh,
        in_specs=(
            P(TOK, "seq"),
            P(TOK),
            P(TOK, "seq"),
            P("seq", TOK),
            P("seq", TOK),
            P(TOK, "seq"),
            P("seq", TOK),
            P("seq", TOK),
            P(TOK, "seq"),
        ),
        out_specs=(P(TOK, "seq"),) * 4,
        check_vma=False,
    )
```

```python
import functools

import jax
import jax.numpy as jnp
from jax import lax
from jax.experimental import pallas as pl
from jax.experimental.pallas import tpu as pltpu
from jax.sharding import PartitionSpec as P

TOK = ("attn", "exp")
HOPS = (2, 1, 4)
F32 = jnp.float32
BF16 = jnp.bfloat16
MIB = 1 << 20
LIMIT = 8
BLOCK = 512
WIDE = 1024
ROWS = 256
TILE = 128
TURN_FIRST = 5
EARLY_ROWS = 1792
TEXT_FIRST = 1
PLACES = {"h": pl.ANY, "v": pltpu.VMEM, "s": pltpu.SMEM}


def contract_first(left, right):
    return lax.dot_general(left, right, (((0,), (0,)), ((), ())), preferred_element_type=F32)


def contract_last(left, right):
    return lax.dot_general(left, right, (((1,), (1,)), ((), ())), preferred_element_type=F32)


def times(left, right):
    return jnp.dot(left, right, preferred_element_type=F32)


def size_of(*arrays):
    return sum(a.size * jnp.dtype(a.dtype).itemsize for a in arrays)


def constrain(x, place):
    if place == "s":
        return x
    return pltpu.with_memory_space_constraint(x, pltpu.VMEM if place == "v" else pltpu.HBM)


def call(
    body, name, outs, ins, places, scratch=(), flops=0, traffic=0, limit=LIMIT, out_places=None, aliases=None, also=()
):
    out_places = out_places or "v" * len(outs)
    shapes = [pltpu.VMEM(*o) if p == "v" else jax.ShapeDtypeStruct(*o) for o, p in zip(outs, out_places)]
    count = len(ins)

    def seen(*refs):
        body(*refs[:count], *refs[count + len(also) :])

    ins, places = (*ins, *also), places + "v" * len(also)
    return pl.pallas_call(
        seen,
        out_shape=shapes,
        in_specs=[pl.BlockSpec(memory_space=PLACES[p]) for p in places],
        out_specs=[pl.BlockSpec(memory_space=PLACES[p]) for p in out_places],
        scratch_shapes=list(scratch),
        input_output_aliases=aliases or {},
        compiler_params=pltpu.CompilerParams(vmem_limit_bytes=limit * MIB),
        cost_estimate=pl.CostEstimate(flops=flops, bytes_accessed=traffic, transcendentals=0),
        name=name,
    )(*[constrain(x, p) for x, p in zip(ins, places)])


def like(x):
    return x.shape, x.dtype


def parity():
    return lax.rem(lax.axis_index("seq"), 2)


def is_speech(arr_ref):
    return arr_ref[:, arr_ref.shape[1] - 1 :] == 0


def pack_body(kind_hbm, tok_hbm, cot_hbm, wide_ref, out_ref, tok_ref, cot_ref, kind_ref, sems):
    copies = [
        pltpu.make_async_copy(kind_hbm, kind_ref, sems.at[2]),
        pltpu.make_async_copy(tok_hbm, tok_ref, sems.at[0]),
        pltpu.make_async_copy(cot_hbm, cot_ref, sems.at[1]),
    ]
    for copy in copies:
        copy.start()
    width = tok_ref.shape[1]
    row = lax.broadcasted_iota(jnp.int32, (tok_ref.shape[0], 128), 0)
    kind = jnp.zeros(row.shape, F32)
    for copy in copies:
        copy.wait()
    for i in range(tok_ref.shape[0]):
        kind = jnp.where(row == i, kind_ref[i].astype(F32), kind)
    out_ref[:, 2 * width :] = kind.astype(BF16)
    out_ref[:, :width] = tok_ref[...]
    out_ref[:, width : 2 * width] = cot_ref[...]


def join_body(*refs):
    *parts, out_ref = refs
    out_ref[...] = jnp.concatenate([part[...].astype(F32) for part in parts], axis=0).astype(BF16)


def join(parts, name, also):
    rows, width = parts[0].shape
    outs = [((len(parts) * rows, width), BF16)]
    return call(join_body, name, outs, parts, "v" * len(parts), also=also)[0]


def column_blocks(src, wide, first, cuts):
    rows = src.shape[0] // cuts
    parts = [pl.ds(j * rows, rows) for j in range(cuts)]
    return [
        [(src.at[part, pl.ds(i * WIDE, WIDE)], wide.at[first + i, part]) for part in parts]
        for i in range(src.shape[1] // WIDE)
    ]


def square_at(wide_ref, i, r):
    per = WIDE // BLOCK
    return wide_ref.at[i // per, pl.ds(r * BLOCK, BLOCK), pl.ds(i % per * BLOCK, BLOCK)]


def started(groups, sems):
    copies, count = [], 0
    for group in groups:
        copies.append([pltpu.make_async_copy(s, d, sems.at[count + i]) for i, (s, d) in enumerate(group)])
        count += len(group)
    for group in copies:
        for copy in group:
            copy.start()
    return copies


def wait(group):
    for copy in group:
        copy.wait()


def load_body(first, after_ref, src_hbm, old_ref, place_ref, sems):
    for group in started(column_blocks(src_hbm, place_ref, first, 4), sems):
        wait(group)


def load(after, src, place, also, first, name):
    return call(
        functools.partial(load_body, first),
        name,
        [like(place)],
        (after, src, place),
        "vhv",
        [pltpu.SemaphoreType.DMA((8,))],
        traffic=size_of(src),
        aliases={2: 0},
        also=also,
    )[0]


def beside(i, fs, ft):
    side, rest = divmod(i * BLOCK, ft // 2)
    return side * (fs // 2) + rest


def partials_body(
    arr_ref, dt_ref, ds_ref, ut_hbm, gs_hbm, us_hbm, old_wide, mine_ref, theirs_ref, wide_ref, part, sems
):
    fs, width = ds_ref.shape
    ft = dt_ref.shape[0]
    ns, nt = fs // WIDE, ft // WIDE
    groups = column_blocks(ut_hbm, wide_ref, nt, 2) + column_blocks(gs_hbm, wide_ref, 2 * nt, 2)
    groups += column_blocks(us_hbm, wide_ref, 2 * nt + ns, 2)
    copies = started(groups, sems)
    x = arr_ref[:, :width]
    c = arr_ref[:, width : 2 * width]
    speech = is_speech(arr_ref)

    def put(k, start, value, pick):
        cut = slice(start, start + BLOCK)
        if pick and start % (fs // 2) < ft // 2:
            value = jnp.where(speech, value, part[k, :, cut])
        part[k, :, cut] = value

    def put_wide(k, start, value, pick):
        for i in range(start, start + WIDE, BLOCK):
            place = i if pick else beside(i // BLOCK, fs, ft)
            put(k, place, value[:, i - start : i - start + BLOCK], pick)

    for k, ref in enumerate((dt_ref, ds_ref)):
        for i in range(0, ref.shape[0], BLOCK):
            place = i if k else beside(i // BLOCK, fs, ft)
            put(2, place, contract_last(c, ref[i : i + BLOCK, :]), k == 1)
    for k in range(2):
        for i in range(nt):
            if k == 1:
                wait(copies[i])
            put_wide(k, i * WIDE, times(x, wide_ref[k * nt + i]), False)
    for k in range(2):
        for i in range(ns):
            wait(copies[nt + k * ns + i])
            put_wide(k, i * WIDE, times(x, wide_ref[2 * nt + k * ns + i]), True)
    half = fs // 2
    odd = parity()
    for k in range(3):
        mine_ref[k] = part[k, :, pl.ds(pl.multiple_of(odd * half, half), half)]
        theirs_ref[k] = part[k, :, pl.ds(pl.multiple_of((1 - odd) * half, half), half)]


def partials(arr, up_t, gate_s, up_s, down_t, down_s, wide):
    rows, fs = arr.shape[0], gate_s.shape[1]
    half = ((3, rows, fs // 2), F32)
    return call(
        partials_body,
        "hidden_partials",
        [half, half, like(wide)],
        (arr, down_t, down_s, up_t, gate_s, up_s, wide),
        "vvvhhhv",
        [pltpu.VMEM((3, rows, fs), F32), pltpu.SemaphoreType.DMA(((4 * fs + 2 * up_t.shape[1]) // WIDE,))],
        2 * rows * (wide.size + down_s.size + down_t.size),
        size_of(up_t, gate_s, up_s),
        aliases={6: 2},
    )


def core_sum_body(mine_ref, got_ref, sum_ref, send_ref):
    total = mine_ref[...] + got_ref[...]
    sum_ref[...] = total
    send_ref[...] = total.astype(BF16)


def hidden_body(sum_ref, got_ref, out_ref):
    total = [sum_ref[k] + got_ref[k].astype(F32) for k in range(3)]
    g, u, dh = total
    sig = jax.nn.sigmoid(g)
    silu = g * sig
    out_ref[0] = (silu * u).astype(BF16)
    out_ref[1] = (dh * u * sig * (1.0 + g * (1.0 - sig))).astype(BF16)
    out_ref[2] = (dh * silu).astype(BF16)


def turn_body(first, count, old_ref, wide_ref):
    row, col = (lax.broadcasted_iota(jnp.int32, (ROWS, ROWS), i) for i in range(2))
    one = (row == col).astype(BF16)
    squares = wide_ref.shape[1] // BLOCK
    for n in range(count * squares):
        i, r = first + n // squares, n % squares
        place = square_at(wide_ref, i, r)
        square = place[...]
        if n % 2:
            turned = square.T
        else:
            parts = [contract_last(one, square[:, j : j + ROWS]) for j in range(0, BLOCK, ROWS)]
            turned = jnp.concatenate([p.astype(BF16) for p in parts], axis=0)
        place[...] = turned


def turn(wide, also, first, count, name):
    return call(
        functools.partial(turn_body, first, count),
        name,
        [like(wide)],
        (wide,),
        "v",
        traffic=4 * count * wide.shape[1] * BLOCK,
        aliases={0: 0},
        also=also,
    )[0]


def mixed_half(h, speech, side, dt_ref, ds_ref):
    half_s, half_t, width = ds_ref.shape[0] // 2, dt_ref.shape[0] // 2, ds_ref.shape[1]
    zero = jnp.zeros_like(h)
    hs, ht = jnp.where(speech, h, zero), jnp.where(speech, zero, h)[:, :half_t]
    rows_s = pl.ds(pl.multiple_of(side * half_s, BLOCK), half_s)
    rows_t = pl.ds(pl.multiple_of(side * half_t, BLOCK), half_t)
    cuts = [slice(i, i + BLOCK) for i in range(0, width, BLOCK)]
    return [times(hs, ds_ref[rows_s, cut]) + times(ht, dt_ref[rows_t, cut]) for cut in cuts]


def mixed_own_body(arr_ref, done_ref, dt_ref, ds_ref, out_ref):
    parts = mixed_half(done_ref[0], is_speech(arr_ref), parity(), dt_ref, ds_ref)
    for i, value in enumerate(parts):
        out_ref[:, i * BLOCK : (i + 1) * BLOCK] = value


def back_body(
    turned, grad_rows, arr_ref, done_ref, other_ref, own_ref, wide_ref, dt_ref, ds_ref,
    keep_ref, send_ref, hs_ref, ht_ref, grad_hbm, dgs, dgt, dus, dut, out, slots, sems,
):
    speech = is_speech(arr_ref)
    fs, ft = hs_ref.shape[1], ht_ref.shape[1]
    ns, nt = fs // BLOCK, ft // BLOCK
    odd = parity() == 1
    for k, (s, t) in enumerate(((hs_ref, ht_ref), (dgs, dgt), (dus, dut))):
        done, other = done_ref[k], other_ref[k]
        value = jnp.concatenate([jnp.where(odd, other, done), jnp.where(odd, done, other)], axis=1)
        zero = jnp.zeros_like(value)
        s[...] = jnp.where(speech, value, zero)
        value = jnp.where(speech, zero, value)
        for i in range(nt):
            start = beside(i, fs, ft)
            t[:, i * BLOCK : (i + 1) * BLOCK] = value[:, start : start + BLOCK]
    width = ds_ref.shape[1]
    for i, value in enumerate(mixed_half(other_ref[0], speech, 1 - parity(), dt_ref, ds_ref)):
        cut = slice(i * BLOCK, (i + 1) * BLOCK)
        out[:, cut] = own_ref[:, cut] + value
    blocks = [(dgt, nt), (dut, nt), (dgs, ns), (dus, ns)]
    blocks = [(ref, i) for ref, n in blocks for i in range(n)]
    c = arr_ref[:, width : 2 * width]
    copies = []
    for i in range(grad_rows // ROWS):
        cut = slice(i * ROWS, (i + 1) * ROWS)
        outer_block(hs_ref[:, cut], c, slots.at[i])
        copies.append(pltpu.make_async_copy(slots.at[i], grad_hbm.at[cut], sems.at[i]))
    for copy in copies:
        copy.start()
    for r in range(width // BLOCK):
        total = jnp.zeros((out.shape[0], BLOCK), F32)
        for b, (ref, j) in enumerate(blocks):
            product = times if b in turned else contract_last
            total += product(ref[:, j * BLOCK : (j + 1) * BLOCK], square_at(wide_ref, b, r)[...])
        start = width + r * BLOCK
        out[:, start : start + BLOCK] = total
    for copy in copies:
        copy.wait()
    half = keep_ref.shape[0]
    keep_ref[...] = out[:half]
    send_ref[...] = out[half:].astype(BF16)


def back(arr, done, other, own, wide, down_t, down_s, turned, grad_rows):
    rows, width = arr.shape[0], down_s.shape[1]
    fs, ft = down_s.shape[0], down_t.shape[0]
    count = grad_rows // ROWS
    hidden = [((rows, fs), BF16), ((rows, ft), BF16)]
    scratch = [pltpu.VMEM(*s) for s in hidden + hidden] + [pltpu.VMEM((rows, 2 * width), F32)]
    scratch += [pltpu.VMEM((count, ROWS, width), BF16), pltpu.SemaphoreType.DMA((count,))]
    return call(
        functools.partial(back_body, turned, grad_rows),
        "token_partials",
        [((rows // 2, 2 * width), F32), ((rows // 2, 2 * width), BF16)] + hidden + [like(down_s)],
        (arr, done, other, own, wide, down_t, down_s),
        "vvvvvvv",
        scratch,
        2 * rows * (wide.size + down_t.size + down_s.size),
        out_places="vvvvh",
    )


def token_sum_body(keep_ref, got_ref, after_ref, next_ref, *send_refs):
    total = keep_ref[...] + got_ref[...].astype(F32)
    own = next_ref.shape[0]
    next_ref[...] = total[:own]
    for i, ref in enumerate(send_refs):
        ref[...] = total[(i + 1) * own : (i + 2) * own].astype(ref.dtype)


def token_sum(keep, got, after, own, name):
    rows, width = keep.shape
    outs = [((own, width), F32)] + [((own, width), BF16)] * (rows // own - 1)
    return call(token_sum_body, name, outs, (keep, got, after), "vvh")


def last_sum_body(keep_ref, got_a, got_b, got_c, mixed_hbm, grad_hbm, mixed_ref, grad_ref, sems):
    total = keep_ref[...] + got_a[...].astype(F32)
    total = (total + got_b[...].astype(F32) + got_c[...].astype(F32)).astype(BF16)
    width = mixed_ref.shape[1]
    mixed_ref[...] = total[:, :width]
    grad_ref[...] = total[:, width:]
    copies = [
        pltpu.make_async_copy(mixed_ref, mixed_hbm, sems.at[0]),
        pltpu.make_async_copy(grad_ref, grad_hbm, sems.at[1]),
    ]
    for copy in copies:
        copy.start()
    for copy in copies:
        copy.wait()


def outer_block(h, c, place):
    for i in range(0, h.shape[1], TILE):
        turned = h[:, i : i + TILE].T
        for j in range(0, c.shape[1], 2 * TILE):
            place[i : i + TILE, j : j + 2 * TILE] = times(turned, c[:, j : j + 2 * TILE]).astype(BF16)


def outer_steps(c, steps, slots, sems):
    copies = []
    for i, (h, place) in enumerate(steps):
        outer_block(h, c, slots.at[i])
        copies.append(pltpu.make_async_copy(slots.at[i], place, sems.at[i]))
        copies[-1].start()
    for copy in copies:
        copy.wait()


def outer_body(speech, text, after_ref, arr_ref, hs_ref, ht_ref, *refs):
    slots, sems = refs[-2:]
    outs = list(refs[-2 - bool(speech) - bool(text) : -2])
    width = outs[0].shape[1]
    steps = []
    for h_ref, blocks in ((hs_ref, speech), (ht_ref, text)):
        out = outs.pop(0) if blocks else None
        cuts = [slice(i * ROWS, (i + 1) * ROWS) for i in blocks]
        steps += [(h_ref[:, cut], out.at[cut]) for cut in cuts]
    outer_steps(arr_ref[:, width : 2 * width], steps, slots, sems)


def flip(value, axes, bit, n):
    return lax.ppermute(value, axes, [(i, i ^ bit) for i in range(n)])


def by_kernels(n_seq, n_tok, tokens, modality, cotangent, gate_s, up_s, down_s, gate_t, up_t, down_t):
    rows, width = tokens.shape
    fs, ft = gate_s.shape[1], gate_t.shape[1]
    wide = ((2 * (fs + ft) // WIDE, width, WIDE), BF16)
    pair = [pltpu.VMEM((rows, width), BF16)] * 2

    packed = ((rows, 2 * width + 128), BF16)
    scratch = pair + [pltpu.SMEM((rows,), jnp.int32), pltpu.SemaphoreType.DMA((3,))]
    wide, arr = call(pack_body, "pack", [wide, packed], (modality, tokens, cotangent), "hhh", scratch)
    bits = (HOPS[0], HOPS[1], HOPS[0] ^ HOPS[1])
    far, *near = [flip(arr, TOK, bits[i], n_tok) for i in (2, 0, 1)]
    wide = load(arr, gate_t, wide, (), 0, "load_gate_text")
    arr = join((arr, *near, far), "join_8", (wide,))
    arr = join((arr, flip(arr, TOK, HOPS[2], n_tok)), "join_16", (wide, down_t, down_s))

    mine, theirs, wide = partials(arr, up_t, gate_s, up_s, down_t, down_s, wide)
    blocks = 2 * (fs + ft) // BLOCK
    got = flip(theirs, "seq", 1, n_seq)
    wide = turn(wide, (down_t, down_s), 0, TURN_FIRST, "turn_1")
    total, send = call(
        core_sum_body, "core_sum", [like(mine), (mine.shape, BF16)], (mine, got), "vv", also=(wide, down_t, down_s)
    )
    got = flip(send, "seq", 2, n_seq)
    wide = turn(wide, (down_t, down_s), TURN_FIRST, blocks - TURN_FIRST, "turn_2")
    done = call(hidden_body, "hidden", [(mine.shape, BF16)], (total, got), "vv", also=(wide, down_t, down_s))[0]
    other = flip(done, "seq", 1, n_seq)
    own = call(
        mixed_own_body, "mixed_own", [((arr.shape[0], width), F32)], (arr, done, down_t, down_s), "vvvv",
        flops=arr.shape[0] * (down_s.size + down_t.size), also=(wide,),
    )[0]
    early = EARLY_ROWS
    keep, send, hs, ht, down_s_grad = back(arr, done, other, own, wide, down_t, down_s, range(blocks), early)

    def outer(after, speech, text, old, name):
        count = len(speech) + len(text)
        outs = [like(w) for w, blocks in ((down_s, speech), (down_t, text)) if blocks]
        return call(
            functools.partial(outer_body, speech, text), name, outs, (after, arr, hs, ht, *old),
            "vvvv" + "h" * len(old), [pltpu.VMEM((count, ROWS, width), BF16), pltpu.SemaphoreType.DMA((count,))],
            2 * arr.shape[0] * count * ROWS * width, 2 * count * ROWS * width, limit=8,
            out_places="h" * len(outs), aliases={4: 0} if old else None,
        )

    ns, nt = fs // ROWS, ft // ROWS
    got = flip(send, TOK, HOPS[2], n_tok)
    down_s_grad, down_t_grad = outer(keep, range(early // ROWS, ns), range(TEXT_FIRST), (down_s_grad,), "down_grad_1")
    keep, *sends = token_sum(keep, got, down_t_grad, rows, "token_sum_4")
    gots = [flip(sends[i], TOK, bits[i], n_tok) for i in (2, 0, 1)]
    down_t_grad = outer(keep, (), range(TEXT_FIRST, nt), (down_t_grad,), "down_grad_2")[0]
    outs = [((rows, width), BF16)] * 2
    mixed, token_grad = call(
        last_sum_body, "token_sum_1", outs, (keep, *gots), "vvvv", pair + [pltpu.SemaphoreType.DMA((2,))],
        out_places="hh",
    )
    return mixed, token_grad, down_s_grad, down_t_grad


def by_arrays(n_seq, n_tok, tokens, modality, cotangent, gate_s, up_s, down_s, gate_t, up_t, down_t):
    width = tokens.shape[1]
    ft = gate_t.shape[1]
    kind = jnp.broadcast_to(modality.astype(BF16)[:, None], (modality.shape[0], 128))
    packed = jnp.concatenate([tokens, cotangent, kind], axis=1)
    arrived = lax.all_gather(packed, TOK, axis=0, tiled=True)
    rows, grads = arrived[:, :width], arrived[:, width : 2 * width]
    speech = arrived[:, 2 * width : 2 * width + 1] == 0

    def pick(s, t):
        return jnp.concatenate([jnp.where(speech, s[:, :ft], t), s[:, ft:]], axis=1)

    def halves(v):
        zero = jnp.zeros((), v.dtype)
        return jnp.where(speech, v, zero), jnp.where(speech, zero, v[:, :ft])

    g = pick(times(rows, gate_s), times(rows, gate_t))
    u = pick(times(rows, up_s), times(rows, up_t))
    dh = pick(contract_last(grads, down_s), contract_last(grads, down_t))
    sums = jnp.stack([g, u, dh])
    sums = sums + flip(sums, "seq", 1, n_seq)
    g, u, dh = sums + flip(sums.astype(BF16), "seq", 2, n_seq).astype(F32)
    sig = jax.nn.sigmoid(g)
    h = (g * sig * u).astype(BF16)
    dg = (dh * u * sig * (1.0 + g * (1.0 - sig))).astype(BF16)
    du = (dh * (g * sig)).astype(BF16)
    (hs, ht), (dgs, dgt), (dus, dut) = halves(h), halves(dg), halves(du)
    mixed = times(hs, down_s) + times(ht, down_t)
    grad = contract_last(dgs, gate_s) + contract_last(dus, up_s)
    grad = grad + contract_last(dgt, gate_t) + contract_last(dut, up_t)
    out = jnp.concatenate([mixed, grad], axis=1).astype(BF16)
    out = out.reshape(n_tok, out.shape[0] // n_tok, out.shape[1])
    out = lax.all_to_all(out, TOK, split_axis=0, concat_axis=0, tiled=True)
    total = jnp.sum(out.astype(F32), axis=0).astype(BF16)
    down_s_grad = contract_first(hs, grads).astype(BF16)
    down_t_grad = contract_first(ht, grads).astype(BF16)
    return total[:, :width], total[:, width:], down_s_grad, down_t_grad


def solution(mesh):
    n_seq, n_tok = mesh.shape["seq"], mesh.shape["attn"] * mesh.shape["exp"]

    def run(*args):
        fs, ft, width = args[3].shape[1], args[6].shape[1], args[0].shape[1]
        fits = n_tok == 8 and args[0].shape[0] == 2 and fs >= ft and ft % (2 * WIDE) == 0
        fits = fits and fs % WIDE == 0 and width % BLOCK == 0
        return (by_kernels if fits else by_arrays)(n_seq, n_tok, *args)

    return jax.shard_map(
        run,
        mesh=mesh,
        in_specs=(
            P(TOK, "seq"),
            P(TOK),
            P(TOK, "seq"),
            P("seq", TOK),
            P("seq", TOK),
            P(TOK, "seq"),
            P("seq", TOK),
            P("seq", TOK),
            P(TOK, "seq"),
        ),
        out_specs=(P(TOK, "seq"),) * 4,
        check_vma=False,
    )
```
